32 devices in a mesh: grp: 8 (over y, x, core), pix: 4 (over z).
Axes of the slice: x: 2, y: 2, z: 4, core: 2. Of those that a mesh axis runs over, the one named last changes fastest.
Arguments:
- latents: bfloat16 [4096, 1024], P('grp'), may hold values from -6 to 6
- pixels: bfloat16 [16, 1024, 1024], P('grp', 'pix'), may hold values from -6 to 6
- pixel_mask: int32 [16, 1024], P('grp', 'pix'), may hold values from 0 to 1, as said below
- group_image: int32 [16], P('grp'), may hold values from 0 to 7
- cotangent: bfloat16 [4096, 1024], P('grp'), may hold values from -6 to 6
- gain_cross: float32 [1024], replicated, may hold values from 0.5 to 1.5
- gain_pixel: float32 [1024], replicated, may hold values from 0.5 to 1.5
- w_query: bfloat16 [1024, 1024], replicated, may hold values from -0.1875 to 0.1875
- w_keyval: bfloat16 [1024, 2048], replicated, may hold values from -0.1875 to 0.1875
- w_cross_out: bfloat16 [1024, 1024], replicated, may hold values from -1.5 to 1.5
- gain_self: float32 [1024], replicated, may hold values from 0.5 to 1.5
- w_qkv: bfloat16 [1024, 3072], replicated, may hold values from -0.1875 to 0.1875
- w_self_out: bfloat16 [1024, 1024], replicated, may hold values from -1.5 to 1.5
- gain_mlp: float32 [1024], replicated, may hold values from 0.5 to 1.5
- w_in: bfloat16 [1024, 4096], replicated, may hold values from -0.1875 to 0.1875
- w_out: bfloat16 [4096, 1024], replicated, may hold values from -0.09375 to 0.09375
Outputs:
- out_latents: bfloat16 [4096, 1024], P('grp')
- grad_latents: float32 [4096, 1024], P('grp')
- grad_pixels: float32 [16, 1024, 1024], P('grp', 'pix')
- grad_gain_cross: float32 [1024], P(('grp', 'pix'))
- grad_gain_pixel: float32 [1024], P(('grp', 'pix'))
- grad_w_query: float32 [1024, 1024], P(('grp', 'pix'))
- grad_w_keyval: float32 [1024, 2048], P(('grp', 'pix'))
- grad_w_cross_out: float32 [1024, 1024], P(('grp', 'pix'))
- grad_gain_self: float32 [1024], P(('grp', 'pix'))
- grad_w_qkv: float32 [1024, 3072], P(('grp', 'pix'))
- grad_w_self_out: float32 [1024, 1024], P(('grp', 'pix'))
- grad_gain_mlp: float32 [1024], P(('grp', 'pix'))
- grad_w_in: float32 [1024, 4096], P(('grp', 'pix'))
- grad_w_out: float32 [4096, 1024], P(('grp', 'pix'))
- image_norms: float32 [8], replicated
The draws below stay inside these ranges and needn't reach their ends.
Inputs may be any that keep to these rules, and one draw needn't show every extreme that they name: `pixel_mask`: each group's pixels fill a prefix of its 1024 slots of length (1024 * s * s) // 82944 for an image side s of 160, 224 or 288; of every 2 groups in a row at least one has side 288 and fills all slots.
All inputs are finite; a program needn't handle non-finite values.
Results may differ from the reference program's by a relative error of at most 0.024.
Values may be sent and summed in bfloat16 or wider, within the bound.
No kernel may reach another device: no remote copies, remote signals or barrier semaphores. Data moves between devices by JAX's collectives and lax.ppermute only.
A program may use at most 256 MiB of HBM per device.

```python
import math
import jax
import jax.numpy as jnp
from jax import lax

D = 1024
HEADS = 8
FF = 4096
LAT = 256
G_DEV = 2
IMAGES = 8
GROUPS = 16
PG = 1024


def draw_pixel_mask(key, part):
    key = jax.random.fold_in(key, 11)
    pick_key, full_key = jax.random.split(key)
    side_list = jnp.array([160, 224, 288], jnp.int32)
    picked = jax.random.randint(pick_key, (GROUPS,), 0, 3)
    image_side = jnp.sum(jnp.where(picked[:, None] == jnp.arange(3, dtype=jnp.int32)[None, :], side_list[None, :], 0), axis=1)
    full_slot = jax.random.randint(full_key, (GROUPS // G_DEV,), 0, G_DEV)
    slot_index = jnp.arange(GROUPS, dtype=jnp.int32) % G_DEV
    is_full = slot_index == jnp.repeat(full_slot, G_DEV)
    image_side = jnp.where(is_full, 288, image_side)
    valid_count = PG * image_side * image_side // 82944
    return (jnp.arange(PG, dtype=jnp.int32)[None, :] < valid_count[:, None]).astype(jnp.int32)


def place_ends(values, stream_key, smallest, largest):
    longest = values.shape.index(max(values.shape))
    spots = []
    for shift in (0, 1):
        where = [jax.random.randint(jax.random.fold_in(stream_key, axis), (), 0, length) for axis, length in enumerate(values.shape)]
        where[longest] = (where[longest] + shift) % values.shape[longest]
        spots.append(tuple(where))
    return values.at[spots[0]].set(smallest).at[spots[1]].set(largest)


def levels(own_key, extent, pieces, smallest, largest):
    gain, own = 1.0, jax.random.fold_in(own_key, 6)
    for dim, blocks in pieces:
        heights = jnp.exp(jax.random.uniform(jax.random.fold_in(own, dim), (blocks,), jnp.float32, smallest / len(pieces), largest / len(pieces)))
        gain = gain * jnp.repeat(heights, extent[dim] // blocks).reshape([-1 if axis == dim else 1 for axis in range(len(extent))])
    return gain


def centred(own_key, dims, scale, most, shards=(), kind=jnp.bfloat16):
    factor_of = levels(own_key, dims, shards, -0.22, 0.18) if shards else 1.0
    drawn = jax.random.normal(own_key, dims, jnp.float32) * scale * factor_of
    return jnp.minimum(jnp.maximum(drawn, -most), most).astype(kind)


def setup_inputs(seed: int = 0) -> dict:
    arg_keys = jax.random.split(jax.random.key(seed), 17)
    latents = centred(arg_keys[0], (GROUPS * LAT, D), 1.0, 6.0, ((0, 8),))
    pixels = centred(arg_keys[1], (GROUPS, PG, D), 1.0, 6.0, ((0, 8), (1, 4)))
    pixel_mask = draw_pixel_mask(jax.random.fold_in(arg_keys[16], 71), 0)
    group_image = place_ends(jax.random.randint(arg_keys[3], (GROUPS,), 0, IMAGES), jax.random.fold_in(arg_keys[3], 1), 0, IMAGES - 1).astype(jnp.int32)
    cotangent = centred(arg_keys[4], (GROUPS * LAT, D), 1.0, 6.0, ((0, 8),))
    gain_cross = jnp.clip(1.0 + 0.1 * jax.random.normal(arg_keys[5], (D,), jnp.float32), 0.5, 1.5)
    gain_pixel = jnp.clip(1.0 + 0.1 * jax.random.normal(arg_keys[6], (D,), jnp.float32), 0.5, 1.5)
    w_query = centred(arg_keys[7], (D, D), D ** -0.5, 0.1875)
    w_keyval = centred(arg_keys[8], (D, 2 * D), D ** -0.5, 0.1875)
    w_cross_out = centred(arg_keys[9], (D, D), (D // 64) ** -0.5, 1.5)
    gain_self = jnp.clip(1.0 + 0.1 * jax.random.normal(arg_keys[10], (D,), jnp.float32), 0.5, 1.5)
    w_qkv = centred(arg_keys[11], (D, 3 * D), D ** -0.5, 0.1875)
    w_self_out = centred(arg_keys[12], (D, D), (D // 64) ** -0.5, 1.5)
    gain_mlp = jnp.clip(1.0 + 0.1 * jax.random.normal(arg_keys[13], (D,), jnp.float32), 0.5, 1.5)
    w_in = centred(arg_keys[14], (D, FF), D ** -0.5, 0.1875)
    w_out = centred(arg_keys[15], (FF, D), FF ** -0.5, 0.09375)
    return {"latents": latents, "pixels": pixels, "pixel_mask": pixel_mask, "group_image": group_image, "cotangent": cotangent, "gain_cross": gain_cross, "gain_pixel": gain_pixel, "w_query": w_query, "w_keyval": w_keyval, "w_cross_out": w_cross_out, "gain_self": gain_self, "w_qkv": w_qkv, "w_self_out": w_self_out, "gain_mlp": gain_mlp, "w_in": w_in, "w_out": w_out}


NEG_FILL = -1e+30
EPSILON = 1e-05
HIGH = lax.Precision.HIGHEST

@jax.custom_vjp
def low(v):
    return lax.optimization_barrier(v.astype(jnp.bfloat16)).astype(jnp.float32)

@jax.custom_vjp
def low_back(v):
    return v

def low_keep(v):
    return (low(v), None)

def low_pass(kept, grad):
    return (grad,)

def back_keep(v):
    return (v, None)

def back_low(kept, grad):
    return (low(grad),)
low.defvjp(low_keep, low_pass)
low_back.defvjp(back_keep, back_low)

def round_both(value_in):
    return low(low_back(value_in))

def matmul(left_side, right_side):
    return jnp.dot(left_side, right_side, precision=HIGH, preferred_element_type=jnp.float32)

def normalize(values, gain_vector):
    center = values - lax.optimization_barrier(jnp.mean(values, axis=-1, keepdims=True))
    spread = lax.optimization_barrier(jnp.mean(center * center, axis=-1, keepdims=True))
    return center * lax.rsqrt(spread + EPSILON) * gain_vector

def attend(queries, key_rows, value_rows, valid_keys):
    row_total = queries.shape[0]
    head_size = queries.shape[1] // HEADS
    q_heads = queries.reshape(row_total, HEADS, head_size)
    k_heads = key_rows.reshape(key_rows.shape[0], HEADS, head_size)
    v_heads = value_rows.reshape(value_rows.shape[0], HEADS, head_size)
    scores = jnp.einsum('qhd,khd->hqk', q_heads, k_heads, precision=HIGH) * (1.0 / math.sqrt(head_size))
    scores = jnp.where(valid_keys[None, None, :], low_back(scores), NEG_FILL)
    row_max = lax.optimization_barrier(jnp.max(scores, axis=-1, keepdims=True))
    exp_weights = jnp.exp(scores - row_max)
    totals = lax.optimization_barrier(jnp.sum(exp_weights, axis=-1))
    numerator = low_back(jnp.einsum('hqk,khd->qhd', low(exp_weights), v_heads, precision=HIGH))
    return (numerator / jnp.transpose(totals)[:, :, None]).reshape(row_total, HEADS * head_size)

def group_block(latent_rows, pixel_rows, valid_keys, weights):
    gain_cross, gain_pixel, w_query, w_keyval, w_cross_out, gain_self, w_qkv, w_self_out, gain_mlp, w_in, w_out = weights
    x_norm = low(normalize(latent_rows, gain_cross))
    y_norm = low(normalize(pixel_rows, gain_pixel))
    queries = round_both(matmul(x_norm, w_query))
    keyval = round_both(matmul(y_norm, w_keyval))
    cross_out = low(attend(queries, keyval[:, :D], keyval[:, D:], valid_keys))
    x_cross = latent_rows + low_back(matmul(cross_out, w_cross_out))
    h_norm = low(normalize(x_cross, gain_self))
    qkv = round_both(matmul(h_norm, w_qkv))
    all_keys = jnp.ones((latent_rows.shape[0],), dtype=bool)
    self_out = low(attend(qkv[:, :D], qkv[:, D:2 * D], qkv[:, 2 * D:], all_keys))
    x_self = x_cross + low_back(matmul(self_out, w_self_out))
    m_norm = low(normalize(x_self, gain_mlp))
    activ = low_back(matmul(m_norm, w_in))
    hidden = low(jax.nn.gelu(activ))
    return x_self + low_back(matmul(hidden, w_out))

def forward(latent_input, pixel_input, weights, valid_all, image_of_group):
    latent_groups = latent_input.reshape(GROUPS, LAT, D)

    def one_group(group_args):
        return group_block(group_args[0], group_args[1], group_args[2], weights)
    final = lax.map(jax.checkpoint(one_group), (latent_groups, pixel_input, valid_all))
    group_norms = jnp.sqrt(lax.optimization_barrier(jnp.mean(final * final, axis=(1, 2))) + 1e-06)
    member = (image_of_group[:, None] == jnp.arange(IMAGES, dtype=jnp.int32)[None, :]).astype(jnp.float32)
    image_sums = lax.optimization_barrier(jnp.sum(member * group_norms[:, None], axis=0))
    counts = jnp.maximum(lax.optimization_barrier(jnp.sum(member, axis=0)), 1.0)
    return (final.reshape(GROUPS * LAT, D), image_sums / counts)

def reference(latents, pixels, pixel_mask, group_image, cotangent, gain_cross, gain_pixel, w_query, w_keyval, w_cross_out, gain_self, w_qkv, w_self_out, gain_mlp, w_in, w_out):
    weights = (gain_cross.astype(jnp.float32), gain_pixel.astype(jnp.float32), w_query.astype(jnp.float32), w_keyval.astype(jnp.float32), w_cross_out.astype(jnp.float32), gain_self.astype(jnp.float32), w_qkv.astype(jnp.float32), w_self_out.astype(jnp.float32), gain_mlp.astype(jnp.float32), w_in.astype(jnp.float32), w_out.astype(jnp.float32))
    valid_all = pixel_mask > 0

    def wrapped(latent_input, pixel_input, weight_tuple):
        return forward(latent_input, pixel_input, weight_tuple, valid_all, group_image)
    (final, averaged), pull_back = jax.vjp(wrapped, latents.astype(jnp.float32), pixels.astype(jnp.float32), weights)
    grad_in, grad_pix, grads = pull_back((cotangent.astype(jnp.float32), LAT * D * averaged))
    return (final.astype(jnp.bfloat16), grad_in, grad_pix, grads[0], grads[1], grads[2], grads[3], grads[4], grads[5], grads[6], grads[7], grads[8], grads[9], grads[10], averaged)
```

```python
import functools
import math

import jax
import jax.numpy as jnp
from jax import lax
from jax.experimental import pallas as pl
from jax.experimental.pallas import tpu as pltpu
from jax.sharding import PartitionSpec as P

HEADS = 8
IMAGES = 8
NEG_FILL = -1e30
EPSILON = 1e-05
BF = jnp.bfloat16
F32 = jnp.float32
LOG2E = 1.0 / math.log(2.0)
LANES = 128
ANY = pl.BlockSpec(memory_space=pl.ANY)
SM = pl.BlockSpec(memory_space=pltpu.SMEM)


def dot(left, right, left_dim, right_dim):
    return lax.dot_general(
        left, right, (((left_dim,), (right_dim,)), ((), ())), preferred_element_type=F32
    )


def tiles(total, most):
    return [(start, min(most, total - start)) for start in range(0, total, most)]


def span(index, size):
    return pl.ds(pl.multiple_of(index * size, size), size)


def loop(count, body):
    lax.fori_loop(0, count, lambda index, carry: (body(index), carry)[1], 0)


class Box:
    def __init__(self, ref, copy=None):
        self.ref, self.copy = ref, copy

    def ready(self):
        if self.copy is not None:
            self.copy.wait()
            self.copy = None
        return self.ref


class Slot:
    def __init__(self, ref, targets, sems):
        self.ref, self.copies, self.started = ref, [], False
        each = ref.shape[0] // len(targets)
        for i, target in enumerate(targets):
            source = ref if len(targets) == 1 else ref.at[pl.ds(i * each, each)]
            self.copies.append(pltpu.make_async_copy(source, target, sems.at[i]))

    def done(self):
        for copy in self.copies:
            copy.start()
        self.started = True


def call(kernel, scalars, loads, outs, scratch, flops):
    parts = [out[2] if len(out) > 2 else 1 for out in outs]
    targets = []
    for out, count in zip(outs, parts):
        shape = (out[0][0] // count,) + tuple(out[0][1:])
        targets += [jax.ShapeDtypeStruct(shape, out[1])] * count
    most = max(parts)

    def whole(*refs):
        refs = list(refs)

        def take(count):
            taken = refs[:count]
            del refs[:count]
            return taken

        scalar_refs, load_refs, target_refs = take(len(scalars)), take(len(loads)), take(len(targets))
        load_bufs, out_bufs, extra = take(len(loads)), take(len(outs)), take(len(scratch))
        load_sems, out_sems = refs
        boxes = []
        for i, (source, buf) in enumerate(zip(load_refs, load_bufs)):
            copy = pltpu.make_async_copy(source, buf, load_sems.at[i])
            copy.start()
            boxes.append(Box(buf, copy))
        slots = []
        for i, (buf, count) in enumerate(zip(out_bufs, parts)):
            slots.append(Slot(buf, target_refs[:count], out_sems.at[i]))
            del target_refs[:count]
        kernel(*scalar_refs, *boxes, *slots, *extra)
        for box in boxes:
            box.ready()
        for slot in slots:
            if not slot.started:
                slot.done()
        for slot in slots:
            for copy in slot.copies:
                copy.wait()

    moved = sum(a.size * a.dtype.itemsize for a in loads)
    return pl.pallas_call(
        whole,
        out_shape=targets,
        in_specs=[SM] * len(scalars) + [ANY] * len(loads),
        out_specs=[ANY] * len(targets),
        scratch_shapes=[pltpu.VMEM(a.shape, a.dtype) for a in loads]
        + [pltpu.VMEM(out[0], out[1]) for out in outs]
        + list(scratch)
        + [pltpu.SemaphoreType.DMA((len(loads),)), pltpu.SemaphoreType.DMA((len(outs), most))],
        compiler_params=pltpu.CompilerParams(vmem_limit_bytes=60 * 2**20),
        cost_estimate=pl.CostEstimate(flops=int(flops), bytes_accessed=int(moved), transcendentals=0),
    )(*scalars, *loads)


def norm_rows(src, gain, dst, rstd, step=128):
    rows = src.shape[0]

    def body(i):
        sl = span(i, step)
        values = src[sl, :].astype(F32)
        center = values - jnp.mean(values, axis=-1, keepdims=True)
        spread = jnp.mean(center * center, axis=-1, keepdims=True)
        scale = lax.rsqrt(spread + EPSILON)
        dst[sl, :] = (center * scale * gain[...]).astype(BF)
        rstd[sl, :] = jnp.broadcast_to(scale, (step, LANES))

    loop(rows // step, body)


def norm_back(dy, normed, rstd, gain, base, out, low, dgain, step=64):
    rows, width = dy.shape

    def body(i, total):
        sl = span(i, step)
        grad = dy[sl, :]
        normal = normed[sl, :].astype(F32)
        gains = gain[...]
        with_norm = grad * normal
        scaled = grad * gains
        mean_scaled = jnp.mean(scaled, axis=-1, keepdims=True)
        mean_norm = jnp.mean(with_norm, axis=-1, keepdims=True)
        result = rstd[sl, :1] * (scaled - mean_scaled - normal * (1.0 / gains) * mean_norm)
        if base is not None:
            result = result + base[sl, :]
        out[sl, :] = result
        if low is not None:
            low[sl, :] = result.astype(BF)
        return total + jnp.sum(with_norm.reshape(step // 8, 8, width), axis=0)

    total = lax.fori_loop(0, rows // step, body, jnp.zeros((8, width), F32))
    dgain[...] = jnp.sum(total, axis=0, keepdims=True) * (1.0 / gain[...])


def head(h, size, base=0):
    return slice(base + h * size, base + (h + 1) * size)


def attend(q, k, v, bias, factor):
    scores = dot(k, q, 1, 1) * factor
    if bias is not None:
        scores = scores + bias
    most = jnp.max(scores, axis=0, keepdims=True)
    weights = jnp.exp2(scores - most)
    total = jnp.sum(weights, axis=0, keepdims=True)
    out = dot(v, weights.astype(BF), 0, 0)
    return out * (1.0 / total), most + jnp.log(total) * LOG2E


def attend_back(q, k, v, bias, lse, d_out, delta, factor, scale):
    scores = dot(k, q, 1, 1) * factor
    if bias is not None:
        scores = scores + bias
    probs = jnp.exp2(scores - lse)
    d_probs = dot(v, d_out, 1, 0)
    d_scores = (probs * (d_probs - delta)).astype(BF)
    dk = dot(d_scores, q, 1, 0) * scale
    dv = dot(probs.astype(BF), d_out, 1, 1)
    dq = dot(d_scores, k, 0, 0) * scale
    return dq, dk, dv


def scatter_slot(me, target, members):
    different = target ^ me
    slot, left = 0, members
    while left > 1:
        left //= 2
        slot = slot + (different & 1) * left
        different = different >> 1
    return slot


def put_blocks(out, me, members, offset, values):
    each = values.shape[0] // members
    for target in range(members):
        out[scatter_slot(me, target, members), offset : offset + each, :] = values[
            target * each : (target + 1) * each
        ]


def pre_kernel(factor, x, gx, wq, y, gy, wkv, bias, xn, q, yn, kv, out_t, lse, rx, ry):
    groups, width, latents = out_t.ref.shape
    size = width // HEADS
    keys = y.ref.shape[0] // groups
    norm_rows(x.ready(), gx.ready(), xn.ref, rx.ref)
    xn.done(), rx.done()
    wq = wq.ready()
    for start, length in tiles(width, 1024):
        cols = slice(start, start + length)
        q.ref[:, cols] = dot(xn.ref[...], wq[:, cols], 1, 0).astype(BF)
    q.done()
    norm_rows(y.ready(), gy.ready(), yn.ref, ry.ref)
    yn.done(), ry.done()
    wkv, kv_ref = wkv.ready(), kv.ref

    def project(i):
        kv_ref[:, span(i, 1024)] = dot(yn.ref[...], wkv[:, span(i, 1024)], 1, 0).astype(BF)

    loop(2 * width // 1024, project)
    kv.done()
    bias = bias.ready()
    for g in range(groups):
        rows, cols = slice(g * latents, (g + 1) * latents), slice(g * keys, (g + 1) * keys)
        for h in range(HEADS):
            result, total = attend(
                q.ref[rows, head(h, size)], kv_ref[cols, head(h, size)],
                kv_ref[cols, head(h, size, width)], bias[cols, :], factor,
            )
            out_t.ref[g, head(h, size), :] = result.astype(BF)
            lse.ref[g, h : h + 1, :] = total


def forward_kernel(factor, block, shards, place, cross_t, x, wco, gself, wqkv, wso, gmlp, win, wout,
                   hn, qkv, self_t, lse, mn, slope, hid_out, xf, low, rself, rmlp, squares,
                   resid, hidden):
    groups, width, latents = cross_t.ref.shape
    size = width // HEADS
    wide = win.ref.shape[1]
    cross_t, x, wco = cross_t.ready(), x.ready(), wco.ready()
    for g in range(groups):
        rows = slice(g * latents, (g + 1) * latents)
        resid[rows, :] = x[rows, :].astype(F32) + dot(cross_t[g], wco[...], 0, 0)
    norm_rows(resid, gself.ready(), hn.ref, rself.ref)
    hn.done(), rself.done()
    wqkv = wqkv.ready()

    def project(i):
        qkv.ref[:, span(i, 1024)] = dot(hn.ref[...], wqkv[:, span(i, 1024)], 1, 0).astype(BF)

    loop(3 * width // 1024, project)
    qkv.done()
    for g in range(groups):
        rows = slice(g * latents, (g + 1) * latents)
        for h in range(HEADS):
            result, total = attend(
                qkv.ref[rows, head(h, size)], qkv.ref[rows, head(h, size, width)],
                qkv.ref[rows, head(h, size, 2 * width)], None, factor,
            )
            self_t.ref[g, head(h, size), :] = result.astype(BF)
            lse.ref[g, h : h + 1, :] = total
    self_t.done(), lse.done()
    wso = wso.ready()
    for g in range(groups):
        rows = slice(g * latents, (g + 1) * latents)
        resid[rows, :] += dot(self_t.ref[g], wso[...], 0, 0)
    norm_rows(resid, gmlp.ready(), mn.ref, rmlp.ref)
    mn.done(), rmlp.done()
    win = win.ready()

    def expand(i):
        act = dot(mn.ref[...], win[:, span(i, 1024)], 1, 0)
        root = math.sqrt(2.0 / math.pi)
        square = act * act
        half = 0.5 + 0.5 * jnp.tanh(act * (root + (root * 0.044715) * square))
        result = act * half
        hidden[:, span(i, 1024)] = result.astype(BF)
        bend = 2.0 * root + (6.0 * root * 0.044715) * square
        slope.ref[:, span(i, 1024)] = (half + result * (1.0 - half) * bend).astype(BF)

    loop(wide // 1024, expand)
    slope.done()
    if hid_out.ref.shape[1] == wide:
        hid_out.ref[...] = hidden[...]
    else:
        for g in range(wide // (block * shards)):
            start = pl.multiple_of(g * block * shards + place[0] * block, block)
            hid_out.ref[:, g * block : (g + 1) * block] = hidden[:, pl.ds(start, block)]
    hid_out.done()
    wout = wout.ready()
    for start, length in tiles(width, 512):
        cols = slice(start, start + length)
        xf.ref[:, cols] = resid[:, cols] + dot(hidden[...], wout[:, cols], 1, 0)
    xf.done()
    per = 64
    for g in range(groups):

        def body(i, total, g=g):
            sl = pl.ds(pl.multiple_of(g * latents + i * per, per), per)
            values = xf.ref[sl, :]
            low.ref[sl, :] = values.astype(BF)
            return total + jnp.sum((values * values).reshape(per // 8, 8, width), axis=0)

        squares.ref[g] = lax.fori_loop(0, latents // per, body, jnp.zeros((8, width), F32))


def mlp_back_kernel(members, me, fac, cot, xf, hid, wout, slope, win, sel, mn, rmlp, gmlp,
                    blocks, gself, r_self, dgain, r_low, d_act, d_mn):
    rows, width = xf.ref.shape
    groups = fac.shape[0]
    latents = rows // groups
    wide = slope.ref.shape[1]
    me = me[0]
    cot, xf = cot.ready(), xf.ready()
    for g in range(groups):
        sl = slice(g * latents, (g + 1) * latents)
        grad = cot[sl, :].astype(F32) + fac[g] * xf[sl, :]
        gself.ref[sl, :] = grad
        r_low[sl, :] = grad.astype(BF)
    put_blocks(blocks.ref, me, members, 0, dot(hid.ready()[...], r_low[...], 0, 0).astype(BF))
    below = hid.ref.shape[1] // members
    wout, slope = wout.ready(), slope.ready()

    def hidden_back(i):
        d_hidden = dot(r_low[...], wout[span(i, 1024), :], 1, 1)
        d_act[:, span(i, 1024)] = (slope[:, span(i, 1024)].astype(F32) * d_hidden).astype(BF)

    loop(wide // 1024, hidden_back)
    part = dot(sel.ready()[...], mn.ready()[...], 1, 1).astype(BF)
    each = part.shape[0] // members
    for j in range(wide // width):
        put_blocks(
            blocks.ref, me, members, below + j * each,
            dot(part, d_act[:, j * width : (j + 1) * width], 1, 0).astype(BF),
        )
    blocks.done()
    win = win.ready()
    for start, length in tiles(width, 512):
        d_mn[:, start : start + length] = dot(d_act[...], win[start : start + length, :], 1, 1)
    norm_back(d_mn, mn.ref, rmlp.ready(), gmlp.ready(), gself.ref, gself.ref, r_self.ref, dgain.ref)


def self_back_kernel(factor, scale, members, me, wso, r_self, self_t, lse, qkv, wqkv, hn, rself, gain,
                     gself, wco, cross_t, sel,
                     gcross, d_out_t, delta, dgain, blocks, d_t, d_qkv, d_hn, r_cross):
    groups, width, latents = self_t.ref.shape
    size = width // HEADS
    me = me[0]
    d_t[...] = dot(wso.ready()[...], r_self.ready()[...], 1, 1)
    self_t, lse, qkv = self_t.ready(), lse.ready(), qkv.ready()
    for g in range(groups):
        rows = slice(g * latents, (g + 1) * latents)
        for h in range(HEADS):
            d_out = d_t[head(h, size), rows]
            row_delta = jnp.sum(
                d_out * self_t[g, head(h, size), :].astype(F32), axis=0, keepdims=True
            )
            dq, dk, dv = attend_back(
                qkv[rows, head(h, size)], qkv[rows, head(h, size, width)],
                qkv[rows, head(h, size, 2 * width)], None, lse[g, h : h + 1, :],
                d_out.astype(BF), row_delta, factor, scale,
            )
            d_qkv[rows, head(h, size)] = dq.astype(BF)
            d_qkv[rows, head(h, size, width)] = dk.astype(BF)
            d_qkv[rows, head(h, size, 2 * width)] = dv.astype(BF)
    wqkv = wqkv.ready()
    for start, length in tiles(width, 512):
        d_hn[:, start : start + length] = dot(d_qkv[...], wqkv[start : start + length, :], 1, 1)
    hn = hn.ready()
    norm_back(d_hn, hn, rself.ready(), gain.ready(), gself.ready(), gcross.ref, r_cross, dgain.ref)
    gcross.done(), dgain.done()
    d_t[...] = dot(wco.ready()[...], r_cross[...], 1, 1)
    cross_t = cross_t.ready()
    for g in range(groups):
        rows = slice(g * latents, (g + 1) * latents)
        for h in range(HEADS):
            d_out = d_t[head(h, size), rows]
            delta.ref[g, h : h + 1, :] = jnp.sum(
                d_out * cross_t[g, head(h, size), :].astype(F32), axis=0, keepdims=True
            )
            d_out_t.ref[g, head(h, size), :] = d_out.astype(BF)
    d_out_t.done(), delta.done()
    sel = sel.ready()
    part = dot(sel[...], hn[...], 1, 1).astype(BF)
    each = part.shape[0] // members
    for j in range(3):
        put_blocks(
            blocks.ref, me, members, j * each,
            dot(part, d_qkv[:, j * width : (j + 1) * width], 1, 0).astype(BF),
        )
    for j, (source, low) in enumerate(((self_t, r_self.ref), (cross_t, r_cross))):
        total = 0.0
        for g in range(groups):
            rows = slice(g * latents, (g + 1) * latents)
            mine = dot(sel[...], source[g], 1, 0).astype(BF)
            total = total + dot(mine, low[rows, :], 1, 0)
        put_blocks(blocks.ref, me, members, (3 + j) * each, total.astype(BF))


def cross_back_kernel(factor, scale, q, kv, bias, lse, d_out_t, delta, dq, dkv):
    groups, width, latents = d_out_t.ref.shape
    size = width // HEADS
    keys = kv.ref.shape[0] // groups
    q, kv, bias, lse, d_out_t, delta = (box.ready() for box in (q, kv, bias, lse, d_out_t, delta))
    for g in range(groups):
        rows, cols = slice(g * latents, (g + 1) * latents), slice(g * keys, (g + 1) * keys)
        for h in range(HEADS):
            dq_h, dk_h, dv_h = attend_back(
                q[rows, head(h, size)], kv[cols, head(h, size)], kv[cols, head(h, size, width)],
                bias[cols, :], lse[g, h : h + 1, :], d_out_t[g, head(h, size), :],
                delta[g, h : h + 1, :], factor, scale,
            )
            dq.ref[g, :, head(h, size)] = dq_h.astype(BF)
            dkv.ref[cols, head(h, size)] = dk_h.astype(BF)
            dkv.ref[cols, head(h, size, width)] = dv_h.astype(BF)


def keyval_weight_kernel(yn, dkv, dwkv):
    yn, dkv = yn.ready(), dkv.ready()

    def body(i):
        dwkv.ref[:, span(i, 512)] = dot(yn[...], dkv[:, span(i, 512)], 0, 0).astype(BF)

    loop(dkv.shape[1] // 512, body)


def pixel_back_kernel(dkv, wkv, yn, ry, gy, gpix, dgain, d_yn):
    width = yn.ref.shape[1]
    dkv, wkv = dkv.ready(), wkv.ready()
    for start, length in tiles(width, 512):
        d_yn[:, start : start + length] = dot(dkv[...], wkv[start : start + length, :], 1, 1)
    norm_back(d_yn, yn.ready(), ry.ready(), gy.ready(), None, gpix.ref, None, dgain.ref)


def query_back_kernel(members, me, sel, xn, dq, wq, rx, gx, gcross, blocks, glat, dgain, d_xn):
    groups, latents, width = dq.ref.shape
    part = dot(sel.ready()[...], xn.ready()[...], 1, 1).astype(BF)
    dq = dq.ready()
    total = 0.0
    for g in range(groups):
        total = total + dot(part[:, g * latents : (g + 1) * latents], dq[g], 1, 0)
    put_blocks(blocks.ref, me[0], members, 0, total.astype(BF))
    blocks.done()
    wq = wq.ready()
    for g in range(groups):
        d_xn[g * latents : (g + 1) * latents, :] = dot(dq[g], wq[...], 1, 1)
    norm_back(d_xn, xn.ref, rx.ready(), gx.ready(), gcross.ready(), glat.ref, None, dgain.ref)


def line_total(own, axis, merge):
    count = lax.axis_size(axis)
    place = lax.axis_index(axis)

    def send(values, pairs):
        return jax.tree.map(lambda value: lax.ppermute(value, axis, pairs), values)

    def choose(test, first, second):
        return jax.tree.map(lambda a, b: jnp.where(test, a, b), first, second)

    half = count // 2
    for s in range(half - 1):
        got = send(own, [(s, s + 1), (count - 1 - s, count - 2 - s)])
        takes = (place == s + 1) | (place == count - 2 - s)
        own = choose(takes, merge(own, got), own)
    got = send(own, [(half - 1, half), (half, half - 1)])
    low_side = place < half
    own = merge(choose(low_side, own, got), choose(low_side, got, own))
    for s in range(half - 1):
        got = send(own, [(half - 1 - s, half - 2 - s), (half + s, half + 1 + s)])
        takes = (place == half - 2 - s) | (place == half + 1 + s)
        own = choose(takes, got, own)
    return own


def merge_outputs(first, second):
    out_a, lse_a = first
    out_b, lse_b = second
    most = jnp.maximum(lse_a, lse_b)
    weight_a, weight_b = jnp.exp2(lse_a - most), jnp.exp2(lse_b - most)
    total = weight_a + weight_b
    heads, queries = lse_a.shape
    part_a = (weight_a / total)[:, None, :]
    part_b = (weight_b / total)[:, None, :]
    shape = (heads, out_a.shape[0] // heads, queries)
    out = part_a * out_a.reshape(shape).astype(F32) + part_b * out_b.reshape(shape).astype(F32)
    return out.reshape(out_a.shape).astype(BF), most + jnp.log2(total)


def merge_sums(first, second):
    return (first.astype(F32) + second.astype(F32)).astype(BF)


def swap_sum(value, axis):
    count = lax.axis_size(axis)
    step = 1
    while step < count:
        value = value + lax.ppermute(value, axis, [(i, i ^ step) for i in range(count)])
        step *= 2
    return value


def scatter_blocks(keep, give, axis):
    count = lax.axis_size(axis)
    bits = count.bit_length() - 1

    def swap(value, bit):
        return lax.ppermute(value, axis, [(i, i ^ (1 << bit)) for i in range(count)])

    def add(first, second):
        return first.astype(F32) + second.astype(F32)

    total = add(keep, swap(give, 0))
    depth = keep.shape[1] // 2
    results = []
    for order, rows in ((range(1, bits), slice(0, depth)), (range(bits - 1, 0, -1), slice(depth, None))):
        part = total[:, rows].reshape((2,) * (bits - 1) + (depth, keep.shape[2]))
        left = list(range(1, bits))
        for bit in order:
            place = left.index(bit)
            own = lax.index_in_dim(part, 0, place, keepdims=False)
            other = lax.index_in_dim(part, 1, place, keepdims=False).astype(BF)
            left.remove(bit)
            part = add(own.astype(BF) if left else own, swap(other, bit))
        results.append(part)
    return jnp.concatenate(results, axis=0)


def per_device(latents, pixels, pixel_mask, group_image, cotangent, gain_cross, gain_pixel, w_query,
               w_keyval, w_cross_out, gain_self, w_qkv, w_self_out, gain_mlp, w_in, w_out):
    groups, keys, width = pixels.shape
    rows = latents.shape[0]
    per = rows // groups
    size = width // HEADS
    wide = w_in.shape[1]
    scale = 1.0 / math.sqrt(size)
    factor = scale * LOG2E
    shards, members = lax.axis_size("pix"), lax.axis_size("grp")
    place = lax.axis_index("pix")
    me = lax.axis_index("grp").reshape(1).astype(jnp.int32)
    block = width // (shards * members)
    wide_block = wide // (shards * members)
    mine = members * block

    y = pixels.reshape(groups * keys, width)
    bias = jnp.where(pixel_mask > 0, 0.0, NEG_FILL).astype(F32).reshape(groups * keys, 1)
    gx, gy, gs, gm = (g.reshape(1, width) for g in (gain_cross, gain_pixel, gain_self, gain_mlp))
    own_row = lax.broadcasted_iota(jnp.int32, (mine, width), 0)
    column = lax.broadcasted_iota(jnp.int32, (mine, width), 1)
    wanted = ((own_row // block) * shards + place) * block + own_row % block
    sel = (column == wanted).astype(BF)

    xn, q, yn, kv, out_t, lse, rx, ry = call(
        functools.partial(pre_kernel, factor), [],
        [latents, gx, w_query, y, gy, w_keyval, bias],
        [((rows, width), BF), ((rows, width), BF), ((groups * keys, width), BF),
         ((groups * keys, 2 * width), BF), ((groups, width, per), BF), ((groups, HEADS, per), F32),
         ((rows, LANES), F32), ((groups * keys, LANES), F32)],
        [], 2 * (rows * width * width + groups * keys * width * 2 * width),
    )

    pieces = []
    half_heads, half_width = HEADS // 2, width // 2
    for g in range(groups):
        for part in range(2):
            pieces.append(line_total(
                (out_t[g, part * half_width : (part + 1) * half_width],
                 lse[g, part * half_heads : (part + 1) * half_heads]),
                "pix", merge_outputs,
            ))
    cross_t = jnp.concatenate([piece[0] for piece in pieces], axis=0).reshape(groups, width, per)
    cross_lse = jnp.concatenate([piece[1] for piece in pieces], axis=0).reshape(groups, HEADS, per)

    own_hidden = wide // shards if wide_block % LANES == 0 else wide
    hn, qkv, self_t, self_lse, mn, slope, hid, xf, out_low, rself, rmlp, squares = call(
        functools.partial(forward_kernel, factor, wide_block, shards),
        [place.reshape(1).astype(jnp.int32)],
        [cross_t, latents, w_cross_out, gs, w_qkv, w_self_out, gm, w_in, w_out],
        [((rows, width), BF), ((rows, 3 * width), BF), ((groups, width, per), BF),
         ((groups, HEADS, per), F32), ((rows, width), BF), ((rows, wide), BF),
         ((rows, own_hidden), BF), ((rows, width), F32), ((rows, width), BF),
         ((rows, LANES), F32), ((rows, LANES), F32), ((groups, 8, width), F32)],
        [pltpu.VMEM((rows, width), F32), pltpu.VMEM((rows, wide), BF)],
        2 * rows * width * (5 * width + 2 * wide),
    )
    if own_hidden == wide:
        hid = lax.dynamic_index_in_dim(
            hid.reshape(rows, members, shards, wide_block), place, 2, keepdims=False
        ).reshape(rows, members * wide_block)

    norms = jnp.sqrt(jnp.sum(squares, axis=(1, 2)) / (per * width) + 1e-06)
    member = (group_image[:, None] == jnp.arange(IMAGES, dtype=jnp.int32)[None, :]).astype(F32)
    counts = jnp.maximum(swap_sum(jnp.sum(member, axis=0), "grp"), 1.0)
    averaged = swap_sum(jnp.sum(member * norms[:, None], axis=0), "grp") / counts
    fac = jnp.sum(member * (averaged / counts)[None, :], axis=1) / norms

    depth = wide_block + block * (wide // width)
    keep_mlp, give_mlp, grad_self, r_self, dg_mlp = call(
        functools.partial(mlp_back_kernel, members), [me, fac],
        [cotangent, xf, hid, w_out, slope, w_in, sel, mn, rmlp, gm],
        [((members, depth, width), BF, 2), ((rows, width), F32), ((rows, width), BF),
         ((1, width), F32)],
        [pltpu.VMEM((rows, width), BF), pltpu.VMEM((rows, wide), BF), pltpu.VMEM((rows, width), F32)],
        2 * rows * width * (2 * wide + 2 * wide // shards),
    )
    sum_mlp = scatter_blocks(keep_mlp, give_mlp, "grp")

    grad_cross, d_out_t, delta, dg_self, keep_self, give_self = call(
        functools.partial(self_back_kernel, factor, scale, members), [me],
        [w_self_out, r_self, self_t, self_lse, qkv, w_qkv, hn, rself, gs, grad_self, w_cross_out,
         cross_t, sel],
        [((rows, width), F32), ((groups, width, per), BF), ((groups, HEADS, per), F32),
         ((1, width), F32), ((members, 5 * block, width), BF, 2)],
        [pltpu.VMEM((width, rows), F32), pltpu.VMEM((rows, 3 * width), BF),
         pltpu.VMEM((rows, width), F32), pltpu.VMEM((rows, width), BF)],
        2 * rows * width * 7 * width,
    )
    sum_self = scatter_blocks(keep_self, give_self, "grp")

    dq, dkv = call(
        functools.partial(cross_back_kernel, factor, scale), [],
        [q, kv, bias, cross_lse, d_out_t, delta],
        [((groups, per, width), BF), ((groups * keys, 2 * width), BF)],
        [], 10 * rows * keys * width,
    )
    dq = jnp.stack([line_total(dq[g], "pix", merge_sums) for g in range(groups)])
    (dwkv,) = call(
        keyval_weight_kernel, [], [yn, dkv], [((width, 2 * width), BF)], [],
        2 * groups * keys * width * 2 * width,
    )
    sum_wkv = lax.psum_scatter(dwkv, ("grp", "pix"), scatter_dimension=0, tiled=True).astype(F32)
    grad_pixels, dg_pixel = call(
        pixel_back_kernel, [], [dkv, w_keyval, yn, ry, gy],
        [((groups * keys, width), F32), ((1, width), F32)],
        [pltpu.VMEM((groups * keys, width), F32)],
        2 * groups * keys * width * 2 * width,
    )
    keep_q, give_q, grad_latents, dg_cross = call(
        functools.partial(query_back_kernel, members), [me],
        [sel, xn, dq, w_query, rx, gx, grad_cross],
        [((members, block, width), BF, 2), ((rows, width), F32), ((1, width), F32)],
        [pltpu.VMEM((rows, width), F32)],
        2 * rows * width * width * 1.3,
    )
    sum_wq = scatter_blocks(keep_q, give_q, "grp")

    def own_gain(total):
        index = lax.axis_index("grp") * shards + place
        return lax.dynamic_slice_in_dim(total.reshape(width), index * block, block, 0)

    def wide_rows(value):
        return jnp.concatenate(jnp.split(value, value.shape[0] // block, axis=0), axis=1)

    sum_gains = swap_sum(jnp.concatenate([dg_self, dg_mlp], axis=0), "grp")
    sum_gx = swap_sum(dg_cross, "grp")
    sum_gy = swap_sum(swap_sum(dg_pixel, "grp"), "pix")
    return (
        out_low,
        grad_latents,
        grad_pixels.reshape(groups, keys, width),
        own_gain(sum_gx),
        own_gain(sum_gy),
        sum_wq,
        sum_wkv,
        sum_self[4 * block : 5 * block],
        own_gain(sum_gains[0]),
        wide_rows(sum_self[: 3 * block]),
        sum_self[3 * block : 4 * block],
        own_gain(sum_gains[1]),
        wide_rows(sum_mlp[wide_block:]),
        sum_mlp[:wide_block],
        averaged,
    )


def solution(mesh):
    both = ("grp", "pix")
    in_specs = (
        P("grp", None), P("grp", "pix", None), P("grp", "pix"), P("grp"), P("grp", None),
    ) + (P(),) * 11
    out_specs = (
        P("grp", None), P("grp", None), P("grp", "pix", None), P(both), P(both),
        P(both, None), P(both, None), P(both, None), P(both), P(both, None), P(both, None),
        P(both), P(both, None), P(both, None), P(),
    )
    return jax.shard_map(
        per_device, mesh=mesh, in_specs=in_specs, out_specs=out_specs, check_vma=False
    )
```

```python
import functools
import math

import jax
import jax.numpy as jnp
from jax import lax
from jax.experimental import pallas as pl
from jax.experimental.pallas import tpu as pltpu
from jax.sharding import PartitionSpec as P

HEADS = 8
IMAGES = 8
NEG_FILL = -1e30
EPSILON = 1e-05
BF = jnp.bfloat16
F32 = jnp.float32
LOG2E = 1.0 / math.log(2.0)
LANES = 128
ANY = pl.BlockSpec(memory_space=pl.ANY)
SM = pl.BlockSpec(memory_space=pltpu.SMEM)


def dot(left, right, left_dim, right_dim):
    return lax.dot_general(
        left, right, (((left_dim,), (right_dim,)), ((), ())), preferred_element_type=F32
    )


def tiles(total, most):
    return [(start, min(most, total - start)) for start in range(0, total, most)]


def span(index, size):
    return pl.ds(pl.multiple_of(index * size, size), size)


def loop(count, body):
    lax.fori_loop(0, count, lambda index, carry: (body(index), carry)[1], 0)


class Stack:
    def __init__(self, arrays, turn=None):
        self.arrays, self.turn = list(arrays), turn


class Box:
    def __init__(self, ref, copies):
        self.ref, self.copies = ref, copies

    def ready(self):
        for copy in self.copies:
            copy.wait()
        self.copies = []
        return self.ref


class Slot:
    def __init__(self, ref, targets, sems):
        self.ref, self.targets, self.sems, self.copies = ref, targets, sems, []

    def send(self, source):
        each = source.shape[0] // len(self.targets)
        for i, target in enumerate(self.targets):
            part = source if len(self.targets) == 1 else source.at[pl.ds(i * each, each)]
            copy = pltpu.make_async_copy(part, target, self.sems.at[i])
            copy.start()
            self.copies.append(copy)

    def done(self):
        self.send(self.ref)


def call(kernel, scalars, loads, outs, scratch, flops):
    loads = [item if isinstance(item, Stack) else Stack([item]) for item in loads]
    single = [len(item.arrays) == 1 for item in loads]
    parts = [out[2] if len(out) > 2 else 1 for out in outs]
    targets = []
    for out, count in zip(outs, parts):
        count = max(count, 1)
        shape = (out[0][0] // count,) + tuple(out[0][1:])
        targets += [jax.ShapeDtypeStruct(shape, out[1])] * count
    most = max(max(parts), 1)
    arrays = [array for item in loads for array in item.arrays]
    deep = max(len(item.arrays) for item in loads)

    def whole(*refs):
        refs = list(refs)

        def take(count):
            taken = refs[:count]
            del refs[:count]
            return taken

        scalar_refs = take(len(scalars))
        load_refs = [take(len(item.arrays)) for item in loads]
        target_refs = take(len(targets))
        load_bufs = take(len(loads))
        out_bufs = [take(1)[0] if count else None for count in parts]
        extra = take(len(scratch))
        load_sems, out_sems = refs
        boxes = []
        for i, (item, sources, buf) in enumerate(zip(loads, load_refs, load_bufs)):
            copies = []
            for j, source in enumerate(sources):
                target = buf
                if not single[i]:
                    count = len(sources)
                    where = j
                    if item.turn is not None:
                        where = lax.rem(scalar_refs[item.turn][0] + (count - j), count)
                    target = buf.at[where]
                copy = pltpu.make_async_copy(source, target, load_sems.at[i, j])
                copy.start()
                copies.append(copy)
            boxes.append(Box(buf, copies))
        slots = []
        for i, (buf, count) in enumerate(zip(out_bufs, parts)):
            count = max(count, 1)
            slots.append(Slot(buf, target_refs[:count], out_sems.at[i]))
            del target_refs[:count]
        kernel(*scalar_refs, *boxes, *slots, *extra)
        for box in boxes:
            box.ready()
        for slot in slots:
            if not slot.copies:
                slot.done()
        for slot in slots:
            for copy in slot.copies:
                copy.wait()

    moved = sum(a.size * a.dtype.itemsize for a in arrays)
    return pl.pallas_call(
        whole,
        out_shape=targets,
        in_specs=[SM] * len(scalars) + [ANY] * len(arrays),
        out_specs=[ANY] * len(targets),
        scratch_shapes=[
            pltpu.VMEM((() if one else (len(item.arrays),)) + item.arrays[0].shape, item.arrays[0].dtype)
            for item, one in zip(loads, single)
        ]
        + [pltpu.VMEM(out[0], out[1]) for out, count in zip(outs, parts) if count]
        + list(scratch)
        + [pltpu.SemaphoreType.DMA((len(loads), deep)), pltpu.SemaphoreType.DMA((len(outs), most))],
        compiler_params=pltpu.CompilerParams(vmem_limit_bytes=60 * 2**20),
        cost_estimate=pl.CostEstimate(flops=int(flops), bytes_accessed=int(moved), transcendentals=0),
    )(*scalars, *arrays)


def norm_rows(src, gain, dst, rstd, step=128):
    rows = src.shape[0]

    def body(i):
        sl = span(i, step)
        values = src[sl, :].astype(F32)
        center = values - jnp.mean(values, axis=-1, keepdims=True)
        spread = jnp.mean(center * center, axis=-1, keepdims=True)
        scale = lax.rsqrt(spread + EPSILON)
        dst[sl, :] = (center * scale * gain[...]).astype(BF)
        rstd[sl, :] = jnp.broadcast_to(scale, (step, LANES))

    loop(rows // step, body)


def norm_back(dy, normed, rstd, gain, base, out, low, step=64):
    def body(i):
        sl = span(i, step)
        grad = dy[sl, :]
        normal = normed[sl, :].astype(F32)
        gains = gain[...]
        scaled = grad * gains
        mean_scaled = jnp.mean(scaled, axis=-1, keepdims=True)
        mean_norm = jnp.mean(grad * normal, axis=-1, keepdims=True)
        result = rstd[sl, :1] * (scaled - mean_scaled - normal * (1.0 / gains) * mean_norm)
        if base is not None:
            result = result + base[sl, :]
        out[sl, :] = result
        if low is not None:
            low[sl, :] = result.astype(BF)

    loop(dy.shape[0] // step, body)


def head(h, size, base=0):
    return slice(base + h * size, base + (h + 1) * size)


def masked_scores(q, k, limit, factor):
    scores = dot(k, q, 1, 1) * factor
    if limit is not None:
        key = lax.broadcasted_iota(jnp.int32, scores.shape, 0)
        scores = jnp.where(key < limit, scores, NEG_FILL)
    return scores


def attend(q, k, v, limit, factor):
    scores = masked_scores(q, k, limit, factor)
    most = jnp.max(scores, axis=0, keepdims=True)
    weights = jnp.exp2(scores - most)
    total = jnp.sum(weights, axis=0, keepdims=True)
    out = dot(v, weights.astype(BF), 0, 0)
    return out * (1.0 / total), most + jnp.log(total) * LOG2E


def attend_back(q, k, v, limit, lse, d_out, delta, factor, scale):
    probs = jnp.exp2(masked_scores(q, k, limit, factor) - lse)
    d_probs = dot(v, d_out, 1, 0)
    d_scores = (probs * (d_probs - delta)).astype(BF)
    dk = dot(d_scores, q, 1, 0) * scale
    dv = dot(probs.astype(BF), d_out, 1, 1)
    dq = dot(d_scores, k, 0, 0) * scale
    return dq, dk, dv


def scatter_slot(me, target, members):
    different = target ^ me
    slot, left = 0, members
    while left > 1:
        left //= 2
        slot = slot + (different & 1) * left
        different = different >> 1
    return slot


def put_blocks(out, me, members, offset, values):
    each = values.shape[0] // members
    for target in range(members):
        out[scatter_slot(me, target, members), offset : offset + each, :] = values[
            target * each : (target + 1) * each
        ]


def shard_part(factor, shard, counts, q, yn, wkv, sel, kv, own_cols, out_t, lse):
    groups, width, latents = out_t.ref.shape
    size = width // HEADS
    keys = yn.shape[0] // groups
    kv_ref, wkv = kv.ref, wkv.ready()

    def project(i):
        kv_ref[:, span(i, 1024)] = dot(yn[...], wkv[:, span(i, 1024)], 1, 0).astype(BF)

    loop(2 * width // 1024, project)
    kv.done()
    own_cols.ref[...] = dot(sel.ready()[...], yn[...], 1, 1).astype(BF)
    own_cols.done()
    for g in range(groups):
        rows, cols = slice(g * latents, (g + 1) * latents), slice(g * keys, (g + 1) * keys)
        limit = counts[g] - shard * keys
        for h in range(HEADS):
            result, total = attend(
                q[rows, head(h, size)], kv_ref[cols, head(h, size)],
                kv_ref[cols, head(h, size, width)], limit, factor,
            )
            out_t.ref[g, head(h, size), :] = result.astype(BF)
            lse.ref[g, h : h + 1, :] = total


def pre_kernel(factor, counts, x, gx, wq, y, gy, wkv, sel,
               xn, q, yn, kv, own_cols, out_t, lse, rx, ry):
    width = x.ref.shape[1]
    norm_rows(x.ready(), gx.ready(), xn.ref, rx.ref)
    xn.done(), rx.done()
    wq = wq.ready()
    for start, length in tiles(width, 1024):
        cols = slice(start, start + length)
        q.ref[:, cols] = dot(xn.ref[...], wq[:, cols], 1, 0).astype(BF)
    q.done()
    norm_rows(y.ready(), gy.ready(), yn.ref, ry.ref)
    yn.done(), ry.done()
    shard_part(factor, 0, counts, q.ref, yn.ref, wkv, sel, kv, own_cols, out_t, lse)


def shard_kernel(factor, shard, counts, y, gy, wkv, sel, q, kv, own_cols, out_t, lse, yn, ry):
    groups, keys, _ = y.ref.shape
    y, gy = y.ready(), gy.ready()
    for g in range(groups):
        rows = pl.ds(g * keys, keys)
        norm_rows(y.at[g], gy, yn.at[rows], ry.at[rows])
    shard_part(factor, shard[0], counts, q.ready(), yn, wkv, sel, kv, own_cols, out_t, lse)


def forward_kernel(factor, block, shards, place, part_t, part_lse, x, wco, gself, wqkv, wso, gmlp, win, wout,
                   cross_t, cross_lse, hn, qkv, self_t, lse, mn, slope, hid_out, xf, low, rself, rmlp,
                   squares, resid, hidden):
    groups, width, latents = cross_t.ref.shape
    size = width // HEADS
    wide = win.ref.shape[1]
    part_lse, part_t = part_lse.ready(), part_t.ready()
    for g in range(groups):
        most = part_lse[0, g]
        for z in range(1, shards):
            most = jnp.maximum(most, part_lse[z, g])
        weights = [jnp.exp2(part_lse[z, g] - most) for z in range(shards)]
        total = functools.reduce(jnp.add, weights)
        cross_lse.ref[g] = most + jnp.log(total) * LOG2E
        weights = [weight / total for weight in weights]
        for h in range(HEADS):
            merged = functools.reduce(jnp.add, [
                weights[z][h : h + 1, :] * part_t[z, g, head(h, size), :].astype(F32)
                for z in range(shards)
            ])
            cross_t.ref[g, head(h, size), :] = merged.astype(BF)
    cross_t.done(), cross_lse.done()
    cross_t, x, wco = cross_t.ref, x.ready(), wco.ready()
    for g in range(groups):
        rows = slice(g * latents, (g + 1) * latents)
        resid[rows, :] = x[rows, :].astype(F32) + dot(cross_t[g], wco[...], 0, 0)
    norm_rows(resid, gself.ready(), hn.ref, rself.ref)
    hn.done(), rself.done()
    wqkv = wqkv.ready()

    def project(i):
        qkv.ref[:, span(i, 1024)] = dot(hn.ref[...], wqkv[:, span(i, 1024)], 1, 0).astype(BF)

    loop(3 * width // 1024, project)
    qkv.done()
    for g in range(groups):
        rows = slice(g * latents, (g + 1) * latents)
        for h in range(HEADS):
            result, total = attend(
                qkv.ref[rows, head(h, size)], qkv.ref[rows, head(h, size, width)],
                qkv.ref[rows, head(h, size, 2 * width)], None, factor,
            )
            self_t.ref[g, head(h, size), :] = result.astype(BF)
            lse.ref[g, h : h + 1, :] = total
    self_t.done(), lse.done()
    wso = wso.ready()
    for g in range(groups):
        rows = slice(g * latents, (g + 1) * latents)
        resid[rows, :] += dot(self_t.ref[g], wso[...], 0, 0)
    norm_rows(resid, gmlp.ready(), mn.ref, rmlp.ref)
    mn.done(), rmlp.done()
    win = win.ready()
    if hid_out.ref.shape[1] == wide:
        hidden = hid_out.ref

    def expand(i):
        act = dot(mn.ref[...], win[:, span(i, 1024)], 1, 0)
        root = math.sqrt(2.0 / math.pi)
        square = act * act
        half = 0.5 + 0.5 * jnp.tanh(act * (root + (root * 0.044715) * square))
        result = act * half
        hidden[:, span(i, 1024)] = result.astype(BF)
        bend = 2.0 * root + (6.0 * root * 0.044715) * square
        slope.ref[:, span(i, 1024)] = (half + result * (1.0 - half) * bend).astype(BF)

    loop(wide // 1024, expand)
    slope.done()
    if hid_out.ref.shape[1] != wide:
        for g in range(wide // (block * shards)):
            start = pl.multiple_of(g * block * shards + place[0] * block, block)
            hid_out.ref[:, g * block : (g + 1) * block] = hidden[:, pl.ds(start, block)]
    hid_out.done()
    wout = wout.ready()
    for start, length in tiles(width, 512):
        cols = slice(start, start + length)
        xf.ref[:, cols] = resid[:, cols] + dot(hidden[...], wout[:, cols], 1, 0)
    xf.done()
    per = 64
    for g in range(groups):

        def body(i, total, g=g):
            sl = pl.ds(pl.multiple_of(g * latents + i * per, per), per)
            values = xf.ref[sl, :]
            low.ref[sl, :] = values.astype(BF)
            return total + jnp.sum((values * values).reshape(per // 8, 8, width), axis=0)

        squares.ref[g] = lax.fori_loop(0, latents // per, body, jnp.zeros((8, width), F32))


def mlp_back_kernel(members, me, fac, cot, xf, hid, wout, slope, win, sel, mn, rmlp, gmlp,
                    blocks, gself, r_self, r_low, d_act, d_mn):
    rows, width = xf.ref.shape
    groups = fac.shape[0]
    latents = rows // groups
    wide = slope.ref.shape[1]
    me = me[0]
    cot, xf = cot.ready(), xf.ready()
    for g in range(groups):
        sl = slice(g * latents, (g + 1) * latents)
        grad = cot[sl, :].astype(F32) + fac[g] * xf[sl, :]
        gself.ref[sl, :] = grad
        r_low[sl, :] = grad.astype(BF)
    put_blocks(blocks.ref, me, members, 0, dot(hid.ready()[...], r_low[...], 0, 0).astype(BF))
    below = hid.ref.shape[1] // members
    wout, slope = wout.ready(), slope.ready()

    def hidden_back(i):
        d_hidden = dot(r_low[...], wout[span(i, 1024), :], 1, 1)
        d_act[:, span(i, 1024)] = (slope[:, span(i, 1024)].astype(F32) * d_hidden).astype(BF)

    loop(wide // 1024, hidden_back)
    part = dot(sel.ready()[...], mn.ready()[...], 1, 1).astype(BF)
    each = part.shape[0] // members
    for j in range(wide // width):
        put_blocks(
            blocks.ref, me, members, below + j * each,
            dot(part, d_act[:, j * width : (j + 1) * width], 1, 0).astype(BF),
        )
    blocks.done()
    win = win.ready()
    for start, length in tiles(width, 512):
        d_mn[:, start : start + length] = dot(d_act[...], win[start : start + length, :], 1, 1)
    norm_back(d_mn, mn.ref, rmlp.ready(), gmlp.ready(), gself.ref, gself.ref, r_self.ref)


def self_back_kernel(factor, scale, members, me, wso, r_self, self_t, lse, qkv, wqkv, hn, rself, gain,
                     gself, wco, cross_t, sel,
                     gcross, d_out_t, delta, blocks, d_t, d_qkv, d_hn, r_cross):
    groups, width, latents = self_t.ref.shape
    size = width // HEADS
    me = me[0]
    d_t[...] = dot(wso.ready()[...], r_self.ready()[...], 1, 1)
    self_t, lse, qkv = self_t.ready(), lse.ready(), qkv.ready()
    for g in range(groups):
        rows = slice(g * latents, (g + 1) * latents)
        for h in range(HEADS):
            d_out = d_t[head(h, size), rows]
            row_delta = jnp.sum(
                d_out * self_t[g, head(h, size), :].astype(F32), axis=0, keepdims=True
            )
            dq, dk, dv = attend_back(
                qkv[rows, head(h, size)], qkv[rows, head(h, size, width)],
                qkv[rows, head(h, size, 2 * width)], None, lse[g, h : h + 1, :],
                d_out.astype(BF), row_delta, factor, scale,
            )
            d_qkv[rows, head(h, size)] = dq.astype(BF)
            d_qkv[rows, head(h, size, width)] = dk.astype(BF)
            d_qkv[rows, head(h, size, 2 * width)] = dv.astype(BF)
    wqkv = wqkv.ready()
    for start, length in tiles(width, 512):
        d_hn[:, start : start + length] = dot(d_qkv[...], wqkv[start : start + length, :], 1, 1)
    hn = hn.ready()
    norm_back(d_hn, hn, rself.ready(), gain.ready(), gself.ready(), gcross.ref, r_cross)
    gcross.done()
    d_t[...] = dot(wco.ready()[...], r_cross[...], 1, 1)
    cross_t = cross_t.ready()
    for g in range(groups):
        rows = slice(g * latents, (g + 1) * latents)
        for h in range(HEADS):
            d_out = d_t[head(h, size), rows]
            delta.ref[g, h : h + 1, :] = jnp.sum(
                d_out * cross_t[g, head(h, size), :].astype(F32), axis=0, keepdims=True
            )
            d_out_t.ref[g, head(h, size), :] = d_out.astype(BF)
    d_out_t.done(), delta.done()
    sel = sel.ready()
    part = dot(sel[...], hn[...], 1, 1).astype(BF)
    each = part.shape[0] // members
    for j in range(3):
        put_blocks(
            blocks.ref, me, members, j * each,
            dot(part, d_qkv[:, j * width : (j + 1) * width], 1, 0).astype(BF),
        )
    for j, (source, low) in enumerate(((self_t, r_self.ref), (cross_t, r_cross))):
        total = 0.0
        for g in range(groups):
            rows = slice(g * latents, (g + 1) * latents)
            mine = dot(sel[...], source[g], 1, 0).astype(BF)
            total = total + dot(mine, low[rows, :], 1, 0)
        put_blocks(blocks.ref, me, members, (3 + j) * each, total.astype(BF))


def cross_back_kernel(factor, scale, members, shards, place, me, counts, q, d_out_t, lse, delta, kv, sel, xn,
                      own_cols, blocks, dq, dkv_own, dkv):
    groups, width, latents = d_out_t.ref.shape
    size = width // HEADS
    keys = kv.ref.shape[1] // groups
    q, d_out_t, lse, delta, kv = (box.ready() for box in (q, d_out_t, lse, delta, kv))

    def one_head(h):
        cols = span(h, size)
        value_cols = pl.ds(pl.multiple_of(width + h * size, size), size)
        for g in range(groups):
            rows = slice(g * latents, (g + 1) * latents)
            total = 0.0
            for z in range(shards):
                pixel_rows = slice(g * keys, (g + 1) * keys)
                dq_h, dk_h, dv_h = attend_back(
                    q[rows, cols], kv[z, pixel_rows, cols], kv[z, pixel_rows, value_cols],
                    counts[g] - z * keys, lse[g, pl.ds(h, 1), :], d_out_t[g, cols, :],
                    delta[g, pl.ds(h, 1), :], factor, scale,
                )
                total = total + dq_h
                dkv[z, pixel_rows, cols] = dk_h.astype(BF)
                dkv[z, pixel_rows, value_cols] = dv_h.astype(BF)
            dq.ref[rows, cols] = total.astype(BF)

    loop(HEADS, one_head)
    dq.done()
    dkv_own.send(dkv.at[place[0]])
    own_cols, sel, xn = own_cols.ready(), sel.ready(), xn.ready()
    each = sel.shape[0] // members
    for j in range(2):
        total = functools.reduce(jnp.add, [
            dot(own_cols[z], dkv[z, :, j * width : (j + 1) * width], 1, 0) for z in range(shards)
        ])
        put_blocks(blocks.ref, me[0], members, j * each, total.astype(BF))
    part = dot(sel[...], xn[...], 1, 1).astype(BF)
    put_blocks(blocks.ref, me[0], members, 2 * each, dot(part, dq.ref[...], 1, 0).astype(BF))


def pixel_back_kernel(dkv, wkv, yn, ry, gy, gpix, d_yn):
    width = yn.ref.shape[1]
    dkv, wkv = dkv.ready(), wkv.ready()
    for start, length in tiles(width, 512):
        d_yn[:, start : start + length] = dot(dkv[...], wkv[start : start + length, :], 1, 1)
    norm_back(d_yn, yn.ready(), ry.ready(), gy.ready(), None, gpix.ref, None)


def query_back_kernel(dq, wq, xn, rx, gx, gcross, glat, d_xn):
    d_xn[...] = dot(dq.ready()[...], wq.ready()[...], 1, 1)
    norm_back(d_xn, xn.ready(), rx.ready(), gx.ready(), gcross.ready(), glat.ref, None)


def swap_sum(value, axis):
    count = lax.axis_size(axis)
    step = 1
    while step < count:
        value = value + lax.ppermute(value, axis, [(i, i ^ step) for i in range(count)])
        step *= 2
    return value


class Scatter:
    def __init__(self, keep, give, axis):
        self.axis, self.count = axis, lax.axis_size(axis)
        bits = self.count.bit_length() - 1
        self.orders = [list(range(1, bits)), list(range(bits - 1, 0, -1))]
        self.left = [list(range(1, bits)) for _ in range(2)]
        self.keep, self.got = [keep], [self.swap(give, 0)]
        self.first = True

    def swap(self, value, bit):
        return lax.ppermute(value, self.axis, [(i, i ^ (1 << bit)) for i in range(self.count)])

    def step(self):
        totals = [a.astype(F32) + b.astype(F32) for a, b in zip(self.keep, self.got)]
        if self.first:
            self.first = False
            (total,) = totals
            depth, width = total.shape[1] // 2, total.shape[2]
            shape = (2,) * len(self.left[0]) + (depth, width)
            totals = [total[:, :depth].reshape(shape), total[:, depth:].reshape(shape)]
        if not self.orders[0]:
            self.keep = totals
            return
        self.keep, self.got = [], []
        for total, order, left in zip(totals, self.orders, self.left):
            bit = order.pop(0)
            place = left.index(bit)
            left.remove(bit)
            other = lax.index_in_dim(total, 1, place, keepdims=False).astype(BF)
            self.keep.append(lax.index_in_dim(total, 0, place, keepdims=False).astype(BF))
            self.got.append(self.swap(other, bit))

    def result(self):
        while self.orders[0]:
            self.step()
        self.step()
        return jnp.concatenate(self.keep, axis=0)


def after(value, *scatters):
    value, keeps = lax.optimization_barrier((value, [scatter.keep for scatter in scatters]))
    for scatter, keep in zip(scatters, keeps):
        scatter.keep = keep
    return value


def per_device(latents, pixels, pixel_mask, group_image, cotangent, gain_cross, gain_pixel, w_query,
               w_keyval, w_cross_out, gain_self, w_qkv, w_self_out, gain_mlp, w_in, w_out):
    groups, keys, width = pixels.shape
    rows = latents.shape[0]
    per = rows // groups
    size = width // HEADS
    wide = w_in.shape[1]
    scale = 1.0 / math.sqrt(size)
    factor = scale * LOG2E
    shards, members = lax.axis_size("pix"), lax.axis_size("grp")
    place = lax.axis_index("pix")
    me = lax.axis_index("grp").reshape(1).astype(jnp.int32)
    block = width // (shards * members)
    wide_block = wide // (shards * members)
    mine = members * block

    y = pixels.reshape(groups * keys, width)
    gx, gy, gs, gm = (g.reshape(1, width) for g in (gain_cross, gain_pixel, gain_self, gain_mlp))
    own_row = lax.broadcasted_iota(jnp.int32, (mine, width), 0)
    column = lax.broadcasted_iota(jnp.int32, (mine, width), 1)
    wanted = ((own_row // block) * shards + place) * block + own_row % block
    sel = (column == wanted).astype(BF)
    own_filled = jnp.sum(pixel_mask, axis=1, dtype=jnp.int32)
    filled = swap_sum(own_filled, "pix")

    turn = [(i, (i + 1) % shards) for i in range(shards)]
    moving = [pixels[g] for g in range(groups)]
    here = place.reshape(1).astype(jnp.int32)
    shapes = [((groups * keys, 2 * width), BF), ((mine, groups * keys), BF), ((groups, width, per), BF),
              ((groups, HEADS, per), F32)]
    stats = ((rows, LANES), F32)
    xn, q, yn, kv, own_cols, out_t, lse, rx, ry = call(
        functools.partial(pre_kernel, factor), [own_filled],
        [latents, gx, w_query, y, gy, w_keyval, sel],
        [((rows, width), BF), ((rows, width), BF), ((groups * keys, width), BF)] + shapes
        + [stats, ((groups * keys, LANES), F32)],
        [], 2 * (rows * width * width + groups * keys * width * 2 * width),
    )
    kvs, cols, outs_t, lses = [kv], [own_cols], [out_t], [lse]
    for s in range(1, shards):
        if s > 1:
            moving, lses[s - 2] = lax.optimization_barrier((moving, lses[s - 2]))
        moving = [lax.ppermute(value, "pix", turn) for value in moving]
        kv, own_cols, out_t, lse = call(
            functools.partial(shard_kernel, factor), [(here + (shards - s)) % shards, filled],
            [Stack(moving), gy, w_keyval, sel, q], shapes,
            [pltpu.VMEM((groups * keys, width), BF), pltpu.VMEM((groups * keys, LANES), F32)],
            2 * groups * keys * width * 2 * width,
        )
        for kept, value in ((kvs, kv), (cols, own_cols), (outs_t, out_t), (lses, lse)):
            kept.append(value)

    own_hidden = wide // shards if wide_block % LANES == 0 else wide
    cross_t, cross_lse, hn, qkv, self_t, self_lse, mn, slope, hid, xf, out_low, rself, rmlp, squares = call(
        functools.partial(forward_kernel, factor, wide_block, shards), [here],
        [Stack(outs_t, 0), Stack(lses, 0), latents, w_cross_out, gs, w_qkv, w_self_out, gm, w_in, w_out],
        [((groups, width, per), BF), ((groups, HEADS, per), F32),
         ((rows, width), BF), ((rows, 3 * width), BF), ((groups, width, per), BF),
         ((groups, HEADS, per), F32), ((rows, width), BF), ((rows, wide), BF),
         ((rows, own_hidden), BF), ((rows, width), F32), ((rows, width), BF),
         ((rows, LANES), F32), ((rows, LANES), F32), ((groups, 8, width), F32)],
        [pltpu.VMEM((rows, width), F32),
         pltpu.VMEM((rows if own_hidden != wide else 16, wide), BF)],
        2 * rows * width * (5 * width + 2 * wide),
    )
    if own_hidden == wide:
        hid = lax.dynamic_index_in_dim(
            hid.reshape(rows, members, shards, wide_block), place, 2, keepdims=False
        ).reshape(rows, members * wide_block)

    norms = jnp.sqrt(jnp.sum(squares, axis=(1, 2)) / (per * width) + 1e-06)
    member = (group_image[:, None] == jnp.arange(IMAGES, dtype=jnp.int32)[None, :]).astype(F32)
    counts = jnp.maximum(swap_sum(jnp.sum(member, axis=0), "grp"), 1.0)
    averaged = swap_sum(jnp.sum(member * norms[:, None], axis=0), "grp") / counts
    fac = jnp.sum(member * (averaged / counts)[None, :], axis=1) / norms

    depth = wide_block + block * (wide // width)
    keep_mlp, give_mlp, grad_self, r_self = call(
        functools.partial(mlp_back_kernel, members), [me, fac],
        [cotangent, xf, hid, w_out, slope, w_in, sel, mn, rmlp, gm],
        [((members, depth, width), BF, 2), ((rows, width), F32), ((rows, width), BF)],
        [pltpu.VMEM((rows, width), BF), pltpu.VMEM((rows, wide), BF), pltpu.VMEM((rows, width), F32)],
        2 * rows * width * (2 * wide + 2 * wide // shards),
    )
    scatter_mlp = Scatter(keep_mlp, give_mlp, "grp")

    grad_cross, d_out_t, delta, keep_self, give_self = call(
        functools.partial(self_back_kernel, factor, scale, members), [me],
        [w_self_out, r_self, self_t, self_lse, qkv, w_qkv, hn, rself, gs, grad_self, w_cross_out,
         cross_t, sel],
        [((rows, width), F32), ((groups, width, per), BF), ((groups, HEADS, per), F32),
         ((members, 5 * block, width), BF, 2)],
        [pltpu.VMEM((width, rows), F32), pltpu.VMEM((rows, 3 * width), BF),
         pltpu.VMEM((rows, width), F32), pltpu.VMEM((rows, width), BF)],
        2 * rows * width * 7 * width,
    )
    scatter_mlp.step()
    scatter_self = Scatter(keep_self, give_self, "grp")
    d_out_t = after(d_out_t, scatter_mlp)

    keep_cross, give_cross, dq, dkv = call(
        functools.partial(cross_back_kernel, factor, scale, members, shards), [here, me, filled],
        [q, d_out_t, cross_lse, delta, Stack(kvs, 0), sel, xn, Stack(cols, 0)],
        [((members, 3 * block, width), BF, 2), ((rows, width), BF), ((groups * keys, 2 * width), BF, 0)],
        [pltpu.VMEM((shards, groups * keys, 2 * width), BF)],
        2 * shards * groups * keys * width * (5 * per // 2 + 2 * mine),
    )
    scatter_cross = Scatter(keep_cross, give_cross, "grp")
    scatter_mlp.step()
    scatter_self.step()
    dkv = after(dkv, scatter_mlp, scatter_self)
    (grad_pixels,) = call(
        pixel_back_kernel, [], [dkv, w_keyval, yn, ry, gy],
        [((groups * keys, width), F32)],
        [pltpu.VMEM((groups * keys, width), F32)],
        2 * groups * keys * width * 2 * width,
    )
    scatter_cross.step()
    scatter_self.step()
    dq, grad_pixels = after((dq, grad_pixels), scatter_cross, scatter_self)
    (grad_latents,) = call(
        query_back_kernel, [], [dq, w_query, xn, rx, gx, grad_cross],
        [((rows, width), F32)],
        [pltpu.VMEM((rows, width), F32)],
        2 * rows * width * width,
    )

    def wide_rows(value):
        return jnp.concatenate(jnp.split(value, value.shape[0] // block, axis=0), axis=1)

    index = lax.axis_index("grp") * shards + place

    def own_gain(weight, d_weight, gain):
        rows_of = lax.dynamic_slice_in_dim(weight, index * block, block, 0).astype(F32)
        gains = lax.dynamic_slice_in_dim(gain, index * block, block, 0)
        return jnp.sum(rows_of * d_weight, axis=1) / gains

    sum_mlp, sum_self, sum_cross = scatter_mlp.result(), scatter_self.result(), scatter_cross.result()
    d_w_in, d_w_qkv = wide_rows(sum_mlp[wide_block:]), wide_rows(sum_self[: 3 * block])
    d_w_keyval, d_w_query = wide_rows(sum_cross[: 2 * block]), sum_cross[2 * block :]
    return (
        out_low,
        grad_latents,
        grad_pixels.reshape(groups, keys, width),
        own_gain(w_query, d_w_query, gain_cross),
        own_gain(w_keyval, d_w_keyval, gain_pixel),
        d_w_query,
        d_w_keyval,
        sum_self[4 * block : 5 * block],
        own_gain(w_qkv, d_w_qkv, gain_self),
        d_w_qkv,
        sum_self[3 * block : 4 * block],
        own_gain(w_in, d_w_in, gain_mlp),
        d_w_in,
        sum_mlp[:wide_block],
        averaged,
    )


def solution(mesh):
    both = ("grp", "pix")
    in_specs = (
        P("grp", None), P("grp", "pix", None), P("grp", "pix"), P("grp"), P("grp", None),
    ) + (P(),) * 11
    out_specs = (
        P("grp", None), P("grp", None), P("grp", "pix", None), P(both), P(both),
        P(both, None), P(both, None), P(both, None), P(both), P(both, None), P(both, None),
        P(both), P(both, None), P(both, None), P(),
    )
    return jax.shard_map(
        per_device, mesh=mesh, in_specs=in_specs, out_specs=out_specs, check_vma=False
    )
```

```python
import functools
import math

import jax
import jax.numpy as jnp
from jax import lax
from jax.experimental import pallas as pl
from jax.experimental.pallas import tpu as pltpu
from jax.sharding import PartitionSpec as P

HEADS = 8
IMAGES = 8
NEG_FILL = -1e30
EPSILON = 1e-05
BF = jnp.bfloat16
F32 = jnp.float32
LOG2E = 1.0 / math.log(2.0)
LANES = 128
HBM = pl.BlockSpec(memory_space=pltpu.HBM)
SM = pl.BlockSpec(memory_space=pltpu.SMEM)


def dot(left, right, left_dim, right_dim):
    return lax.dot_general(
        left, right, (((left_dim,), (right_dim,)), ((), ())), preferred_element_type=F32
    )


def tiles(total, most):
    return [(start, min(most, total - start)) for start in range(0, total, most)]


def span(index, size):
    return pl.ds(pl.multiple_of(index * size, size), size)


def loop(count, body):
    lax.fori_loop(0, count, lambda index, carry: (body(index), carry)[1], 0)


class Stack:
    separate = False

    def __init__(self, shape, dtype, pieces):
        self.shape, self.dtype, self.pieces = shape, dtype, pieces


def whole_of(array):
    return Stack(array.shape, array.dtype, [(array, None, None)])


def in_pieces(array, count):
    size = array.shape[0] // count
    pieces = [
        (array, lambda scalars, j=j: j, lambda scalars, j=j: pl.ds(j * size, size)) for j in range(count)
    ]
    stack = Stack((count, size) + array.shape[1:], array.dtype, pieces)
    stack.separate = True
    return stack


def part_of(array, start, size):
    def which(scalars):
        return pl.ds(pl.multiple_of(start(scalars), size) if callable(start) else start, size)

    return Stack((size,) + array.shape[1:], array.dtype, [(array, None, which)])


class Box:
    def __init__(self, ref, copies):
        self.ref, self.copies = ref, copies

    def ready(self):
        for copy in self.copies:
            copy.wait()
        self.copies = []
        return self.ref


class Pieces(Box):
    def __init__(self, ref, copies, sems):
        super().__init__(ref, [])
        self.sources, self.sems = copies, sems

    def wait_piece(self, index):
        pltpu.make_async_copy(self.sources[0], self.ref.at[index], self.sems.at[index]).wait()


class Slot:
    def __init__(self, ref, targets, sems):
        self.ref, self.targets, self.sems, self.copies = ref, targets, sems, []

    def send(self, source):
        each = source.shape[0] // len(self.targets)
        for i, target in enumerate(self.targets):
            part = source if len(self.targets) == 1 else source.at[pl.ds(i * each, each)]
            copy = pltpu.make_async_copy(part, target, self.sems.at[i])
            copy.start()
            self.copies.append(copy)

    def send_to(self, pieces):
        for i, (source, index) in enumerate(pieces):
            copy = pltpu.make_async_copy(source, self.targets[0].at[index], self.sems.at[i])
            copy.start()
            self.copies.append(copy)

    def done(self):
        self.send(self.ref)


def call(kernel, scalars, loads, outs, scratch, flops):
    loads = [item if isinstance(item, Stack) else whole_of(item) for item in loads]
    parts = [out[2] if len(out) > 2 else 1 for out in outs]
    targets = []
    for out, count in zip(outs, parts):
        count = max(count, 1)
        shape = (out[0][0] // count,) + tuple(out[0][1:])
        targets += [jax.ShapeDtypeStruct(shape, out[1])] * count
    most = max(max(parts), 2)
    arrays = [piece[0] for item in loads for piece in item.pieces]
    deep = max(len(item.pieces) for item in loads)

    def whole(*refs):
        refs = list(refs)

        def take(count):
            taken = refs[:count]
            del refs[:count]
            return taken

        scalar_refs = take(len(scalars))
        load_refs = [take(len(item.pieces)) for item in loads]
        target_refs = take(len(targets))
        load_bufs = take(len(loads))
        out_bufs = [take(1)[0] if count else None for count in parts]
        extra = take(len(scratch))
        load_sems, out_sems = refs
        boxes = []
        for i, (item, sources, buf) in enumerate(zip(loads, load_refs, load_bufs)):
            copies = []
            for j, (source, (_, where, which)) in enumerate(zip(sources, item.pieces)):
                copy = pltpu.make_async_copy(
                    source if which is None else source.at[which(scalar_refs)],
                    buf if where is None else buf.at[where(scalar_refs)],
                    load_sems.at[i, j],
                )
                copy.start()
                copies.append(copy)
            if item.separate:
                boxes.append(Pieces(buf, [source.at[item.pieces[0][2](scalar_refs)]], load_sems.at[i]))
            else:
                boxes.append(Box(buf, copies))
        slots = []
        for i, (buf, count) in enumerate(zip(out_bufs, parts)):
            count = max(count, 1)
            slots.append(Slot(buf, target_refs[:count], out_sems.at[i]))
            del target_refs[:count]
        kernel(*scalar_refs, *boxes, *slots, *extra)
        for box in boxes:
            box.ready()
        for slot in slots:
            if not slot.copies:
                slot.done()
        for slot in slots:
            for copy in slot.copies:
                copy.wait()

    moved = sum(a.size * a.dtype.itemsize for a in arrays)
    return pl.pallas_call(
        whole,
        out_shape=targets,
        in_specs=[SM] * len(scalars) + [HBM] * len(arrays),
        out_specs=[HBM] * len(targets),
        scratch_shapes=[pltpu.VMEM(item.shape, item.dtype) for item in loads]
        + [pltpu.VMEM(out[0], out[1]) for out, count in zip(outs, parts) if count]
        + list(scratch)
        + [pltpu.SemaphoreType.DMA((len(loads), deep)), pltpu.SemaphoreType.DMA((len(outs), most))],
        compiler_params=pltpu.CompilerParams(vmem_limit_bytes=60 * 2**20),
        cost_estimate=pl.CostEstimate(flops=int(flops), bytes_accessed=int(moved), transcendentals=0),
    )(*scalars, *arrays)


def norm_rows(src, gain, dst, rstd, step=128):
    rows = src.shape[0]

    def body(i):
        sl = span(i, step)
        values = src[sl, :].astype(F32)
        center = values - jnp.mean(values, axis=-1, keepdims=True)
        spread = jnp.mean(center * center, axis=-1, keepdims=True)
        scale = lax.rsqrt(spread + EPSILON)
        dst[sl, :] = (center * scale * gain[...]).astype(BF)
        rstd[sl, :] = jnp.broadcast_to(scale, (step, LANES))

    loop(rows // step, body)


def norm_back(dy, normed, rstd, gain, base, out, low, step=64):
    def body(i):
        sl = span(i, step)
        grad = dy[sl, :]
        normal = normed[sl, :].astype(F32)
        gains = gain[...]
        scaled = grad * gains
        mean_scaled = jnp.mean(scaled, axis=-1, keepdims=True)
        mean_norm = jnp.mean(grad * normal, axis=-1, keepdims=True)
        result = rstd[sl, :1] * (scaled - mean_scaled - normal * (1.0 / gains) * mean_norm)
        if base is not None:
            result = result + base[sl, :]
        out[sl, :] = result
        if low is not None:
            low[sl, :] = result.astype(BF)

    loop(dy.shape[0] // step, body)


def head(h, size, base=0):
    return slice(base + h * size, base + (h + 1) * size)


def attend(heads, limit, factor, scores, weights):
    for i, (q, k, _, _) in enumerate(heads):
        scores[i] = dot(k(), q(), 1, 1)
    totals = []
    for i in range(len(heads)):
        values = scores[i] * factor
        if limit is not None:
            key = lax.broadcasted_iota(jnp.int32, values.shape, 0)
            values = jnp.where(key < limit, values, NEG_FILL)
        most = jnp.max(values, axis=0, keepdims=True)
        values = jnp.exp2(values - most)
        total = jnp.sum(values, axis=0, keepdims=True)
        weights[i] = values.astype(BF)
        totals.append((1.0 / total, most + jnp.log(total) * LOG2E))
    for i, (_, _, v, put) in enumerate(heads):
        inverse, lse = totals[i]
        put(dot(v(), weights[i], 0, 0) * inverse, lse)


def attend_scratch(keys, queries):
    return [pltpu.VMEM((HEADS, keys, queries), F32), pltpu.VMEM((HEADS, keys, queries), BF)]


def scatter_slot(me, target, members):
    different = target ^ me
    slot, left = 0, members
    while left > 1:
        left //= 2
        slot = slot + (different & 1) * left
        different = different >> 1
    return slot


def put_blocks(out, me, members, offset, values):
    each = values.shape[0] // members
    for target in range(members):
        out[scatter_slot(me, target, members), offset : offset + each, :] = values[
            target * each : (target + 1) * each
        ]


def pre_kernel(factor, filled, x, gx, wq, y, gy, wkv, sel,
               xn, q, yn, kv, own_cols, out_t, lse, rx, ry, scores, weights):
    groups, width, latents = out_t.ref.shape
    size = width // HEADS
    keys = y.ref.shape[0] // groups
    norm_rows(x.ready(), gx.ready(), xn.ref, rx.ref)
    xn.done(), rx.done()
    wq = wq.ready()
    for start, length in tiles(width, 1024):
        cols = slice(start, start + length)
        q.ref[:, cols] = dot(xn.ref[...], wq[:, cols], 1, 0).astype(BF)
    q.done()
    norm_rows(y.ready(), gy.ready(), yn.ref, ry.ref)
    yn.done(), ry.done()
    kv_ref, wkv = kv.ref, wkv.ready()

    def project(i):
        kv_ref[:, span(i, 1024)] = dot(yn.ref[...], wkv[:, span(i, 1024)], 1, 0).astype(BF)

    loop(2 * width // 1024, project)
    kv.done()
    own_cols.ref[...] = dot(sel.ready()[...], yn.ref[...], 1, 1).astype(BF)
    own_cols.done()
    for g in range(groups):
        rows, cols = slice(g * latents, (g + 1) * latents), slice(g * keys, (g + 1) * keys)
        heads = []
        for h in range(HEADS):

            def put(result, total, h=h):
                out_t.ref[g, head(h, size), :] = result.astype(BF)
                lse.ref[g, h : h + 1, :] = total

            heads.append((
                lambda h=h: q.ref[rows, head(h, size)], lambda h=h: kv_ref[cols, head(h, size)],
                lambda h=h: kv_ref[cols, head(h, size, width)], put,
            ))
        attend(heads, filled[g], factor, scores, weights)


def shard_kernel(factor, group, y, gy, wkv, sel, q, filled, kv, own_cols, out_t, lse, yn, ry, scores, weights):
    width, latents = out_t.ref.shape
    size = width // HEADS
    norm_rows(y.ready(), gy.ready(), yn, ry)
    kv_ref, wkv = kv.ref, wkv.ready()

    def project(i):
        kv_ref[:, span(i, 1024)] = dot(yn[...], wkv[:, span(i, 1024)], 1, 0).astype(BF)

    loop(2 * width // 1024, project)
    kv.done()
    own_cols.ref[...] = dot(sel.ready()[...], yn[...], 1, 1).astype(BF)
    own_cols.done()
    q = q.ready()
    limit = filled.ready()[group : group + 1, :latents].astype(F32).astype(jnp.int32)
    heads = []
    for h in range(HEADS):

        def put(result, total, h=h):
            out_t.ref[head(h, size), :] = result.astype(BF)
            lse.ref[h : h + 1, :] = total

        heads.append((
            lambda h=h: q[:, head(h, size)], lambda h=h: kv_ref[:, head(h, size)],
            lambda h=h: kv_ref[:, head(h, size, width)], put,
        ))
    attend(heads, limit, factor, scores, weights)


def forward_kernel(factor, block, shards, place, part_t, part_lse, x, wco, gself, wqkv, wso, gmlp, win, wout,
                   cross_t, cross_lse, hn, qkv, self_t, lse, mn, slope, hid_out, xf, low, rself, rmlp,
                   squares, resid, hidden, scores, weights):
    groups, width, latents = cross_t.ref.shape
    size = width // HEADS
    wide = win.ref.shape[1]
    part_lse, part_t = part_lse.ready(), part_t.ready()
    for g in range(groups):
        most = part_lse[0, g]
        for z in range(1, shards):
            most = jnp.maximum(most, part_lse[z, g])
        shares = [jnp.exp2(part_lse[z, g] - most) for z in range(shards)]
        total = functools.reduce(jnp.add, shares)
        cross_lse.ref[g] = most + jnp.log(total) * LOG2E
        shares = [share / total for share in shares]
        for h in range(HEADS):
            merged = functools.reduce(jnp.add, [
                shares[z][h : h + 1, :] * part_t[z, g, head(h, size), :].astype(F32)
                for z in range(shards)
            ])
            cross_t.ref[g, head(h, size), :] = merged.astype(BF)
    cross_t.done(), cross_lse.done()
    cross_t, x, wco = cross_t.ref, x.ready(), wco.ready()
    for g in range(groups):
        rows = slice(g * latents, (g + 1) * latents)
        resid[rows, :] = x[rows, :].astype(F32) + dot(cross_t[g], wco[...], 0, 0)
    norm_rows(resid, gself.ready(), hn.ref, rself.ref)
    hn.done(), rself.done()
    wqkv = wqkv.ready()

    def project(i):
        qkv.ref[:, span(i, 1024)] = dot(hn.ref[...], wqkv[:, span(i, 1024)], 1, 0).astype(BF)

    loop(3 * width // 1024, project)
    qkv.done()
    for g in range(groups):
        rows = slice(g * latents, (g + 1) * latents)
        heads = []
        for h in range(HEADS):

            def put(result, total, h=h):
                self_t.ref[g, head(h, size), :] = result.astype(BF)
                lse.ref[g, h : h + 1, :] = total

            heads.append((
                lambda h=h: qkv.ref[rows, head(h, size)], lambda h=h: qkv.ref[rows, head(h, size, width)],
                lambda h=h: qkv.ref[rows, head(h, size, 2 * width)], put,
            ))
        attend(heads, None, factor, scores, weights)
    self_t.done(), lse.done()
    wso = wso.ready()
    for g in range(groups):
        rows = slice(g * latents, (g + 1) * latents)
        resid[rows, :] += dot(self_t.ref[g], wso[...], 0, 0)
    norm_rows(resid, gmlp.ready(), mn.ref, rmlp.ref)
    mn.done(), rmlp.done()
    win = win.ready()
    if hid_out.ref.shape[1] == wide:
        hidden = hid_out.ref

    def expand(i):
        act = dot(mn.ref[...], win[:, span(i, 1024)], 1, 0)
        root = math.sqrt(2.0 / math.pi)
        square = act * act
        half = 0.5 + 0.5 * jnp.tanh(act * (root + (root * 0.044715) * square))
        result = act * half
        hidden[:, span(i, 1024)] = result.astype(BF)
        bend = 2.0 * root + (6.0 * root * 0.044715) * square
        slope.ref[:, span(i, 1024)] = (half + result * (1.0 - half) * bend).astype(BF)

    loop(wide // 1024, expand)
    slope.done()
    if hid_out.ref.shape[1] != wide:
        for g in range(wide // (block * shards)):
            start = pl.multiple_of(g * block * shards + place[0] * block, block)
            hid_out.ref[:, g * block : (g + 1) * block] = hidden[:, pl.ds(start, block)]
    hid_out.done()
    wout = wout.ready()
    for start, length in tiles(width, 512):
        cols = slice(start, start + length)
        xf.ref[:, cols] = resid[:, cols] + dot(hidden[...], wout[:, cols], 1, 0)
    xf.done()
    per = 64
    for g in range(groups):

        def body(i, total, g=g):
            sl = pl.ds(pl.multiple_of(g * latents + i * per, per), per)
            values = xf.ref[sl, :]
            low.ref[sl, :] = values.astype(BF)
            return total + jnp.sum((values * values).reshape(per // 8, 8, width), axis=0)

        squares.ref[g] = lax.fori_loop(0, latents // per, body, jnp.zeros((8, width), F32))


def mlp_back_kernel(members, me, fac, cot, xf, wout, slope, hid, win, sel, mn, rmlp, gmlp,
                    blocks, gself, r_self, r_low, d_act, d_mn):
    rows, width = xf.ref.shape
    groups = fac.shape[0]
    latents = rows // groups
    wide = slope.ref.shape[1]
    me = me[0]
    cot, xf = cot.ready(), xf.ready()
    step = 64
    for g in range(groups):

        def add(i, g=g):
            sl = pl.ds(pl.multiple_of(g * latents + i * step, step), step)
            grad = cot[sl, :].astype(F32) + fac[g] * xf[sl, :]
            gself.ref[sl, :] = grad
            r_low[sl, :] = grad.astype(BF)

        loop(latents // step, add)
    slope, tile = slope.ready(), wout.ref.shape[1]

    def hidden_back(i):
        wout.wait_piece(i)
        cols = span(i, tile)
        d_hidden = dot(r_low[...], wout.ref[i], 1, 1)
        d_act[:, cols] = (slope[:, cols].astype(F32) * d_hidden).astype(BF)

    loop(wide // tile, hidden_back)
    put_blocks(blocks.ref, me, members, 0, dot(hid.ready()[...], r_low[...], 0, 0).astype(BF))
    below = hid.ref.shape[1] // members
    part = dot(sel.ready()[...], mn.ready()[...], 1, 1).astype(BF)
    each = part.shape[0] // members
    for j in range(wide // width):
        put_blocks(
            blocks.ref, me, members, below + j * each,
            dot(part, d_act[:, j * width : (j + 1) * width], 1, 0).astype(BF),
        )
    blocks.done()
    win = win.ready()
    for start, length in tiles(width, 512):
        d_mn[:, start : start + length] = dot(d_act[...], win[start : start + length, :], 1, 1)
    norm_back(d_mn, mn.ref, rmlp.ready(), gmlp.ready(), gself.ref, gself.ref, r_self.ref)


def self_back_kernel(factor, scale, members, me, wso, r_self, self_t, lse, qkv, hn, sel,
                     d_qkv, blocks, d_t, scores, probs, d_probs, d_scores, low):
    groups, width, latents = self_t.ref.shape
    size = width // HEADS
    me = me[0]
    d_t[...] = dot(wso.ready()[...], r_self.ready()[...], 1, 1)
    self_t, lse, qkv = self_t.ready(), lse.ready(), qkv.ready()
    for g in range(groups):
        rows = slice(g * latents, (g + 1) * latents)
        deltas = []
        for h in range(HEADS):
            d_out = d_t[head(h, size), rows]
            deltas.append(jnp.sum(
                d_out * self_t[g, head(h, size), :].astype(F32), axis=0, keepdims=True
            ))
            low[h] = d_out.astype(BF)
        for h in range(HEADS):
            scores[h] = dot(qkv[rows, head(h, size, width)], qkv[rows, head(h, size)], 1, 1)
            d_probs[h] = dot(qkv[rows, head(h, size, 2 * width)], low[h], 1, 0)
        for h in range(HEADS):
            values = jnp.exp2(scores[h] * factor - lse[g, h : h + 1, :])
            probs[h] = values.astype(BF)
            d_scores[h] = (values * (d_probs[h] - deltas[h])).astype(BF)
        for h in range(HEADS):
            dq = dot(qkv[rows, head(h, size, width)], d_scores[h], 0, 0) * scale
            d_qkv.ref[rows, head(h, size)] = dq.T.astype(BF)
            dk = dot(d_scores[h], qkv[rows, head(h, size)], 1, 0) * scale
            d_qkv.ref[rows, head(h, size, width)] = dk.astype(BF)
            dv = dot(probs[h], low[h], 1, 1)
            d_qkv.ref[rows, head(h, size, 2 * width)] = dv.astype(BF)
    d_qkv.done()
    sel = sel.ready()
    part = dot(sel[...], hn.ready()[...], 1, 1).astype(BF)
    each = part.shape[0] // members
    for j in range(3):
        put_blocks(
            blocks.ref, me, members, j * each,
            dot(part, d_qkv.ref[:, j * width : (j + 1) * width], 1, 0).astype(BF),
        )
    put_blocks(blocks.ref, me, members, 3 * each, weight_part(sel, self_t, r_self.ref))


def weight_part(sel, source_t, low):
    groups, _, latents = source_t.shape
    total = 0.0
    for g in range(groups):
        mine = dot(sel[...], source_t[g], 1, 0).astype(BF)
        total = total + dot(mine, low[g * latents : (g + 1) * latents, :], 1, 0)
    return total.astype(BF)


def between_kernel(d_qkv, wqkv, hn, rself, gain, gself, wco, cross_t,
                   r_cross, d_out_t, delta, gcross, d_hn, d_t):
    groups, width, latents = cross_t.ref.shape
    size = width // HEADS
    d_qkv, wqkv = d_qkv.ready(), wqkv.ready()
    for start, length in tiles(width, 512):
        d_hn[:, start : start + length] = dot(d_qkv[...], wqkv[start : start + length, :], 1, 1)
    norm_back(
        d_hn, hn.ready(), rself.ready(), gain.ready(), gself.ready(), gcross.ref, r_cross.ref
    )
    gcross.done(), r_cross.done()
    d_t[...] = dot(wco.ready()[...], r_cross.ref[...], 1, 1)
    cross_t = cross_t.ready()
    for g in range(groups):
        rows = slice(g * latents, (g + 1) * latents)
        for h in range(HEADS):
            d_out = d_t[head(h, size), rows]
            delta.ref[g, h : h + 1, :] = jnp.sum(
                d_out * cross_t[g, head(h, size), :].astype(F32), axis=0, keepdims=True
            )
            d_out_t.ref[g, head(h, size), :] = d_out.astype(BF)


def cross_back_kernel(factor, scale, members, place, me, filled, q, d_out_t, lse, delta, kv, sel, xn,
                      own_cols, cross_t, r_cross, blocks, more, dq, dkv_own, dkv):
    groups, width, latents = d_out_t.ref.shape
    size = width // HEADS
    keys = dkv_own.targets[0].shape[1]
    q, d_out_t, lse, delta, kv = (box.ready() for box in (q, d_out_t, lse, delta, kv))

    def one_head(h):
        cols = span(h, size)
        value_cols = pl.ds(pl.multiple_of(width + h * size, size), size)
        for g in range(groups):
            rows = slice(g * latents, (g + 1) * latents)
            q_h, k_h, d_out = q[rows, cols], kv[g, :, cols], d_out_t[g, cols, :]
            scores = dot(k_h, q_h, 1, 1) * factor
            key = lax.broadcasted_iota(jnp.int32, scores.shape, 0)
            scores = jnp.where(key < filled[g], scores, NEG_FILL)
            probs = jnp.exp2(scores - lse[g, pl.ds(h, 1), :])
            d_probs = dot(kv[g, :, value_cols], d_out, 1, 0)
            d_scores = (probs * (d_probs - delta[g, pl.ds(h, 1), :])).astype(BF)
            dkv[g, :, cols] = (dot(d_scores, q_h, 1, 0) * scale).astype(BF)
            dkv[g, :, value_cols] = dot(probs.astype(BF), d_out, 1, 1).astype(BF)
            dq.ref[rows, cols] = (dot(k_h, d_scores, 0, 0) * scale).T.astype(BF)

    def some_heads(i):
        for j in range(2):
            one_head(2 * i + j)

    loop(HEADS // 2, some_heads)
    dq.done()
    own_rows = pl.ds(pl.multiple_of(place[0] * keys, keys), keys)
    dkv_own.send_to([(dkv.at[g, own_rows], g) for g in range(groups)])
    own_cols, sel, xn = own_cols.ready(), sel.ready(), xn.ready()
    each = sel.shape[0] // members
    for j in range(2):
        total = functools.reduce(jnp.add, [
            dot(own_cols[g], dkv[g, :, j * width : (j + 1) * width], 1, 0) for g in range(groups)
        ])
        put_blocks(blocks.ref, me[0], members, j * each, total.astype(BF))
    blocks.done()
    part = dot(sel[...], xn[...], 1, 1).astype(BF)
    put_blocks(more.ref, me[0], members, 0, dot(part, dq.ref[...], 1, 0).astype(BF))
    put_blocks(more.ref, me[0], members, each, weight_part(sel, cross_t.ready(), r_cross.ready()))


def pixel_back_kernel(dkv, wkv, yn, ry, gy, gpix, d_yn):
    width = yn.ref.shape[1]
    dkv, wkv = dkv.ready(), wkv.ready()
    for start, length in tiles(width, 512):
        d_yn[:, start : start + length] = dot(dkv[...], wkv[start : start + length, :], 1, 1)
    norm_back(d_yn, yn.ready(), ry.ready(), gy.ready(), None, gpix.ref, None)


def query_back_kernel(dq, wq, xn, rx, gx, gcross, glat, d_xn):
    d_xn[...] = dot(dq.ready()[...], wq.ready()[...], 1, 1)
    norm_back(d_xn, xn.ready(), rx.ready(), gx.ready(), gcross.ready(), glat.ref, None)


def finish_kernel(heights, gained, index, keep, got, *refs):
    keep, got = keep.ready(), got.ready()
    weights, gains = refs[: len(gained)], refs[len(gained) : 2 * len(gained)]
    outs = refs[2 * len(gained) :]
    width = keep.shape[1]
    start = 0
    for i, pieces in enumerate(heights):
        for j, height in enumerate(pieces):
            rows = slice(start, start + height)
            outs[i].ref[:, j * width : (j + 1) * width] = keep[rows, :].astype(F32) + got[rows, :].astype(F32)
            start += height
        outs[i].done()
    for n, i in enumerate(gained):
        products = weights[n].ready()[...].astype(F32) * outs[i].ref[...]
        ones = jnp.ones((8, products.shape[1]), F32)
        sums = lax.dot_general(
            ones, products, (((1,), (1,)), ((), ())),
            precision=lax.Precision.HIGHEST, preferred_element_type=F32,
        )
        outs[len(heights) + n].ref[...] = sums[:1, :] / gains[n].ready()[...]


def swap_sum(value, axis):
    count = lax.axis_size(axis)
    step = 1
    while step < count:
        value = value + lax.ppermute(value, axis, [(i, i ^ step) for i in range(count)])
        step *= 2
    return value


class Scatter:
    def __init__(self, keep, give, axis, order):
        self.axis, self.count = axis, lax.axis_size(axis)
        bits = self.count.bit_length() - 1
        self.left = list(range(1, bits))
        self.order = [bit for bit in order if bit < bits] + [bit for bit in self.left if bit not in order]
        shape = (2,) * (bits - 1) + keep.shape[1:]
        self.keep, self.got = keep.reshape(shape), self.swap(give, 0).reshape(shape)

    def swap(self, value, bit):
        return lax.ppermute(value, self.axis, [(i, i ^ (1 << bit)) for i in range(self.count)])

    def step(self):
        bit = self.order.pop(0)
        place = self.left.index(bit)
        self.left.remove(bit)

        def half(which):
            first, second = (lax.index_in_dim(a, which, place, keepdims=False) for a in (self.keep, self.got))
            return (first.astype(F32) + second.astype(F32)).astype(BF)

        self.keep, self.got = half(0), self.swap(half(1), bit)

    def rest(self):
        while self.order:
            self.step()
        return self.keep, self.got


def after(value, *scatters):
    value, keeps = lax.optimization_barrier((value, [scatter.keep for scatter in scatters]))
    for scatter, keep in zip(scatters, keeps):
        scatter.keep = keep
    return value


def hold(value, *scatters):
    value, gots = lax.optimization_barrier((value, [scatter.got for scatter in scatters]))
    for scatter, got in zip(scatters, gots):
        scatter.got = got
    return value


def per_device(latents, pixels, pixel_mask, group_image, cotangent, gain_cross, gain_pixel, w_query,
               w_keyval, w_cross_out, gain_self, w_qkv, w_self_out, gain_mlp, w_in, w_out):
    groups, keys, width = pixels.shape
    rows = latents.shape[0]
    per = rows // groups
    size = width // HEADS
    wide = w_in.shape[1]
    scale = 1.0 / math.sqrt(size)
    factor = scale * LOG2E
    shards, members = lax.axis_size("pix"), lax.axis_size("grp")
    place = lax.axis_index("pix")
    me = lax.axis_index("grp").reshape(1).astype(jnp.int32)
    block = width // (shards * members)
    wide_block = wide // (shards * members)
    mine = members * block

    y = pixels.reshape(groups * keys, width)
    gx, gy, gs, gm = (g.reshape(1, width) for g in (gain_cross, gain_pixel, gain_self, gain_mlp))
    own_row = lax.broadcasted_iota(jnp.int32, (mine, width), 0)
    column = lax.broadcasted_iota(jnp.int32, (mine, width), 1)
    wanted = ((own_row // block) * shards + place) * block + own_row % block
    sel = (column == wanted).astype(BF)
    own_filled = jnp.sum(pixel_mask, axis=1, dtype=jnp.int32)
    extra = jnp.pad(own_filled.astype(BF), (0, 16 - groups))[:, None]
    turn = [(i, (i + 1) % shards) for i in range(shards)]
    moving = [jnp.concatenate([pixels[0], jnp.broadcast_to(extra, (16, width))], axis=0)]
    moving += [pixels[g] for g in range(1, groups)]
    here = place.reshape(1).astype(jnp.int32)
    stats = ((rows, LANES), F32)
    xn, q, yn, kv, own_cols, out_t, lse, rx, ry = call(
        functools.partial(pre_kernel, factor), [own_filled],
        [latents, gx, w_query, y, gy, w_keyval, sel],
        [((rows, width), BF), ((rows, width), BF), ((groups * keys, width), BF),
         ((groups * keys, 2 * width), BF), ((mine, groups * keys), BF), ((groups, width, per), BF),
         ((groups, HEADS, per), F32), stats, ((groups * keys, LANES), F32)],
        attend_scratch(keys, per), 2 * (rows * width * width + groups * keys * width * 2 * width),
    )

    def slot(s):
        return lambda scalars: lax.rem(scalars[0][0] + (shards - s), shards)

    def own_place(s, *index):
        return lambda scalars: (slot(s)(scalars),) + index

    def key_rows(s):
        return lambda scalars: pl.ds(pl.multiple_of(slot(s)(scalars) * keys, keys), keys)

    def kv_place(s, g):
        return lambda scalars: (g, key_rows(s)(scalars))

    def col_place(s, g):
        return lambda scalars: (g, slice(None), key_rows(s)(scalars))

    own = [pl.ds(g * keys, keys) for g in range(groups)]
    kv_pieces = [(kv, kv_place(0, g), lambda scalars, g=g: own[g]) for g in range(groups)]
    col_pieces = [
        (own_cols, col_place(0, g), lambda scalars, g=g: (slice(None), own[g])) for g in range(groups)
    ]
    out_pieces, lse_pieces = [(out_t, own_place(0), None)], [(lse, own_place(0), None)]
    filled = own_filled
    ahead = [lse, lse]
    for s in range(1, shards):
        for g in range(groups):
            if s > 1:
                moving[g], ahead[g] = lax.optimization_barrier((moving[g], ahead[g]))
            moving[g] = lax.ppermute(moving[g], "pix", turn)
        filled = filled + moving[0][keys : keys + groups, 0].astype(jnp.int32)
        for g in range(groups):
            kv, own_cols, out_t, lse = call(
                functools.partial(shard_kernel, factor, g), [],
                [part_of(moving[g], 0, keys), gy, w_keyval, sel, part_of(q, g * per, per),
                 part_of(moving[0], keys, 16)],
                [((keys, 2 * width), BF), ((mine, keys), BF), ((width, per), BF), ((HEADS, per), F32)],
                [pltpu.VMEM((keys, width), BF), pltpu.VMEM((keys, LANES), F32)] + attend_scratch(keys, per),
                2 * keys * width * 2 * width,
            )
            kv_pieces.append((kv, kv_place(s, g), None))
            col_pieces.append((own_cols, col_place(s, g), None))
            out_pieces.append((out_t, own_place(s, g), None))
            lse_pieces.append((lse, own_place(s, g), None))
            ahead[g] = lse

    own_hidden = wide // shards if wide_block % LANES == 0 else wide
    cross_t, cross_lse, hn, qkv, self_t, self_lse, mn, slope, hid, xf, out_low, rself, rmlp, squares = call(
        functools.partial(forward_kernel, factor, wide_block, shards), [here],
        [Stack((shards, groups, width, per), BF, out_pieces),
         Stack((shards, groups, HEADS, per), F32, lse_pieces), latents, w_cross_out, gs, w_qkv, w_self_out, gm, w_in, w_out],
        [((groups, width, per), BF), ((groups, HEADS, per), F32),
         ((rows, width), BF), ((rows, 3 * width), BF), ((groups, width, per), BF),
         ((groups, HEADS, per), F32), ((rows, width), BF), ((rows, wide), BF),
         ((rows, own_hidden), BF), ((rows, width), F32), ((rows, width), BF),
         ((rows, LANES), F32), ((rows, LANES), F32), ((groups, 8, width), F32)],
        [pltpu.VMEM((rows, width), F32),
         pltpu.VMEM((rows if own_hidden != wide else 16, wide), BF)] + attend_scratch(per, per),
        2 * rows * width * (5 * width + 2 * wide),
    )
    if own_hidden == wide:
        hid = lax.dynamic_index_in_dim(
            hid.reshape(rows, members, shards, wide_block), place, 2, keepdims=False
        ).reshape(rows, members * wide_block)

    norms = jnp.sqrt(jnp.sum(squares, axis=(1, 2)) / (per * width) + 1e-06)
    member = (group_image[:, None] == jnp.arange(IMAGES, dtype=jnp.int32)[None, :]).astype(F32)
    counts = jnp.maximum(swap_sum(jnp.sum(member, axis=0), "grp"), 1.0)
    averaged = swap_sum(jnp.sum(member * norms[:, None], axis=0), "grp") / counts
    fac = jnp.sum(member * (averaged / counts)[None, :], axis=1) / norms

    depth = wide_block + block * (wide // width)
    keep_mlp, give_mlp, grad_self, r_self = call(
        functools.partial(mlp_back_kernel, members), [me, fac],
        [cotangent, xf, in_pieces(w_out, 4), slope, hid, w_in, sel, mn, rmlp, gm],
        [((members, depth, width), BF, 2), ((rows, width), F32), ((rows, width), BF)],
        [pltpu.VMEM((rows, width), BF), pltpu.VMEM((rows, wide), BF), pltpu.VMEM((rows, width), F32)],
        2 * rows * width * (2 * wide + 2 * wide // shards),
    )
    scatter_mlp = Scatter(keep_mlp, give_mlp, "grp", [1, 2])

    d_qkv, keep_self, give_self = call(
        functools.partial(self_back_kernel, factor, scale, members), [me],
        [w_self_out, r_self, self_t, self_lse, qkv, hn, sel],
        [((rows, 3 * width), BF), ((members, 4 * block, width), BF, 2)],
        [pltpu.VMEM((width, rows), F32)] + attend_scratch(per, per) * 2 + [pltpu.VMEM((HEADS, size, per), BF)],
        2 * rows * width * 3 * width,
    )
    scatter_self = Scatter(keep_self, give_self, "grp", [2, 1])
    d_qkv = hold(d_qkv, scatter_mlp)
    scatter_mlp.step()
    d_qkv = after(d_qkv, scatter_mlp)

    r_cross, d_out_t, delta, grad_cross = call(
        between_kernel, [], [d_qkv, w_qkv, hn, rself, gs, grad_self, w_cross_out, cross_t],
        [((rows, width), BF), ((groups, width, per), BF), ((groups, HEADS, per), F32), ((rows, width), F32)],
        [pltpu.VMEM((rows, width), F32), pltpu.VMEM((width, rows), F32)],
        2 * rows * width * 4 * width,
    )
    d_out_t = hold(d_out_t, scatter_self)
    scatter_self.step()
    d_out_t = after(d_out_t, scatter_self)

    keep_keyval, give_keyval, keep_cross, give_cross, dq, dkv = call(
        functools.partial(cross_back_kernel, factor, scale, members), [here, me, filled],
        [q, d_out_t, cross_lse, delta, Stack((groups, shards * keys, 2 * width), BF, kv_pieces), sel, xn,
         Stack((groups, mine, shards * keys), BF, col_pieces), cross_t, r_cross],
        [((members, 2 * block, width), BF, 2), ((members, 2 * block, width), BF, 2), ((rows, width), BF),
         ((groups, keys, 2 * width), BF, 0)],
        [pltpu.VMEM((groups, shards * keys, 2 * width), BF)],
        2 * shards * groups * keys * width * (5 * per // 2 + 2 * mine),
    )
    scatter_keyval = Scatter(keep_keyval, give_keyval, "grp", [1, 2])
    scatter_cross = Scatter(keep_cross, give_cross, "grp", [2, 1])
    dq = hold(dq, scatter_mlp, scatter_self)
    scatter_mlp.step()
    scatter_self.step()
    dkv = after(dkv, scatter_mlp, scatter_self)
    (grad_pixels,) = call(
        pixel_back_kernel, [], [dkv.reshape(groups * keys, 2 * width), w_keyval, yn, ry, gy],
        [((groups * keys, width), F32)],
        [pltpu.VMEM((groups * keys, width), F32)],
        2 * groups * keys * width * 2 * width,
    )
    index = lax.axis_index("grp") * shards + place
    index_ref = index.reshape(1).astype(jnp.int32)
    all_gains = jnp.stack([gain_cross, gain_pixel, gain_self, gain_mlp])
    own_gains = lax.dynamic_slice_in_dim(all_gains, index * block, block, 1)

    def finish(scatter, heights, gained):
        keep, got = scatter.rest()
        wides = [(heights_of[0], width * len(heights_of)) for heights_of in heights]
        return call(
            functools.partial(finish_kernel, heights, list(gained)), [index_ref],
            [keep, got]
            + [part_of(weight, lambda scalars: scalars[0][0] * block, block) for weight, _ in gained.values()]
            + [own_gains[row : row + 1] for _, row in gained.values()],
            [(shape, F32) for shape in wides] + [((1, block), F32)] * len(gained),
            [], 1e6,
        )

    grad_pixels = hold(grad_pixels, scatter_keyval, scatter_cross, scatter_self)
    scatter_keyval.step()
    scatter_cross.step()
    grad_pixels = after(grad_pixels, scatter_keyval, scatter_cross)
    d_w_qkv, d_w_self_out, d_g_self = finish(scatter_self, [[block] * 3, [block]], {0: (w_qkv, 2)})
    dq, d_w_qkv, scatter_mlp.got = lax.optimization_barrier((dq, d_w_qkv, scatter_mlp.got))
    dq, grad_pixels = after((dq, grad_pixels), scatter_keyval, scatter_cross)
    (grad_latents,) = call(
        query_back_kernel, [], [dq, w_query, xn, rx, gx, grad_cross],
        [((rows, width), F32)],
        [pltpu.VMEM((rows, width), F32)],
        2 * rows * width * width,
    )

    grad_latents = hold(grad_latents, scatter_mlp, scatter_keyval, scatter_cross)
    scatter_keyval.step()
    scatter_cross.step()
    d_w_out, d_w_in, d_g_mlp = finish(
        scatter_mlp, [[wide_block], [block] * (wide // width)], {1: (w_in, 3)}
    )
    d_w_keyval, d_g_pixel = finish(scatter_keyval, [[block] * 2], {0: (w_keyval, 1)})
    d_w_query, d_w_cross_out, d_g_cross = finish(scatter_cross, [[block], [block]], {0: (w_query, 0)})
    return (
        out_low,
        grad_latents,
        grad_pixels.reshape(groups, keys, width),
        d_g_cross.reshape(block),
        d_g_pixel.reshape(block),
        d_w_query,
        d_w_keyval,
        d_w_cross_out,
        d_g_self.reshape(block),
        d_w_qkv,
        d_w_self_out,
        d_g_mlp.reshape(block),
        d_w_in,
        d_w_out,
        averaged,
    )


def solution(mesh):
    both = ("grp", "pix")
    in_specs = (
        P("grp", None), P("grp", "pix", None), P("grp", "pix"), P("grp"), P("grp", None),
    ) + (P(),) * 11
    out_specs = (
        P("grp", None), P("grp", None), P("grp", "pix", None), P(both), P(both),
        P(both, None), P(both, None), P(both, None), P(both), P(both, None), P(both, None),
        P(both), P(both, None), P(both, None), P(),
    )
    return jax.shard_map(
        per_device, mesh=mesh, in_specs=in_specs, out_specs=out_specs, check_vma=False
    )
```

```python
import functools
import math

import jax
import jax.numpy as jnp
from jax import lax
from jax.experimental import pallas as pl
from jax.experimental.pallas import tpu as pltpu
from jax.sharding import PartitionSpec as P

HEADS = 8
IMAGES = 8
NEG_FILL = -1e30
EPSILON = 1e-05
BF = jnp.bfloat16
F32 = jnp.float32
LOG2E = 1.0 / math.log(2.0)
LANES = 128
COUNTS = 64
HBM = pl.BlockSpec(memory_space=pltpu.HBM)
SM = pl.BlockSpec(memory_space=pltpu.SMEM)


def dot(left, right, left_dim, right_dim):
    return lax.dot_general(
        left, right, (((left_dim,), (right_dim,)), ((), ())), preferred_element_type=F32
    )


def tiles(total, most):
    return [(start, min(most, total - start)) for start in range(0, total, most)]


def span(index, size):
    return pl.ds(pl.multiple_of(index * size, size), size)


def loop(count, body):
    lax.fori_loop(0, count, lambda index, carry: (body(index), carry)[1], 0)


class Stack:
    separate = False

    def __init__(self, shape, dtype, pieces):
        self.shape, self.dtype, self.pieces = shape, dtype, pieces


def whole_of(array):
    return Stack(array.shape, array.dtype, [(array, None, None)])


def in_pieces(array, count):
    size = array.shape[0] // count
    pieces = [
        (array, lambda scalars, j=j: j, lambda scalars, j=j: pl.ds(j * size, size)) for j in range(count)
    ]
    stack = Stack((count, size) + array.shape[1:], array.dtype, pieces)
    stack.separate = True
    return stack


def part_of(array, start, size):
    def which(scalars):
        return pl.ds(pl.multiple_of(start(scalars), size) if callable(start) else start, size)

    return Stack((size,) + array.shape[1:], array.dtype, [(array, None, which)])


class Box:
    def __init__(self, ref, copies):
        self.ref, self.copies = ref, copies

    def ready(self):
        for copy in self.copies:
            copy.wait()
        self.copies = []
        return self.ref


class Pieces(Box):
    def __init__(self, ref, copies, sems):
        super().__init__(ref, [])
        self.sources, self.sems = copies, sems

    def wait_piece(self, index):
        pltpu.make_async_copy(self.sources[0], self.ref.at[index], self.sems.at[index]).wait()


class Slot:
    def __init__(self, ref, targets, sems):
        self.ref, self.targets, self.sems, self.copies = ref, targets, sems, []

    def send(self, source):
        each = source.shape[0] // len(self.targets)
        for i, target in enumerate(self.targets):
            part = source if len(self.targets) == 1 else source.at[pl.ds(i * each, each)]
            copy = pltpu.make_async_copy(part, target, self.sems.at[i])
            copy.start()
            self.copies.append(copy)

    def send_to(self, pieces):
        for i, (source, index) in enumerate(pieces):
            copy = pltpu.make_async_copy(source, self.targets[0].at[index], self.sems.at[i])
            copy.start()
            self.copies.append(copy)

    def done(self):
        self.send(self.ref)


def call(kernel, scalars, loads, outs, scratch, flops):
    loads = [item if isinstance(item, Stack) else whole_of(item) for item in loads]
    parts = [out[2] if len(out) > 2 else 1 for out in outs]
    targets = []
    for out, count in zip(outs, parts):
        count = max(count, 1)
        shape = (out[0][0] // count,) + tuple(out[0][1:])
        targets += [jax.ShapeDtypeStruct(shape, out[1])] * count
    most = max(max(parts), 2)
    arrays = [piece[0] for item in loads for piece in item.pieces]
    deep = max(len(item.pieces) for item in loads)

    def whole(*refs):
        refs = list(refs)

        def take(count):
            taken = refs[:count]
            del refs[:count]
            return taken

        scalar_refs = take(len(scalars))
        load_refs = [take(len(item.pieces)) for item in loads]
        target_refs = take(len(targets))
        load_bufs = take(len(loads))
        out_bufs = [take(1)[0] if count else None for count in parts]
        extra = take(len(scratch))
        load_sems, out_sems = refs
        boxes = []
        for i, (item, sources, buf) in enumerate(zip(loads, load_refs, load_bufs)):
            copies = []
            for j, (source, (_, where, which)) in enumerate(zip(sources, item.pieces)):
                copy = pltpu.make_async_copy(
                    source if which is None else source.at[which(scalar_refs)],
                    buf if where is None else buf.at[where(scalar_refs)],
                    load_sems.at[i, j],
                )
                copy.start()
                copies.append(copy)
            if item.separate:
                boxes.append(Pieces(buf, [source.at[item.pieces[0][2](scalar_refs)]], load_sems.at[i]))
            else:
                boxes.append(Box(buf, copies))
        slots = []
        for i, (buf, count) in enumerate(zip(out_bufs, parts)):
            count = max(count, 1)
            slots.append(Slot(buf, target_refs[:count], out_sems.at[i]))
            del target_refs[:count]
        kernel(*scalar_refs, *boxes, *slots, *extra)
        for box in boxes:
            box.ready()
        for slot in slots:
            if not slot.copies:
                slot.done()
        for slot in slots:
            for copy in slot.copies:
                copy.wait()

    moved = sum(a.size * a.dtype.itemsize for a in arrays)
    return pl.pallas_call(
        whole,
        out_shape=targets,
        in_specs=[SM] * len(scalars) + [HBM] * len(arrays),
        out_specs=[HBM] * len(targets),
        scratch_shapes=[pltpu.VMEM(item.shape, item.dtype) for item in loads]
        + [pltpu.VMEM(out[0], out[1]) for out, count in zip(outs, parts) if count]
        + list(scratch)
        + [pltpu.SemaphoreType.DMA((len(loads), deep)), pltpu.SemaphoreType.DMA((len(outs), most))],
        compiler_params=pltpu.CompilerParams(vmem_limit_bytes=60 * 2**20),
        cost_estimate=pl.CostEstimate(flops=int(flops), bytes_accessed=int(moved), transcendentals=0),
    )(*scalars, *arrays)


def norm_rows(src, gain, dst, rstd, step=128):
    rows = src.shape[0]

    def body(i):
        sl = span(i, step)
        values = src[sl, :].astype(F32)
        center = values - jnp.mean(values, axis=-1, keepdims=True)
        spread = jnp.mean(center * center, axis=-1, keepdims=True)
        scale = lax.rsqrt(spread + EPSILON)
        dst[sl, :] = (center * scale * gain[...]).astype(BF)
        rstd[sl, :] = jnp.broadcast_to(scale, (step, LANES))

    loop(rows // step, body)


def norm_back(dy, normed, rstd, gain, base, out, low, step=64):
    def body(i):
        sl = span(i, step)
        grad = dy[sl, :]
        normal = normed[sl, :].astype(F32)
        gains = gain[...]
        scaled = grad * gains
        mean_scaled = jnp.mean(scaled, axis=-1, keepdims=True)
        mean_norm = jnp.mean(grad * normal, axis=-1, keepdims=True)
        result = rstd[sl, :1] * (scaled - mean_scaled - normal * (1.0 / gains) * mean_norm)
        if base is not None:
            result = result + base[sl, :]
        out[sl, :] = result
        if low is not None:
            low[sl, :] = result.astype(BF)

    loop(dy.shape[0] // step, body)


def head(h, size, base=0):
    return slice(base + h * size, base + (h + 1) * size)


def attend(heads, limit, factor, scores, weights):
    for i, (q, k, _, _) in enumerate(heads):
        scores[i] = dot(k(), q(), 1, 1)
    totals = []
    for i in range(len(heads)):
        values = scores[i] * factor
        if limit is not None:
            key = lax.broadcasted_iota(jnp.int32, values.shape, 0)
            values = jnp.where(key < limit, values, NEG_FILL)
        most = jnp.max(values, axis=0, keepdims=True)
        values = jnp.exp2(values - most)
        total = jnp.sum(values, axis=0, keepdims=True)
        weights[i] = values.astype(BF)
        totals.append((1.0 / total, most + jnp.log(total) * LOG2E))
    for i, (_, _, v, put) in enumerate(heads):
        inverse, lse = totals[i]
        put(dot(v(), weights[i], 0, 0) * inverse, lse)


def attend_scratch(keys, queries):
    return [pltpu.VMEM((HEADS, keys, queries), F32), pltpu.VMEM((HEADS, keys, queries), BF)]


def scatter_slot(me, target, members):
    different = target ^ me
    slot, left = 0, members
    while left > 1:
        left //= 2
        slot = slot + (different & 1) * left
        different = different >> 1
    return slot


def put_blocks(out, me, members, offset, values):
    each = values.shape[0] // members
    for target in range(members):
        out[scatter_slot(me, target, members), offset : offset + each, :] = values[
            target * each : (target + 1) * each
        ]


def pre_kernel(factor, filled, x, gx, wq, y, gy, wkv, sel,
               xn, q, yn, kv, own_cols, out_t, lse, rx, ry, scores, weights):
    groups, width, latents = out_t.ref.shape
    size = width // HEADS
    keys = y.ref.shape[0] // groups
    norm_rows(x.ready(), gx.ready(), xn.ref, rx.ref)
    xn.done(), rx.done()
    wq = wq.ready()
    for start, length in tiles(width, 1024):
        cols = slice(start, start + length)
        q.ref[:, cols] = dot(xn.ref[...], wq[:, cols], 1, 0).astype(BF)
    q.done()
    norm_rows(y.ready(), gy.ready(), yn.ref, ry.ref)
    yn.done(), ry.done()
    kv_ref, wkv = kv.ref, wkv.ready()

    def project(i):
        kv_ref[:, span(i, 1024)] = dot(yn.ref[...], wkv[:, span(i, 1024)], 1, 0).astype(BF)

    loop(2 * width // 1024, project)
    kv.done()
    own_cols.ref[...] = dot(sel.ready()[...], yn.ref[...], 1, 1).astype(BF)
    own_cols.done()
    for g in range(groups):
        rows, cols = slice(g * latents, (g + 1) * latents), slice(g * keys, (g + 1) * keys)
        heads = []
        for h in range(HEADS):

            def put(result, total, h=h):
                out_t.ref[g, head(h, size), :] = result.astype(BF)
                lse.ref[g, h : h + 1, :] = total

            heads.append((
                lambda h=h: q.ref[rows, head(h, size)], lambda h=h: kv_ref[cols, head(h, size)],
                lambda h=h: kv_ref[cols, head(h, size, width)], put,
            ))
        attend(heads, filled[g], factor, scores, weights)


def shard_kernel(factor, group, y, gy, wkv, sel, q, filled, kv, own_cols, out_t, lse, yn, ry, scores, weights):
    width, latents = out_t.ref.shape
    shard_body(factor, group, y, gy, wkv, sel, q, filled, kv, own_cols, out_t.ref, lse.ref, yn, ry, scores, weights)


def shard_body(factor, group, y, gy, wkv, sel, q, filled, kv, own_cols, out_t, lse, yn, ry, scores, weights):
    width, latents = out_t.shape
    size = width // HEADS
    norm_rows(y.ready(), gy.ready(), yn, ry)
    kv_ref, wkv = kv.ref, wkv.ready()

    def project(i):
        kv_ref[:, span(i, 1024)] = dot(yn[...], wkv[:, span(i, 1024)], 1, 0).astype(BF)

    loop(2 * width // 1024, project)
    kv.done()
    own_cols.ref[...] = dot(sel.ready()[...], yn[...], 1, 1).astype(BF)
    own_cols.done()
    q = q.ready()
    limit = filled.ready()[group : group + 1, :latents].astype(F32).astype(jnp.int32)
    heads = []
    for h in range(HEADS):

        def put(result, total, h=h):
            out_t[head(h, size), :] = result.astype(BF)
            lse[h : h + 1, :] = total

        heads.append((
            lambda h=h: q[:, head(h, size)], lambda h=h: kv_ref[:, head(h, size)],
            lambda h=h: kv_ref[:, head(h, size, width)], put,
        ))
    attend(heads, limit, factor, scores, weights)


def last_shard_kernel(factor, group, shards, place, y, gy, wkv, sel, q, filled, part_t, part_lse,
                      kv, own_cols, out_t, lse, yn, ry, scores, weights):
    width, _ = out_t.ref.shape
    size = width // HEADS
    mine = lax.rem(place[0] + 1, shards)
    shard_body(
        factor, group, y, gy, wkv, sel, q, filled, kv, own_cols,
        part_t.ref.at[mine], part_lse.ref.at[mine], yn, ry, scores, weights,
    )
    part_t, part_lse = part_t.ready(), part_lse.ready()
    most = functools.reduce(jnp.maximum, [part_lse[z] for z in range(shards)])
    shares = [jnp.exp2(part_lse[z] - most) for z in range(shards)]
    total = functools.reduce(jnp.add, shares)
    lse.ref[...] = most + jnp.log(total) * LOG2E
    shares = [share / total for share in shares]
    for h in range(HEADS):
        merged = functools.reduce(jnp.add, [
            shares[z][h : h + 1, :] * part_t[z, head(h, size), :].astype(F32) for z in range(shards)
        ])
        out_t.ref[head(h, size), :] = merged.astype(BF)


def forward_kernel(factor, block, shards, place, image, cross_t, x, wco, gself, wqkv, wso, gmlp, win, wout,
                   hn, qkv, self_t, lse, mn, slope, hid_out, xf, low, rself, rmlp,
                   sums, norms, resid, hidden, scores, weights):
    groups, width, latents = cross_t.ref.shape
    size = width // HEADS
    wide = win.ref.shape[1]
    cross_t, x, wco = cross_t.ready(), x.ready(), wco.ready()
    for g in range(groups):
        rows = slice(g * latents, (g + 1) * latents)
        resid[rows, :] = x[rows, :].astype(F32) + dot(cross_t[g], wco[...], 0, 0)
    norm_rows(resid, gself.ready(), hn.ref, rself.ref)
    hn.done(), rself.done()
    wqkv = wqkv.ready()

    def project(i):
        qkv.ref[:, span(i, 1024)] = dot(hn.ref[...], wqkv[:, span(i, 1024)], 1, 0).astype(BF)

    loop(3 * width // 1024, project)
    qkv.done()
    for g in range(groups):
        rows = slice(g * latents, (g + 1) * latents)
        heads = []
        for h in range(HEADS):

            def put(result, total, h=h):
                self_t.ref[g, head(h, size), :] = result.astype(BF)
                lse.ref[g, h : h + 1, :] = total

            heads.append((
                lambda h=h: qkv.ref[rows, head(h, size)], lambda h=h: qkv.ref[rows, head(h, size, width)],
                lambda h=h: qkv.ref[rows, head(h, size, 2 * width)], put,
            ))
        attend(heads, None, factor, scores, weights)
    self_t.done(), lse.done()
    wso = wso.ready()
    for g in range(groups):
        rows = slice(g * latents, (g + 1) * latents)
        resid[rows, :] += dot(self_t.ref[g], wso[...], 0, 0)
    norm_rows(resid, gmlp.ready(), mn.ref, rmlp.ref)
    mn.done(), rmlp.done()
    win = win.ready()
    if hid_out.ref.shape[1] == wide:
        hidden = hid_out.ref

    def expand(i):
        act = dot(mn.ref[...], win[:, span(i, 1024)], 1, 0)
        root = math.sqrt(2.0 / math.pi)
        square = act * act
        half = 0.5 + 0.5 * jnp.tanh(act * (root + (root * 0.044715) * square))
        result = act * half
        hidden[:, span(i, 1024)] = result.astype(BF)
        bend = 2.0 * root + (6.0 * root * 0.044715) * square
        slope.ref[:, span(i, 1024)] = (half + result * (1.0 - half) * bend).astype(BF)

    loop(wide // 1024, expand)
    slope.done()
    if hid_out.ref.shape[1] != wide:
        for g in range(wide // (block * shards)):
            start = pl.multiple_of(g * block * shards + place[0] * block, block)
            hid_out.ref[:, g * block : (g + 1) * block] = hidden[:, pl.ds(start, block)]
    hid_out.done()
    wout = wout.ready()
    for start, length in tiles(width, 512):
        cols = slice(start, start + length)
        xf.ref[:, cols] = resid[:, cols] + dot(hidden[...], wout[:, cols], 1, 0)
    xf.done()
    per = 64
    lane = lax.broadcasted_iota(jnp.int32, (1, LANES), 1)
    found = jnp.zeros((1, LANES), F32)
    for g in range(groups):

        def body(i, total, g=g):
            sl = pl.ds(pl.multiple_of(g * latents + i * per, per), per)
            values = xf.ref[sl, :]
            low.ref[sl, :] = values.astype(BF)
            return total + jnp.sum((values * values).reshape(per // 8, 8, width), axis=0)

        total = lax.fori_loop(0, latents // per, body, jnp.zeros((8, width), F32))
        total = jnp.sum(jnp.sum(total, axis=1, keepdims=True), axis=0, keepdims=True)
        norm = jnp.sqrt(total / (latents * width) + 1e-06)
        norms.ref[g : g + 1, :] = jnp.broadcast_to(norm, (1, LANES))
        found = found + jnp.where(lane == image[g], norm, 0.0)
        found = found + jnp.where(lane == image[g] + COUNTS, 1.0, 0.0)
    sums.ref[...] = found


def mlp_back_kernel(members, me, image, sums, norms, cot, xf, wout, slope, hid, win, sel, mn, rmlp, gmlp,
                    blocks, gself, r_self, averaged, r_low, d_act, d_mn):
    rows, width = xf.ref.shape
    groups = image.shape[0]
    latents = rows // groups
    wide = slope.ref.shape[1]
    me = me[0]
    sums, norms = sums.ready()[...], norms.ready()
    lane = lax.broadcasted_iota(jnp.int32, (1, LANES), 1)
    counts = jnp.maximum(pltpu.roll(sums, COUNTS, 1), 1.0)
    means = sums / counts
    averaged.ref[...] = means[:, :IMAGES]
    shares = means / counts
    cot, xf = cot.ready(), xf.ready()
    step = 64
    for g in range(groups):
        share = jnp.sum(jnp.where(lane == image[g], shares, 0.0), axis=1, keepdims=True)
        fac = share / norms[g : g + 1, :1]

        def add(i, g=g, fac=fac):
            sl = pl.ds(pl.multiple_of(g * latents + i * step, step), step)
            grad = cot[sl, :].astype(F32) + fac * xf[sl, :]
            gself.ref[sl, :] = grad
            r_low[sl, :] = grad.astype(BF)

        loop(latents // step, add)
    slope, tile = slope.ready(), wout.ref.shape[1]

    def hidden_back(i):
        wout.wait_piece(i)
        cols = span(i, tile)
        d_hidden = dot(r_low[...], wout.ref[i], 1, 1)
        d_act[:, cols] = (slope[:, cols].astype(F32) * d_hidden).astype(BF)

    loop(wide // tile, hidden_back)
    put_blocks(blocks.ref, me, members, 0, dot(hid.ready()[...], r_low[...], 0, 0).astype(BF))
    below = hid.ref.shape[1] // members
    part = dot(sel.ready()[...], mn.ready()[...], 1, 1).astype(BF)
    each = part.shape[0] // members
    for j in range(wide // width):
        put_blocks(
            blocks.ref, me, members, below + j * each,
            dot(part, d_act[:, j * width : (j + 1) * width], 1, 0).astype(BF),
        )
    blocks.done()
    win = win.ready()
    for start, length in tiles(width, 512):
        d_mn[:, start : start + length] = dot(d_act[...], win[start : start + length, :], 1, 1)
    norm_back(d_mn, mn.ref, rmlp.ready(), gmlp.ready(), gself.ref, gself.ref, r_self.ref)


def self_back_kernel(factor, scale, members, me, wso, r_self, self_t, lse, qkv, hn, sel,
                     d_qkv, blocks, d_t, scores, probs, d_probs, d_scores, low):
    groups, width, latents = self_t.ref.shape
    size = width // HEADS
    me = me[0]
    d_t[...] = dot(wso.ready()[...], r_self.ready()[...], 1, 1)
    self_t, lse, qkv = self_t.ready(), lse.ready(), qkv.ready()
    for g in range(groups):
        rows = slice(g * latents, (g + 1) * latents)
        deltas = []
        for h in range(HEADS):
            d_out = d_t[head(h, size), rows]
            deltas.append(jnp.sum(
                d_out * self_t[g, head(h, size), :].astype(F32), axis=0, keepdims=True
            ))
            low[h] = d_out.astype(BF)
        for h in range(HEADS):
            scores[h] = dot(qkv[rows, head(h, size, width)], qkv[rows, head(h, size)], 1, 1)
            d_probs[h] = dot(qkv[rows, head(h, size, 2 * width)], low[h], 1, 0)
        for h in range(HEADS):
            values = jnp.exp2(scores[h] * factor - lse[g, h : h + 1, :])
            probs[h] = values.astype(BF)
            d_scores[h] = (values * (d_probs[h] - deltas[h])).astype(BF)
        for h in range(HEADS):
            dq = dot(qkv[rows, head(h, size, width)], d_scores[h], 0, 0) * scale
            d_qkv.ref[rows, head(h, size)] = dq.T.astype(BF)
            dk = dot(d_scores[h], qkv[rows, head(h, size)], 1, 0) * scale
            d_qkv.ref[rows, head(h, size, width)] = dk.astype(BF)
            dv = dot(probs[h], low[h], 1, 1)
            d_qkv.ref[rows, head(h, size, 2 * width)] = dv.astype(BF)
    d_qkv.done()
    sel = sel.ready()
    part = dot(sel[...], hn.ready()[...], 1, 1).astype(BF)
    each = part.shape[0] // members
    for j in range(3):
        put_blocks(
            blocks.ref, me, members, j * each,
            dot(part, d_qkv.ref[:, j * width : (j + 1) * width], 1, 0).astype(BF),
        )
    put_blocks(blocks.ref, me, members, 3 * each, weight_part(sel, self_t, r_self.ref))


def weight_part(sel, source_t, low):
    groups, _, latents = source_t.shape
    total = 0.0
    for g in range(groups):
        mine = dot(sel[...], source_t[g], 1, 0).astype(BF)
        total = total + dot(mine, low[g * latents : (g + 1) * latents, :], 1, 0)
    return total.astype(BF)


def between_kernel(d_qkv, wqkv, hn, rself, gain, gself, wco, cross_t, keep, got,
                   total, r_cross, d_out_t, delta, gcross, d_hn, d_t):
    groups, width, latents = cross_t.ref.shape
    size = width // HEADS
    d_qkv, wqkv = d_qkv.ready(), wqkv.ready()
    for start, length in tiles(width, 512):
        d_hn[:, start : start + length] = dot(d_qkv[...], wqkv[start : start + length, :], 1, 1)
    keep, got = keep.ready(), got.ready()

    def add(i):
        total.ref[i] = keep[i] + got[i]

    loop(keep.shape[0], add)
    total.done()
    norm_back(
        d_hn, hn.ready(), rself.ready(), gain.ready(), gself.ready(), gcross.ref, r_cross.ref
    )
    gcross.done(), r_cross.done()
    d_t[...] = dot(wco.ready()[...], r_cross.ref[...], 1, 1)
    cross_t = cross_t.ready()
    for g in range(groups):
        rows = slice(g * latents, (g + 1) * latents)
        for h in range(HEADS):
            d_out = d_t[head(h, size), rows]
            delta.ref[g, h : h + 1, :] = jnp.sum(
                d_out * cross_t[g, head(h, size), :].astype(F32), axis=0, keepdims=True
            )
            d_out_t.ref[g, head(h, size), :] = d_out.astype(BF)


def cross_back_kernel(factor, scale, members, groups, place, me, filled, q, d_out_t, lse, delta, *refs):
    kvs, refs = refs[:groups], refs[groups:]
    sel, xn, own_cols, cross_t, r_cross, blocks, more, dq, dkv_own, dkv = refs
    _, width, latents = d_out_t.ref.shape
    size = width // HEADS
    keys = dkv_own.targets[0].shape[1]
    q, d_out_t, lse, delta = (box.ready() for box in (q, d_out_t, lse, delta))
    for g in range(groups):
        kv = kvs[g].ready()
        rows = slice(g * latents, (g + 1) * latents)

        def one_head(h, g=g, kv=kv, rows=rows):
            cols = span(h, size)
            value_cols = pl.ds(pl.multiple_of(width + h * size, size), size)
            q_h, k_h, d_out = q[rows, cols], kv[:, cols], d_out_t[g, cols, :]
            scores = dot(k_h, q_h, 1, 1) * factor
            key = lax.broadcasted_iota(jnp.int32, scores.shape, 0)
            scores = jnp.where(key < filled[g], scores, NEG_FILL)
            probs = jnp.exp2(scores - lse[g, pl.ds(h, 1), :])
            d_probs = dot(kv[:, value_cols], d_out, 1, 0)
            d_scores = (probs * (d_probs - delta[g, pl.ds(h, 1), :])).astype(BF)
            dkv[g, :, cols] = (dot(d_scores, q_h, 1, 0) * scale).astype(BF)
            dkv[g, :, value_cols] = dot(probs.astype(BF), d_out, 1, 1).astype(BF)
            dq.ref[rows, cols] = (dot(k_h, d_scores, 0, 0) * scale).T.astype(BF)

        def some_heads(i):
            for j in range(4):
                one_head(4 * i + j)

        loop(HEADS // 4, some_heads)
    dq.done()
    own_rows = pl.ds(pl.multiple_of(place[0] * keys, keys), keys)
    dkv_own.send_to([(dkv.at[g, own_rows], g) for g in range(groups)])
    own_cols, sel, xn = own_cols.ready(), sel.ready(), xn.ready()
    each = sel.shape[0] // members
    for j in range(2):
        total = functools.reduce(jnp.add, [
            dot(own_cols[g], dkv[g, :, j * width : (j + 1) * width], 1, 0) for g in range(groups)
        ])
        put_blocks(blocks.ref, me[0], members, j * each, total.astype(BF))
    blocks.done()
    part = dot(sel[...], xn[...], 1, 1).astype(BF)
    put_blocks(more.ref, me[0], members, 0, dot(part, dq.ref[...], 1, 0).astype(BF))
    put_blocks(more.ref, me[0], members, each, weight_part(sel, cross_t.ready(), r_cross.ready()))


def pixel_back_kernel(dkv, wkv, yn, ry, gy, gpix, d_yn):
    times_pieces(d_yn, dkv.ready(), wkv)
    norm_back(d_yn, yn.ready(), ry.ready(), gy.ready(), None, gpix.ref, None)


def query_back_kernel(dq, wq, xn, rx, gx, gcross, glat, d_xn):
    times_pieces(d_xn, dq.ready(), wq)
    norm_back(d_xn, xn.ready(), rx.ready(), gx.ready(), gcross.ready(), glat.ref, None)


def times_pieces(out, left, weight):
    count, size, _ = weight.ref.shape

    def body(i):
        weight.wait_piece(i)
        out[:, span(i, size)] = dot(left[...], weight.ref[i], 1, 1)

    loop(count, body)


def finish_kernel(heights, gained, index, keep, got, *refs):
    keep, got = keep.ready(), got.ready()
    weights, gains = refs[: len(gained)], refs[len(gained) : 2 * len(gained)]
    outs = refs[2 * len(gained) :]
    width = keep.shape[1]
    start = 0
    for i, pieces in enumerate(heights):
        for j, height in enumerate(pieces):
            rows = slice(start, start + height)
            outs[i].ref[:, j * width : (j + 1) * width] = keep[rows, :].astype(F32) + got[rows, :].astype(F32)
            start += height
        outs[i].done()
    for n, i in enumerate(gained):
        products = weights[n].ready()[...].astype(F32) * outs[i].ref[...]
        ones = jnp.ones((8, products.shape[1]), F32)
        sums = lax.dot_general(
            ones, products, (((1,), (1,)), ((), ())),
            precision=lax.Precision.HIGHEST, preferred_element_type=F32,
        )
        outs[len(heights) + n].ref[...] = sums[:1, :] / gains[n].ready()[...]


def swap_sum(value, axis):
    count = lax.axis_size(axis)
    step = 1
    while step < count:
        value = value + lax.ppermute(value, axis, [(i, i ^ step) for i in range(count)])
        step *= 2
    return value


class Scatter:
    def __init__(self, keep, give, axis, order):
        self.axis, self.count = axis, lax.axis_size(axis)
        bits = self.count.bit_length() - 1
        self.left = list(range(1, bits))
        self.order = [bit for bit in order if bit < bits] + [bit for bit in self.left if bit not in order]
        shape = (2,) * (bits - 1) + keep.shape[1:]
        self.keep, self.got = keep.reshape(shape), self.swap(give, 0).reshape(shape)

    def swap(self, value, bit):
        return lax.ppermute(value, self.axis, [(i, i ^ (1 << bit)) for i in range(self.count)])

    def step(self):
        bit = self.order.pop(0)
        place = self.left.index(bit)
        self.left.remove(bit)

        def half(which):
            first, second = (lax.index_in_dim(a, which, place, keepdims=False) for a in (self.keep, self.got))
            return (first.astype(F32) + second.astype(F32)).astype(BF)

        self.keep, self.got = half(0), self.swap(half(1), bit)

    def step_with(self, keep, give):
        bit = self.order.pop(0)
        place = self.left.index(bit)
        self.left.remove(bit)
        assert place == 0
        shape = (2,) * len(self.left) + keep.shape[1:]
        self.keep, self.got = keep.reshape(shape), self.swap(give, bit).reshape(shape)

    def rest(self):
        while self.order:
            self.step()
        return self.keep, self.got


def after(value, *scatters):
    value, keeps = lax.optimization_barrier((value, [scatter.keep for scatter in scatters]))
    for scatter, keep in zip(scatters, keeps):
        scatter.keep = keep
    return value


def hold(value, *scatters):
    value, gots = lax.optimization_barrier((value, [scatter.got for scatter in scatters]))
    for scatter, got in zip(scatters, gots):
        scatter.got = got
    return value


def per_device(latents, pixels, pixel_mask, group_image, cotangent, gain_cross, gain_pixel, w_query,
               w_keyval, w_cross_out, gain_self, w_qkv, w_self_out, gain_mlp, w_in, w_out):
    groups, keys, width = pixels.shape
    rows = latents.shape[0]
    per = rows // groups
    size = width // HEADS
    wide = w_in.shape[1]
    scale = 1.0 / math.sqrt(size)
    factor = scale * LOG2E
    shards, members = lax.axis_size("pix"), lax.axis_size("grp")
    place = lax.axis_index("pix")
    me = lax.axis_index("grp").reshape(1).astype(jnp.int32)
    block = width // (shards * members)
    wide_block = wide // (shards * members)
    mine = members * block

    y = pixels.reshape(groups * keys, width)
    gx, gy, gs, gm = (g.reshape(1, width) for g in (gain_cross, gain_pixel, gain_self, gain_mlp))
    own_row = lax.broadcasted_iota(jnp.int32, (mine, width), 0)
    column = lax.broadcasted_iota(jnp.int32, (mine, width), 1)
    wanted = ((own_row // block) * shards + place) * block + own_row % block
    sel = (column == wanted).astype(BF)
    own_filled = jnp.sum(pixel_mask, axis=1, dtype=jnp.int32)
    extra = jnp.pad(own_filled.astype(BF), (0, 16 - groups))[:, None]
    turn = [(i, (i + 1) % shards) for i in range(shards)]
    moving = [jnp.concatenate([pixels[0], jnp.broadcast_to(extra, (16, width))], axis=0)]
    moving += [pixels[g] for g in range(1, groups)]
    here = place.reshape(1).astype(jnp.int32)
    stats = ((rows, LANES), F32)
    xn, q, yn, kv, own_cols, out_t, lse, rx, ry = call(
        functools.partial(pre_kernel, factor), [own_filled],
        [latents, gx, w_query, y, gy, w_keyval, sel],
        [((rows, width), BF), ((rows, width), BF), ((groups * keys, width), BF),
         ((groups * keys, 2 * width), BF), ((mine, groups * keys), BF), ((groups, width, per), BF),
         ((groups, HEADS, per), F32), stats, ((groups * keys, LANES), F32)],
        attend_scratch(keys, per), 2 * (rows * width * width + groups * keys * width * 2 * width),
    )

    def slot(s):
        return lambda scalars: lax.rem(scalars[0][0] + (shards - s), shards)

    def key_rows(s):
        return lambda scalars: pl.ds(pl.multiple_of(slot(s)(scalars) * keys, keys), keys)

    def col_place(s, g):
        return lambda scalars: (g, slice(None), key_rows(s)(scalars))

    own = [pl.ds(g * keys, keys) for g in range(groups)]
    kv_pieces = [[(kv, key_rows(0), lambda scalars, g=g: own[g])] for g in range(groups)]
    col_pieces = [
        (own_cols, col_place(0, g), lambda scalars, g=g: (slice(None), own[g])) for g in range(groups)
    ]
    out_pieces = [[(out_t, slot(0), lambda scalars, g=g: g)] for g in range(groups)]
    lse_pieces = [[(lse, slot(0), lambda scalars, g=g: g)] for g in range(groups)]
    filled = own_filled
    ahead = [lse, lse]
    merged = []
    for s in range(1, shards):
        for g in range(groups):
            if s > 1:
                moving[g], ahead[g] = lax.optimization_barrier((moving[g], ahead[g]))
            moving[g] = lax.ppermute(moving[g], "pix", turn)
        filled = filled + moving[0][keys : keys + groups, 0].astype(jnp.int32)
        if s < shards - 1:
            moving[-1], filled = lax.optimization_barrier((moving[-1], filled))
        for g in range(groups):
            if 0 < g and s == shards - 1:
                moving[g], ahead[g - 1] = lax.optimization_barrier((moving[g], ahead[g - 1]))
            ins = [part_of(moving[g], 0, keys), gy, w_keyval, sel, part_of(q, g * per, per),
                   part_of(moving[0], keys, 16)]
            outs = [((keys, 2 * width), BF), ((mine, keys), BF), ((width, per), BF), ((HEADS, per), F32)]
            scratch = [pltpu.VMEM((keys, width), BF), pltpu.VMEM((keys, LANES), F32)]
            scratch += attend_scratch(keys, per)
            flops = 2 * keys * width * 2 * width
            if s < shards - 1:
                kv, own_cols, out_t, lse = call(
                    functools.partial(shard_kernel, factor, g), [], ins, outs, scratch, flops
                )
                out_pieces[g].append((out_t, slot(s), None))
                lse_pieces[g].append((lse, slot(s), None))
            else:
                kv, own_cols, out_t, lse = call(
                    functools.partial(last_shard_kernel, factor, g, shards), [here],
                    ins + [Stack((shards, width, per), BF, out_pieces[g]),
                           Stack((shards, HEADS, per), F32, lse_pieces[g])],
                    outs, scratch, flops,
                )
                merged.append([out_t, lse])
            kv_pieces[g].append((kv, key_rows(s), None))
            col_pieces.append((own_cols, col_place(s, g), None))
            ahead[g] = lse
    for g in range(groups - 1):
        merged[g][1] = ahead[g]

    def by_group(arrays):
        return Stack(
            (groups,) + arrays[0].shape, arrays[0].dtype,
            [(array, lambda scalars, g=g: g, None) for g, array in enumerate(arrays)],
        )

    cross_t = by_group([pair[0] for pair in merged])
    cross_lse = by_group([pair[1] for pair in merged])
    image = group_image.astype(jnp.int32)

    own_hidden = wide // shards if wide_block % LANES == 0 else wide
    hn, qkv, self_t, self_lse, mn, slope, hid, xf, out_low, rself, rmlp, sums, norms = call(
        functools.partial(forward_kernel, factor, wide_block, shards), [here, image],
        [cross_t, latents, w_cross_out, gs, w_qkv, w_self_out, gm, w_in, w_out],
        [((rows, width), BF), ((rows, 3 * width), BF), ((groups, width, per), BF),
         ((groups, HEADS, per), F32), ((rows, width), BF), ((rows, wide), BF),
         ((rows, own_hidden), BF), ((rows, width), F32), ((rows, width), BF),
         stats, stats, ((1, LANES), F32), ((8, LANES), F32)],
        [pltpu.VMEM((rows, width), F32),
         pltpu.VMEM((rows if own_hidden != wide else 16, wide), BF)] + attend_scratch(per, per),
        2 * rows * width * (5 * width + 2 * wide),
    )
    if own_hidden == wide:
        hid = lax.dynamic_index_in_dim(
            hid.reshape(rows, members, shards, wide_block), place, 2, keepdims=False
        ).reshape(rows, members * wide_block)

    sums = swap_sum(sums, "grp")

    depth = wide_block + block * (wide // width)
    keep_mlp, give_mlp, grad_self, r_self, averaged = call(
        functools.partial(mlp_back_kernel, members), [me, image],
        [sums, norms, cotangent, xf, in_pieces(w_out, 4), slope, hid, w_in, sel, mn, rmlp, gm],
        [((members, depth, width), BF, 2), ((rows, width), F32), ((rows, width), BF), ((1, IMAGES), F32)],
        [pltpu.VMEM((rows, width), BF), pltpu.VMEM((rows, wide), BF), pltpu.VMEM((rows, width), F32)],
        2 * rows * width * (2 * wide + 2 * wide // shards),
    )
    scatter_mlp = Scatter(keep_mlp, give_mlp, "grp", [1, 2])

    d_qkv, keep_self, give_self = call(
        functools.partial(self_back_kernel, factor, scale, members), [me],
        [w_self_out, r_self, self_t, self_lse, qkv, hn, sel],
        [((rows, 3 * width), BF), ((members, 4 * block, width), BF, 2)],
        [pltpu.VMEM((width, rows), F32)] + attend_scratch(per, per) * 2 + [pltpu.VMEM((HEADS, size, per), BF)],
        2 * rows * width * 3 * width,
    )
    scatter_self = Scatter(keep_self, give_self, "grp", [2, 1])
    keep_next, give_next, r_cross, d_out_t, delta, grad_cross = call(
        between_kernel, [],
        [d_qkv, w_qkv, hn, rself, gs, grad_self, w_cross_out, cross_t, keep_mlp,
         scatter_mlp.got.reshape(keep_mlp.shape)],
        [(keep_mlp.shape, BF, 2), ((rows, width), BF), ((groups, width, per), BF),
         ((groups, HEADS, per), F32), ((rows, width), F32)],
        [pltpu.VMEM((rows, width), F32), pltpu.VMEM((width, rows), F32)],
        2 * rows * width * 4 * width,
    )
    scatter_mlp.step_with(keep_next, give_next)
    d_out_t = hold(d_out_t, scatter_self)
    scatter_self.step()
    d_out_t = after(d_out_t, scatter_self)

    keep_keyval, give_keyval, keep_cross, give_cross, dq, dkv = call(
        functools.partial(cross_back_kernel, factor, scale, members, groups), [here, me, filled],
        [q, d_out_t, cross_lse, delta]
        + [Stack((shards * keys, 2 * width), BF, pieces) for pieces in kv_pieces]
        + [sel, xn, Stack((groups, mine, shards * keys), BF, col_pieces), cross_t, r_cross],
        [((members, 2 * block, width), BF, 2), ((members, 2 * block, width), BF, 2), ((rows, width), BF),
         ((groups, keys, 2 * width), BF, 0)],
        [pltpu.VMEM((groups, shards * keys, 2 * width), BF)],
        2 * shards * groups * keys * width * (5 * per // 2 + 2 * mine),
    )
    scatter_keyval = Scatter(keep_keyval, give_keyval, "grp", [1, 2])
    scatter_cross = Scatter(keep_cross, give_cross, "grp", [2, 1])
    dq = hold(dq, scatter_mlp, scatter_self)
    scatter_mlp.step()
    scatter_self.step()
    dkv = after(dkv, scatter_mlp, scatter_self)
    (grad_pixels,) = call(
        pixel_back_kernel, [], [dkv.reshape(groups * keys, 2 * width), in_pieces(w_keyval, 4), yn, ry, gy],
        [((groups * keys, width), F32)],
        [pltpu.VMEM((groups * keys, width), F32)],
        2 * groups * keys * width * 2 * width,
    )
    index = lax.axis_index("grp") * shards + place
    index_ref = index.reshape(1).astype(jnp.int32)
    all_gains = jnp.stack([gain_cross, gain_pixel, gain_self, gain_mlp])
    own_gains = lax.dynamic_slice_in_dim(all_gains, index * block, block, 1)

    def finish(scatters, heights, gained):
        ends = [scatter.rest() for scatter in scatters]

        def joined(arrays):
            pieces, start = [], 0
            for array in arrays:
                where = pl.ds(start, array.shape[0])
                pieces.append((array, lambda scalars, where=where: where, None))
                start += array.shape[0]
            return Stack((start, width), BF, pieces)

        wides = [(heights_of[0], width * len(heights_of)) for heights_of in heights]
        return call(
            functools.partial(finish_kernel, heights, list(gained)), [index_ref],
            [joined([keep for keep, _ in ends]), joined([got for _, got in ends])]
            + [part_of(weight, lambda scalars: scalars[0][0] * block, block) for weight, _ in gained.values()]
            + [own_gains[row : row + 1] for _, row in gained.values()],
            [(shape, F32) for shape in wides] + [((1, block), F32)] * len(gained),
            [], 1e6,
        )

    grad_pixels = hold(grad_pixels, scatter_keyval, scatter_cross, scatter_self)
    scatter_keyval.step()
    scatter_cross.step()
    grad_pixels = after(grad_pixels, scatter_keyval, scatter_cross)
    d_w_qkv, d_w_self_out, d_g_self = finish([scatter_self], [[block] * 3, [block]], {0: (w_qkv, 2)})
    dq, d_w_qkv, scatter_mlp.got = lax.optimization_barrier((dq, d_w_qkv, scatter_mlp.got))
    dq, grad_pixels = after((dq, grad_pixels), scatter_keyval, scatter_cross)
    (grad_latents,) = call(
        query_back_kernel, [], [dq, in_pieces(w_query, 2), xn, rx, gx, grad_cross],
        [((rows, width), F32)],
        [pltpu.VMEM((rows, width), F32)],
        2 * rows * width * width,
    )

    grad_latents = hold(grad_latents, scatter_mlp, scatter_keyval, scatter_cross)
    scatter_keyval.step()
    scatter_cross.step()
    d_w_out, d_w_in, d_g_mlp = finish(
        [scatter_mlp], [[wide_block], [block] * (wide // width)], {1: (w_in, 3)}
    )
    d_w_keyval, d_w_query, d_w_cross_out, d_g_pixel, d_g_cross = finish(
        [scatter_keyval, scatter_cross], [[block] * 2, [block], [block]], {0: (w_keyval, 1), 1: (w_query, 0)}
    )
    return (
        out_low,
        grad_latents,
        grad_pixels.reshape(groups, keys, width),
        d_g_cross.reshape(block),
        d_g_pixel.reshape(block),
        d_w_query,
        d_w_keyval,
        d_w_cross_out,
        d_g_self.reshape(block),
        d_w_qkv,
        d_w_self_out,
        d_g_mlp.reshape(block),
        d_w_in,
        d_w_out,
        averaged.reshape(IMAGES),
    )


def solution(mesh):
    both = ("grp", "pix")
    in_specs = (
        P("grp", None), P("grp", "pix", None), P("grp", "pix"), P("grp"), P("grp", None),
    ) + (P(),) * 11
    out_specs = (
        P("grp", None), P("grp", None), P("grp", "pix", None), P(both), P(both),
        P(both, None), P(both, None), P(both, None), P(both), P(both, None), P(both, None),
        P(both), P(both, None), P(both, None), P(),
    )
    return jax.shard_map(
        per_device, mesh=mesh, in_specs=in_specs, out_specs=out_specs, check_vma=False
    )
```

```python
import functools
import math

import jax
import jax.numpy as jnp
from jax import lax
from jax.experimental import pallas as pl
from jax.experimental.pallas import tpu as pltpu
from jax.sharding import PartitionSpec as P

HEADS = 8
IMAGES = 8
NEG_FILL = -1e30
EPSILON = 1e-05
BF = jnp.bfloat16
F32 = jnp.float32
LOG2E = 1.0 / math.log(2.0)
LANES = 128
COUNTS = 64
HBM = pl.BlockSpec(memory_space=pltpu.HBM)
SM = pl.BlockSpec(memory_space=pltpu.SMEM)


def dot(left, right, left_dim, right_dim):
    return lax.dot_general(
        left, right, (((left_dim,), (right_dim,)), ((), ())), preferred_element_type=F32
    )


def tiles(total, most):
    return [(start, min(most, total - start)) for start in range(0, total, most)]


def span(index, size):
    return pl.ds(pl.multiple_of(index * size, size), size)


def loop(count, body):
    lax.fori_loop(0, count, lambda index, carry: (body(index), carry)[1], 0)


class Stack:
    separate = False

    def __init__(self, shape, dtype, pieces):
        self.shape, self.dtype, self.pieces = shape, dtype, pieces


def whole_of(array):
    return Stack(array.shape, array.dtype, [(array, None, None)])


class Near:
    def __init__(self, array, start=0, size=None):
        self.array = pltpu.with_memory_space_constraint(array, pltpu.VMEM)
        self.start, self.size = start, size

    def box(self, ref):
        return Box(ref if self.size is None else ref.at[pl.ds(self.start, self.size)], [])


def in_pieces(array, count):
    size = array.shape[0] // count
    pieces = [
        (array, lambda scalars, j=j: j, lambda scalars, j=j: pl.ds(j * size, size)) for j in range(count)
    ]
    stack = Stack((count, size) + array.shape[1:], array.dtype, pieces)
    stack.separate = True
    return stack


def each_of(array):
    pieces = [(array, lambda scalars, j=j: j, lambda scalars, j=j: j) for j in range(array.shape[0])]
    stack = Stack(array.shape, array.dtype, pieces)
    stack.separate = True
    return stack


def part_of(array, start, size):
    def which(scalars):
        return pl.ds(pl.multiple_of(start(scalars), size) if callable(start) else start, size)

    return Stack((size,) + array.shape[1:], array.dtype, [(array, None, which)])


class Box:
    def __init__(self, ref, copies):
        self.ref, self.copies = ref, copies

    def ready(self):
        for copy in self.copies:
            copy.wait()
        self.copies = []
        return self.ref


class Pieces(Box):
    def __init__(self, ref, copies, sems):
        super().__init__(ref, [])
        self.sources, self.sems = copies, sems

    def wait_piece(self, index):
        pltpu.make_async_copy(self.sources[0], self.ref.at[index], self.sems.at[index]).wait()


class Slot:
    def __init__(self, ref, targets, sems):
        self.ref, self.targets, self.sems, self.copies = ref, targets, sems, []

    def send(self, source):
        each = source.shape[0] // len(self.targets)
        for i, target in enumerate(self.targets):
            part = source if len(self.targets) == 1 else source.at[pl.ds(i * each, each)]
            copy = pltpu.make_async_copy(part, target, self.sems.at[i])
            copy.start()
            self.copies.append(copy)

    def send_rows(self, start, size, part):
        rows = pl.ds(start, size)
        copy = pltpu.make_async_copy(self.ref.at[rows], self.targets[0].at[rows], self.sems.at[part])
        copy.start()
        self.copies.append(copy)

    def send_to(self, pieces):
        for i, (source, index) in enumerate(pieces):
            copy = pltpu.make_async_copy(source, self.targets[0].at[index], self.sems.at[i])
            copy.start()
            self.copies.append(copy)

    def done(self):
        self.send(self.ref)


def call(kernel, scalars, loads, outs, scratch, flops):
    order = [isinstance(item, Near) for item in loads]
    near = [item for item in loads if isinstance(item, Near)]
    loads = [item for item in loads if not isinstance(item, Near)]
    loads = [item if isinstance(item, Stack) else whole_of(item) for item in loads]
    parts = [out[2] if len(out) > 2 else 1 for out in outs]
    targets = []
    for out, count in zip(outs, parts):
        count = max(count, 1)
        shape = (out[0][0] // count,) + tuple(out[0][1:])
        targets += [jax.ShapeDtypeStruct(shape, out[1])] * count
    most = max(max(parts), 2)
    arrays = [piece[0] for item in loads for piece in item.pieces]
    deep = max(len(item.pieces) for item in loads)

    def whole(*refs):
        refs = list(refs)

        def take(count):
            taken = refs[:count]
            del refs[:count]
            return taken

        scalar_refs = take(len(scalars))
        near_boxes = [item.box(ref) for item, ref in zip(near, take(len(near)))]
        load_refs = [take(len(item.pieces)) for item in loads]
        target_refs = take(len(targets))
        load_bufs = take(len(loads))
        out_bufs = [take(1)[0] if count else None for count in parts]
        extra = take(len(scratch))
        load_sems, out_sems = refs
        boxes, first, late = [], [], {}
        for i, (item, sources, buf) in enumerate(zip(loads, load_refs, load_bufs)):
            copies = []
            for j, (source, (_, where, which)) in enumerate(zip(sources, item.pieces)):
                copy = pltpu.make_async_copy(
                    source if which is None else source.at[which(scalar_refs)],
                    buf if where is None else buf.at[where(scalar_refs)],
                    load_sems.at[i, j],
                )
                copies.append(copy)
                if item.separate and j:
                    late.setdefault(j, []).append(copy)
                else:
                    first.append(copy)
            after_item = i + 1 == len(loads) or not (item.separate and loads[i + 1].separate)
            if after_item:
                for copy in first + [copy for j in sorted(late) for copy in late[j]]:
                    copy.start()
                first, late = [], {}
            if item.separate:
                boxes.append(Pieces(buf, [source.at[item.pieces[0][2](scalar_refs)]], load_sems.at[i]))
            else:
                boxes.append(Box(buf, copies))
        slots = []
        for i, (buf, count) in enumerate(zip(out_bufs, parts)):
            count = max(count, 1)
            slots.append(Slot(buf, target_refs[:count], out_sems.at[i]))
            del target_refs[:count]
        far = list(boxes)
        everything = [near_boxes.pop(0) if is_near else far.pop(0) for is_near in order]
        kernel(*scalar_refs, *everything, *slots, *extra)
        for box in boxes:
            box.ready()
        for slot in slots:
            if not slot.copies:
                slot.done()
        for slot in slots:
            for copy in slot.copies:
                copy.wait()

    moved = sum(a.size * a.dtype.itemsize for a in arrays)
    return pl.pallas_call(
        whole,
        out_shape=targets,
        in_specs=[SM] * len(scalars) + [pl.BlockSpec(memory_space=pltpu.VMEM)] * len(near) + [HBM] * len(arrays),
        out_specs=[HBM] * len(targets),
        scratch_shapes=[pltpu.VMEM(item.shape, item.dtype) for item in loads]
        + [pltpu.VMEM(out[0], out[1]) for out, count in zip(outs, parts) if count]
        + list(scratch)
        + [pltpu.SemaphoreType.DMA((len(loads), deep)), pltpu.SemaphoreType.DMA((len(outs), most))],
        compiler_params=pltpu.CompilerParams(vmem_limit_bytes=60 * 2**20),
        cost_estimate=pl.CostEstimate(flops=int(flops), bytes_accessed=int(moved), transcendentals=0),
    )(*scalars, *[item.array for item in near], *arrays)


def norm_rows(src, gain, dst, rstd, step=128):
    rows = src.shape[0]

    def body(i):
        sl = span(i, step)
        values = src[sl, :].astype(F32)
        center = values - jnp.mean(values, axis=-1, keepdims=True)
        spread = jnp.mean(center * center, axis=-1, keepdims=True)
        scale = lax.rsqrt(spread + EPSILON)
        dst[sl, :] = (center * scale * gain[...]).astype(BF)
        rstd[sl, :] = jnp.broadcast_to(scale, (step, LANES))

    loop(rows // step, body)


def norm_back(dy, normed, rstd, gain, base, out, low, step=64):
    rows = dy.shape[0]
    half = rows // 2

    def body(i):
        sl = span(i, step)
        grad = dy[sl, :]
        normal = normed[sl, :].astype(F32)
        gains = gain[...]
        scaled = grad * gains
        mean_scaled = jnp.mean(scaled, axis=-1, keepdims=True)
        mean_norm = jnp.mean(grad * normal, axis=-1, keepdims=True)
        result = rstd[sl, :1] * (scaled - mean_scaled - normal * (1.0 / gains) * mean_norm)
        if base is not None:
            result = result + base[sl, :]
        out.ref[sl, :] = result
        if low is not None:
            low.ref[sl, :] = result.astype(BF)

    for part in range(2):
        loop(half // step, lambda i: body(part * (half // step) + i))
        for slot in (out, low):
            if slot is not None:
                slot.send_rows(part * half, half, part)


def head(h, size, base=0):
    return slice(base + h * size, base + (h + 1) * size)


def attend(heads, limit, factor, scores, weights):
    for i, (q, k, _, _) in enumerate(heads):
        scores[i] = dot(k(), q(), 1, 1)
    totals = []
    for i in range(len(heads)):
        values = scores[i] * factor
        if limit is not None:
            key = lax.broadcasted_iota(jnp.int32, values.shape, 0)
            values = jnp.where(key < limit, values, NEG_FILL)
        most = jnp.max(values, axis=0, keepdims=True)
        values = jnp.exp2(values - most)
        total = jnp.sum(values, axis=0, keepdims=True)
        weights[i] = values.astype(BF)
        totals.append((1.0 / total, most + jnp.log(total) * LOG2E))
    for i, (_, _, v, put) in enumerate(heads):
        inverse, lse = totals[i]
        put(dot(v(), weights[i], 0, 0) * inverse, lse)


def attend_scratch(keys, queries):
    return [pltpu.VMEM((HEADS, keys, queries), F32), pltpu.VMEM((HEADS, keys, queries), BF)]


def scatter_slot(me, target, members):
    different = target ^ me
    slot, left = 0, members
    while left > 1:
        left //= 2
        slot = slot + (different & 1) * left
        different = different >> 1
    return slot


def put_blocks(out, me, members, offset, values):
    each = values.shape[0] // members
    for target in range(members):
        out[scatter_slot(me, target, members), offset : offset + each, :] = values[
            target * each : (target + 1) * each
        ]


def pre_kernel(factor, filled, x, gx, wq, y, gy, wkv, sel,
               xn, q, yn, kv, own_cols, out_t, lse, rx, ry, scores, weights):
    groups, width, latents = out_t.ref.shape
    size = width // HEADS
    keys = y.ref.shape[0] // groups
    norm_rows(x.ready(), gx.ready(), xn.ref, rx.ref)
    xn.done(), rx.done()
    wq = wq.ready()
    for start, length in tiles(width, 1024):
        cols = slice(start, start + length)
        q.ref[:, cols] = dot(xn.ref[...], wq[:, cols], 1, 0).astype(BF)
    q.done()
    norm_rows(y.ready(), gy.ready(), yn.ref, ry.ref)
    yn.done(), ry.done()
    kv_ref, wkv = kv.ref, wkv.ready()

    def project(i):
        kv_ref[:, span(i, 1024)] = dot(yn.ref[...], wkv[:, span(i, 1024)], 1, 0).astype(BF)

    loop(2 * width // 1024, project)
    kv.done()
    own_cols.ref[...] = dot(sel.ready()[...], yn.ref[...], 1, 1).astype(BF)
    own_cols.done()
    for g in range(groups):
        rows, cols = slice(g * latents, (g + 1) * latents), slice(g * keys, (g + 1) * keys)
        heads = []
        for h in range(HEADS):

            def put(result, total, h=h):
                out_t.ref[g, head(h, size), :] = result.astype(BF)
                lse.ref[g, h : h + 1, :] = total

            heads.append((
                lambda h=h: q.ref[rows, head(h, size)], lambda h=h: kv_ref[cols, head(h, size)],
                lambda h=h: kv_ref[cols, head(h, size, width)], put,
            ))
        attend(heads, filled[g], factor, scores, weights)


def shard_kernel(factor, group, y, gy, wkv, sel, q, filled, kv, own_cols, out_t, lse, yn, ry, scores, weights):
    width, latents = out_t.ref.shape
    shard_body(factor, group, y, gy, wkv, sel, q, filled, kv, own_cols, out_t.ref, lse.ref, yn, ry, scores, weights)


def shard_body(factor, group, y, gy, wkv, sel, q, filled, kv, own_cols, out_t, lse, yn, ry, scores, weights):
    width, latents = out_t.shape
    size = width // HEADS
    norm_rows(y.ready(), gy.ready(), yn, ry)
    kv_ref, wkv = kv.ref, wkv.ready()

    def project(i):
        kv_ref[:, span(i, 1024)] = dot(yn[...], wkv[:, span(i, 1024)], 1, 0).astype(BF)

    loop(2 * width // 1024, project)
    kv.done()
    own_cols.ref[...] = dot(sel.ready()[...], yn[...], 1, 1).astype(BF)
    own_cols.done()
    q = q.ready()
    limit = filled.ready()[group : group + 1, :latents].astype(F32).astype(jnp.int32)
    heads = []
    for h in range(HEADS):

        def put(result, total, h=h):
            out_t[head(h, size), :] = result.astype(BF)
            lse[h : h + 1, :] = total

        heads.append((
            lambda h=h: q[:, head(h, size)], lambda h=h: kv_ref[:, head(h, size)],
            lambda h=h: kv_ref[:, head(h, size, width)], put,
        ))
    attend(heads, limit, factor, scores, weights)


def last_shard_kernel(factor, group, shards, place, y, gy, wkv, sel, q, filled, part_t, part_lse,
                      kv, own_cols, out_t, lse, yn, ry, scores, weights):
    width, _ = out_t.ref.shape
    size = width // HEADS
    mine = lax.rem(place[0] + 1, shards)
    shard_body(
        factor, group, y, gy, wkv, sel, q, filled, kv, own_cols,
        part_t.ref.at[mine], part_lse.ref.at[mine], yn, ry, scores, weights,
    )
    part_t, part_lse = part_t.ready(), part_lse.ready()
    most = functools.reduce(jnp.maximum, [part_lse[z] for z in range(shards)])
    shares = [jnp.exp2(part_lse[z] - most) for z in range(shards)]
    total = functools.reduce(jnp.add, shares)
    lse.ref[...] = most + jnp.log(total) * LOG2E
    shares = [share / total for share in shares]
    for h in range(HEADS):
        merged = functools.reduce(jnp.add, [
            shares[z][h : h + 1, :] * part_t[z, head(h, size), :].astype(F32) for z in range(shards)
        ])
        out_t.ref[head(h, size), :] = merged.astype(BF)


def forward_kernel(factor, block, shards, place, image, cross_t, x, wco, gself, wqkv, wso, gmlp, win, wout,
                   hn, qkv, self_t, lse, mn, slope, hid_out, xf, low, rself, rmlp,
                   sums, norms, resid, hidden, scores, weights):
    groups, width, latents = cross_t.ref.shape
    size = width // HEADS
    wide = win.ref.shape[1]
    cross_t, x, wco = cross_t.ready(), x.ready(), wco.ready()
    for g in range(groups):
        rows = slice(g * latents, (g + 1) * latents)
        resid[rows, :] = x[rows, :].astype(F32) + dot(cross_t[g], wco[...], 0, 0)
    norm_rows(resid, gself.ready(), hn.ref, rself.ref)
    hn.done(), rself.done()
    wqkv = wqkv.ready()

    def project(i):
        qkv.ref[:, span(i, 1024)] = dot(hn.ref[...], wqkv[:, span(i, 1024)], 1, 0).astype(BF)

    loop(3 * width // 1024, project)
    qkv.done()
    for g in range(groups):
        rows = slice(g * latents, (g + 1) * latents)
        heads = []
        for h in range(HEADS):

            def put(result, total, h=h):
                self_t.ref[g, head(h, size), :] = result.astype(BF)
                lse.ref[g, h : h + 1, :] = total

            heads.append((
                lambda h=h: qkv.ref[rows, head(h, size)], lambda h=h: qkv.ref[rows, head(h, size, width)],
                lambda h=h: qkv.ref[rows, head(h, size, 2 * width)], put,
            ))
        attend(heads, None, factor, scores, weights)
    self_t.done(), lse.done()
    wso = wso.ready()
    for g in range(groups):
        rows = slice(g * latents, (g + 1) * latents)
        resid[rows, :] += dot(self_t.ref[g], wso[...], 0, 0)
    norm_rows(resid, gmlp.ready(), mn.ref, rmlp.ref)
    mn.done(), rmlp.done()
    win = win.ready()
    if hid_out.ref.shape[1] == wide:
        hidden = hid_out.ref

    def expand(i):
        act = dot(mn.ref[...], win[:, span(i, 1024)], 1, 0).astype(BF)
        root = math.sqrt(2.0 / math.pi)
        square = act * act
        half = BF(0.5) + BF(0.5) * jnp.tanh(act * (BF(root) + BF(root * 0.044715) * square))
        result = act * half
        hidden[:, span(i, 1024)] = result
        bend = BF(2.0 * root) + BF(6.0 * root * 0.044715) * square
        slope.ref[i] = half + result * (BF(1.0) - half) * bend

    loop(wide // 1024, expand)
    slope.done()
    if hid_out.ref.shape[1] != wide:
        for g in range(wide // (block * shards)):
            start = pl.multiple_of(g * block * shards + place[0] * block, block)
            hid_out.ref[:, g * block : (g + 1) * block] = hidden[:, pl.ds(start, block)]
    hid_out.done()
    wout = wout.ready()
    for start, length in tiles(width, 512):
        cols = slice(start, start + length)
        xf.ref[:, cols] = resid[:, cols] + dot(hidden[...], wout[:, cols], 1, 0)
    xf.done()
    per = 64
    lane = lax.broadcasted_iota(jnp.int32, (1, LANES), 1)
    found = jnp.zeros((1, LANES), F32)
    for g in range(groups):

        def body(i, total, g=g):
            sl = pl.ds(pl.multiple_of(g * latents + i * per, per), per)
            values = xf.ref[sl, :]
            low.ref[sl, :] = values.astype(BF)
            return total + jnp.sum((values * values).reshape(per // 8, 8, width), axis=0)

        total = lax.fori_loop(0, latents // per, body, jnp.zeros((8, width), F32))
        total = jnp.sum(jnp.sum(total, axis=1, keepdims=True), axis=0, keepdims=True)
        norm = jnp.sqrt(total / (latents * width) + 1e-06)
        norms.ref[g : g + 1, :] = jnp.broadcast_to(norm, (1, LANES))
        found = found + jnp.where(lane == image[g], norm, 0.0)
        found = found + jnp.where(lane == image[g] + COUNTS, 1.0, 0.0)
    sums.ref[...] = found


def mlp_back_kernel(members, me, image, sums, norms, cot, xf, wout, slope, hid, win, sel, mn, rmlp, gmlp,
                    blocks, gself, r_self, averaged, r_low, d_act, d_mn):
    rows, width = xf.ref.shape
    groups = image.shape[0]
    latents = rows // groups
    count, tile = slope.ref.shape[0], slope.ref.shape[2]
    wide = count * tile
    me = me[0]
    sums, norms = sums.ready()[...], norms.ready()
    lane = lax.broadcasted_iota(jnp.int32, (1, LANES), 1)
    counts = jnp.maximum(pltpu.roll(sums, COUNTS, 1), 1.0)
    means = sums / counts
    averaged.ref[...] = means[:, :IMAGES]
    shares = means / counts
    cot, xf = cot.ready(), xf.ready()
    step = 64
    for g in range(groups):
        share = jnp.sum(jnp.where(lane == image[g], shares, 0.0), axis=1, keepdims=True)
        fac = share / norms[g : g + 1, :1]

        def add(i, g=g, fac=fac):
            sl = pl.ds(pl.multiple_of(g * latents + i * step, step), step)
            grad = cot[sl, :].astype(F32) + fac * xf[sl, :]
            gself.ref[sl, :] = grad
            r_low[sl, :] = grad.astype(BF)

        loop(latents // step, add)

    def hidden_back(i):
        wout.wait_piece(i)
        d_hidden = dot(r_low[...], wout.ref[i], 1, 1)
        slope.wait_piece(i)
        d_act[:, span(i, tile)] = (slope.ref[i].astype(F32) * d_hidden).astype(BF)

    loop(count, hidden_back)
    put_blocks(blocks.ref, me, members, 0, dot(hid.ready()[...], r_low[...], 0, 0).astype(BF))
    below = hid.ref.shape[1] // members
    part = dot(sel.ready()[...], mn.ready()[...], 1, 1).astype(BF)
    each = part.shape[0] // members
    for j in range(wide // width):
        put_blocks(
            blocks.ref, me, members, below + j * each,
            dot(part, d_act[:, j * width : (j + 1) * width], 1, 0).astype(BF),
        )
    blocks.done()
    win = win.ready()
    for start, length in tiles(width, 512):
        d_mn[:, start : start + length] = dot(d_act[...], win[start : start + length, :], 1, 1)
    norm_back(d_mn, mn.ref, rmlp.ready(), gmlp.ready(), gself.ref, gself, r_self)


def self_back_kernel(factor, scale, members, me, wso, r_self, self_t, lse, qkv, hn, sel,
                     d_qkv, blocks, d_t, scores, probs, d_probs, d_scores, low):
    groups, width, latents = self_t.ref.shape
    size = width // HEADS
    me = me[0]
    d_t[...] = dot(wso.ready()[...], r_self.ready()[...], 1, 1)
    self_t, lse, qkv = self_t.ready(), lse.ready(), qkv.ready()
    for g in range(groups):
        rows = slice(g * latents, (g + 1) * latents)
        deltas = []
        for h in range(HEADS):
            d_out = d_t[head(h, size), rows]
            deltas.append(jnp.sum(
                d_out * self_t[g, head(h, size), :].astype(F32), axis=0, keepdims=True
            ))
            low[h] = d_out.astype(BF)
        for h in range(HEADS):
            scores[h] = dot(qkv[rows, head(h, size, width)], qkv[rows, head(h, size)], 1, 1)
            d_probs[h] = dot(qkv[rows, head(h, size, 2 * width)], low[h], 1, 0)
        for h in range(HEADS):
            values = jnp.exp2(scores[h] * factor - lse[g, h : h + 1, :])
            probs[h] = values.astype(BF)
            d_scores[h] = (values * (d_probs[h] - deltas[h])).astype(BF)
        for h in range(HEADS):
            dq = dot(qkv[rows, head(h, size, width)], d_scores[h], 0, 0) * scale
            d_qkv.ref[rows, head(h, size)] = dq.T.astype(BF)
            dk = dot(d_scores[h], qkv[rows, head(h, size)], 1, 0) * scale
            d_qkv.ref[rows, head(h, size, width)] = dk.astype(BF)
            dv = dot(probs[h], low[h], 1, 1)
            d_qkv.ref[rows, head(h, size, 2 * width)] = dv.astype(BF)
    d_qkv.done()
    sel = sel.ready()
    part = dot(sel[...], hn.ready()[...], 1, 1).astype(BF)
    each = part.shape[0] // members
    for j in range(3):
        put_blocks(
            blocks.ref, me, members, j * each,
            dot(part, d_qkv.ref[:, j * width : (j + 1) * width], 1, 0).astype(BF),
        )
    put_blocks(blocks.ref, me, members, 3 * each, weight_part(sel, self_t, r_self.ref))


def weight_part(sel, source_t, low):
    groups, _, latents = source_t.shape
    total = 0.0
    for g in range(groups):
        mine = dot(sel[...], source_t[g], 1, 0).astype(BF)
        total = total + dot(mine, low[g * latents : (g + 1) * latents, :], 1, 0)
    return total.astype(BF)


def between_kernel(d_qkv, wqkv, hn, rself, gain, gself, wco, cross_t, keep, got,
                   total, r_cross, d_out_t, delta, gcross, d_hn, d_t):
    groups, width, latents = cross_t.ref.shape
    size = width // HEADS
    times_pieces(d_hn, d_qkv.ready(), wqkv)
    keep, got = keep.ready(), got.ready()

    def add(i):
        total.ref[i] = keep[i] + got[i]

    loop(keep.shape[0], add)
    total.done()
    norm_back(
        d_hn, hn.ready(), rself.ready(), gain.ready(), gself.ready(), gcross, r_cross
    )
    d_t[...] = dot(wco.ready()[...], r_cross.ref[...], 1, 1)
    cross_t = cross_t.ready()
    for g in range(groups):
        rows = slice(g * latents, (g + 1) * latents)
        for h in range(HEADS):
            d_out = d_t[head(h, size), rows]
            delta.ref[g, h : h + 1, :] = jnp.sum(
                d_out * cross_t[g, head(h, size), :].astype(F32), axis=0, keepdims=True
            )
            d_out_t.ref[g, head(h, size), :] = d_out.astype(BF)


def cross_back_kernel(factor, scale, members, groups, place, me, filled, q, d_out_t, lse, delta, *refs):
    kvs, refs = refs[:groups], refs[groups:]
    sel, xn, own_cols, cross_t, r_cross, blocks, more, dq, dkv_own, dkv = refs
    _, width, latents = d_out_t.ref.shape
    size = width // HEADS
    keys = dkv_own.targets[0].shape[1]
    q, d_out_t, lse, delta = (box.ready() for box in (q, d_out_t, lse, delta))
    for g in range(groups):
        kv = kvs[g].ready()
        rows = slice(g * latents, (g + 1) * latents)

        def one_head(h, g=g, kv=kv, rows=rows):
            cols = span(h, size)
            value_cols = pl.ds(pl.multiple_of(width + h * size, size), size)
            q_h, k_h, d_out = q[rows, cols], kv[:, cols], d_out_t[g, cols, :]
            scores = dot(k_h, q_h, 1, 1) * factor
            key = lax.broadcasted_iota(jnp.int32, scores.shape, 0)
            scores = jnp.where(key < filled[g], scores, NEG_FILL)
            probs = jnp.exp2(scores - lse[g, pl.ds(h, 1), :])
            d_probs = dot(kv[:, value_cols], d_out, 1, 0)
            d_scores = (probs * (d_probs - delta[g, pl.ds(h, 1), :])).astype(BF)
            dkv[g, :, cols] = (dot(d_scores, q_h, 1, 0) * scale).astype(BF)
            dkv[g, :, value_cols] = dot(probs.astype(BF), d_out, 1, 1).astype(BF)
            dq.ref[rows, cols] = (dot(k_h, d_scores, 0, 0) * scale).T.astype(BF)

        def some_heads(i):
            for j in range(4):
                one_head(4 * i + j)

        loop(HEADS // 4, some_heads)
    dq.done()
    own_rows = pl.ds(pl.multiple_of(place[0] * keys, keys), keys)
    dkv_own.send_to([(dkv.at[g, own_rows], g) for g in range(groups)])
    own_cols, sel, xn = own_cols.ready(), sel.ready(), xn.ready()
    each = sel.shape[0] // members
    for j in range(2):
        total = functools.reduce(jnp.add, [
            dot(own_cols[g], dkv[g, :, j * width : (j + 1) * width], 1, 0) for g in range(groups)
        ])
        put_blocks(blocks.ref, me[0], members, j * each, total.astype(BF))
    blocks.done()
    part = dot(sel[...], xn[...], 1, 1).astype(BF)
    put_blocks(more.ref, me[0], members, 0, dot(part, dq.ref[...], 1, 0).astype(BF))
    put_blocks(more.ref, me[0], members, each, weight_part(sel, cross_t.ready(), r_cross.ready()))


def pixel_back_kernel(dkv, wkv, yn, ry, gy, gpix, d_yn):
    times_pieces(d_yn, dkv.ready(), wkv)
    norm_back(d_yn, yn.ready(), ry.ready(), gy.ready(), None, gpix, None)


def query_back_kernel(dq, wq, xn, rx, gx, gcross, glat, d_xn):
    times_pieces(d_xn, dq.ready(), wq)
    norm_back(d_xn, xn.ready(), rx.ready(), gx.ready(), gcross.ready(), glat, None)


def times_pieces(out, left, weight):
    count, size, _ = weight.ref.shape

    def body(i):
        weight.wait_piece(i)
        out[:, span(i, size)] = dot(left[...], weight.ref[i], 1, 1)

    loop(count, body)


def finish_kernel(heights, gained, count, index, keep, *refs):
    gots, refs = [got.ready() for got in refs[:count]], refs[count:]
    keep = keep.ready()
    weights, gains = refs[: len(gained)], refs[len(gained) : 2 * len(gained)]
    outs = refs[2 * len(gained) :]
    width = keep.shape[1]
    start, base = 0, 0
    for i, pieces in enumerate(heights):
        for j, height in enumerate(pieces):
            if start - base >= gots[0].shape[0]:
                base += gots.pop(0).shape[0]
            came = gots[0][start - base : start - base + height, :]
            outs[i].ref[:, j * width : (j + 1) * width] = (
                keep[start : start + height, :].astype(F32) + came.astype(F32)
            )
            start += height
        outs[i].done()
    for n, i in enumerate(gained):
        products = weights[n].ready()[...].astype(F32) * outs[i].ref[...]
        ones = jnp.ones((8, products.shape[1]), F32)
        sums = lax.dot_general(
            ones, products, (((1,), (1,)), ((), ())),
            precision=lax.Precision.HIGHEST, preferred_element_type=F32,
        )
        outs[len(heights) + n].ref[...] = sums[:1, :] / gains[n].ready()[...]


def swap_sum(value, axis):
    count = lax.axis_size(axis)
    step = 1
    while step < count:
        value = value + lax.ppermute(value, axis, [(i, i ^ step) for i in range(count)])
        step *= 2
    return value


class Scatter:
    def __init__(self, keep, give, axis, order):
        self.axis, self.count = axis, lax.axis_size(axis)
        bits = self.count.bit_length() - 1
        self.left = list(range(1, bits))
        self.order = [bit for bit in order if bit < bits] + [bit for bit in self.left if bit not in order]
        shape = (2,) * (bits - 1) + keep.shape[1:]
        self.keep, self.got = keep.reshape(shape), self.swap(give, 0).reshape(shape)

    def swap(self, value, bit):
        return lax.ppermute(value, self.axis, [(i, i ^ (1 << bit)) for i in range(self.count)])

    def step(self):
        bit = self.order.pop(0)
        place = self.left.index(bit)
        self.left.remove(bit)

        def half(which):
            first, second = (lax.index_in_dim(a, which, place, keepdims=False) for a in (self.keep, self.got))
            return (first.astype(F32) + second.astype(F32)).astype(BF)

        self.keep, self.got = half(0), self.swap(half(1), bit)

    def step_with(self, keep, give):
        bit = self.order.pop(0)
        place = self.left.index(bit)
        self.left.remove(bit)
        assert place == 0
        shape = (2,) * len(self.left) + keep.shape[1:]
        self.keep, self.got = keep.reshape(shape), self.swap(give, bit).reshape(shape)

    def rest(self):
        while self.order:
            self.step()
        return self.keep, self.got


def after(value, *scatters):
    value, keeps = lax.optimization_barrier((value, [scatter.keep for scatter in scatters]))
    for scatter, keep in zip(scatters, keeps):
        scatter.keep = keep
    return value


def hold(value, *scatters):
    value, gots = lax.optimization_barrier((value, [scatter.got for scatter in scatters]))
    for scatter, got in zip(scatters, gots):
        scatter.got = got
    return value


def per_device(latents, pixels, pixel_mask, group_image, cotangent, gain_cross, gain_pixel, w_query,
               w_keyval, w_cross_out, gain_self, w_qkv, w_self_out, gain_mlp, w_in, w_out):
    groups, keys, width = pixels.shape
    rows = latents.shape[0]
    per = rows // groups
    size = width // HEADS
    wide = w_in.shape[1]
    scale = 1.0 / math.sqrt(size)
    factor = scale * LOG2E
    shards, members = lax.axis_size("pix"), lax.axis_size("grp")
    place = lax.axis_index("pix")
    me = lax.axis_index("grp").reshape(1).astype(jnp.int32)
    block = width // (shards * members)
    wide_block = wide // (shards * members)
    mine = members * block

    y = pixels.reshape(groups * keys, width)
    gx, gy, gs, gm = (g.reshape(1, width) for g in (gain_cross, gain_pixel, gain_self, gain_mlp))
    own_row = lax.broadcasted_iota(jnp.int32, (mine, width), 0)
    column = lax.broadcasted_iota(jnp.int32, (mine, width), 1)
    wanted = ((own_row // block) * shards + place) * block + own_row % block
    sel = (column == wanted).astype(BF)
    own_filled = jnp.sum(pixel_mask, axis=1, dtype=jnp.int32)
    extra = jnp.pad(own_filled.astype(BF), (0, 16 - groups))[:, None]
    turn = [(i, (i + 1) % shards) for i in range(shards)]
    moving = [jnp.concatenate([pixels[0], jnp.broadcast_to(extra, (16, width))], axis=0)]
    moving += [pixels[g] for g in range(1, groups)]
    here = place.reshape(1).astype(jnp.int32)
    stats = ((rows, LANES), F32)
    xn, q, yn, kv, own_cols, out_t, lse, rx, ry = call(
        functools.partial(pre_kernel, factor), [own_filled],
        [latents, gx, w_query, y, gy, w_keyval, sel],
        [((rows, width), BF), ((rows, width), BF), ((groups * keys, width), BF),
         ((groups * keys, 2 * width), BF), ((mine, groups * keys), BF), ((groups, width, per), BF),
         ((groups, HEADS, per), F32), stats, ((groups * keys, LANES), F32)],
        attend_scratch(keys, per), 2 * (rows * width * width + groups * keys * width * 2 * width),
    )

    def slot(s):
        return lambda scalars: lax.rem(scalars[0][0] + (shards - s), shards)

    def key_rows(s):
        return lambda scalars: pl.ds(pl.multiple_of(slot(s)(scalars) * keys, keys), keys)

    def col_place(s, g):
        return lambda scalars: (g, slice(None), key_rows(s)(scalars))

    own = [pl.ds(g * keys, keys) for g in range(groups)]
    kv_pieces = [[(kv, key_rows(0), lambda scalars, g=g: own[g])] for g in range(groups)]
    col_pieces = [
        (own_cols, col_place(0, g), lambda scalars, g=g: (slice(None), own[g])) for g in range(groups)
    ]
    out_pieces = [[(out_t, slot(0), lambda scalars, g=g: g)] for g in range(groups)]
    lse_pieces = [[(lse, slot(0), lambda scalars, g=g: g)] for g in range(groups)]
    filled = own_filled
    ahead = [lse, lse]
    merged = []
    for s in range(1, shards):
        for g in range(groups):
            if s > 1:
                moving[g], ahead[g] = lax.optimization_barrier((moving[g], ahead[g]))
            moving[g] = lax.ppermute(moving[g], "pix", turn)
        filled = filled + moving[0][keys : keys + groups, 0].astype(jnp.int32)
        if s < shards - 1:
            moving[-1], filled = lax.optimization_barrier((moving[-1], filled))
        for g in range(groups):
            if 0 < g and s == shards - 1:
                moving[g], ahead[g - 1] = lax.optimization_barrier((moving[g], ahead[g - 1]))
            ins = [Near(moving[g], 0, keys), gy, w_keyval, sel, part_of(q, g * per, per),
                   Near(moving[0], keys, 16)]
            outs = [((keys, 2 * width), BF), ((mine, keys), BF), ((width, per), BF), ((HEADS, per), F32)]
            scratch = [pltpu.VMEM((keys, width), BF), pltpu.VMEM((keys, LANES), F32)]
            scratch += attend_scratch(keys, per)
            flops = 2 * keys * width * 2 * width
            if s < shards - 1:
                kv, own_cols, out_t, lse = call(
                    functools.partial(shard_kernel, factor, g), [], ins, outs, scratch, flops
                )
                out_pieces[g].append((out_t, slot(s), None))
                lse_pieces[g].append((lse, slot(s), None))
            else:
                here_now, filled = lax.optimization_barrier((here, filled)) if g else (here, filled)
                kv, own_cols, out_t, lse = call(
                    functools.partial(last_shard_kernel, factor, g, shards), [here_now],
                    ins + [Stack((shards, width, per), BF, out_pieces[g]),
                           Stack((shards, HEADS, per), F32, lse_pieces[g])],
                    outs, scratch, flops,
                )
                merged.append([out_t, lse])
            kv_pieces[g].append((kv, key_rows(s), None))
            col_pieces.append((own_cols, col_place(s, g), None))
            ahead[g] = lse
    for g in range(groups - 1):
        merged[g][1] = ahead[g]

    def by_group(arrays):
        return Stack(
            (groups,) + arrays[0].shape, arrays[0].dtype,
            [(array, lambda scalars, g=g: g, None) for g, array in enumerate(arrays)],
        )

    cross_t = by_group([pair[0] for pair in merged])
    cross_lse = by_group([pair[1] for pair in merged])
    image = group_image.astype(jnp.int32)

    own_hidden = wide // shards if wide_block % LANES == 0 else wide
    hn, qkv, self_t, self_lse, mn, slope, hid, xf, out_low, rself, rmlp, sums, norms = call(
        functools.partial(forward_kernel, factor, wide_block, shards), [here, image],
        [cross_t, latents, w_cross_out, gs, w_qkv, w_self_out, gm, w_in, w_out],
        [((rows, width), BF), ((rows, 3 * width), BF), ((groups, width, per), BF),
         ((groups, HEADS, per), F32), ((rows, width), BF), ((wide // 1024, rows, 1024), BF),
         ((rows, own_hidden), BF), ((rows, width), F32), ((rows, width), BF),
         stats, stats, ((1, LANES), F32), ((8, LANES), F32)],
        [pltpu.VMEM((rows, width), F32),
         pltpu.VMEM((rows if own_hidden != wide else 16, wide), BF)] + attend_scratch(per, per),
        2 * rows * width * (5 * width + 2 * wide),
    )
    if own_hidden == wide:
        hid = lax.dynamic_index_in_dim(
            hid.reshape(rows, members, shards, wide_block), place, 2, keepdims=False
        ).reshape(rows, members * wide_block)

    sums = swap_sum(sums, "grp")

    depth = wide_block + block * (wide // width)
    keep_mlp, give_mlp, grad_self, r_self, averaged = call(
        functools.partial(mlp_back_kernel, members), [me, image],
        [sums, norms, cotangent, xf, in_pieces(w_out, wide // 1024), each_of(slope), hid, w_in, sel, mn, rmlp, gm],
        [((members, depth, width), BF, 2), ((rows, width), F32), ((rows, width), BF), ((1, IMAGES), F32)],
        [pltpu.VMEM((rows, width), BF), pltpu.VMEM((rows, wide), BF), pltpu.VMEM((rows, width), F32)],
        2 * rows * width * (2 * wide + 2 * wide // shards),
    )
    scatter_mlp = Scatter(keep_mlp, give_mlp, "grp", [1, 2])

    d_qkv, keep_self, give_self = call(
        functools.partial(self_back_kernel, factor, scale, members), [me],
        [w_self_out, r_self, self_t, self_lse, qkv, hn, sel],
        [((rows, 3 * width), BF), ((members, 4 * block, width), BF, 2)],
        [pltpu.VMEM((width, rows), F32)] + attend_scratch(per, per) * 2 + [pltpu.VMEM((HEADS, size, per), BF)],
        2 * rows * width * 3 * width,
    )
    scatter_self = Scatter(keep_self, give_self, "grp", [2, 1])
    keep_next, give_next, r_cross, d_out_t, delta, grad_cross = call(
        between_kernel, [],
        [d_qkv, in_pieces(w_qkv, 4), hn, rself, gs, grad_self, w_cross_out, cross_t, keep_mlp,
         Near(scatter_mlp.got.reshape(keep_mlp.shape))],
        [(keep_mlp.shape, BF, 2), ((rows, width), BF), ((groups, width, per), BF),
         ((groups, HEADS, per), F32), ((rows, width), F32)],
        [pltpu.VMEM((rows, width), F32), pltpu.VMEM((width, rows), F32)],
        2 * rows * width * 4 * width,
    )
    scatter_mlp.step_with(keep_next, give_next)
    d_out_t = hold(d_out_t, scatter_self)
    scatter_self.step()
    d_out_t = after(d_out_t, scatter_self)

    keep_keyval, give_keyval, keep_cross, give_cross, dq, dkv = call(
        functools.partial(cross_back_kernel, factor, scale, members, groups), [here, me, filled],
        [q, d_out_t, cross_lse, delta]
        + [Stack((shards * keys, 2 * width), BF, pieces) for pieces in kv_pieces]
        + [sel, xn, Stack((groups, mine, shards * keys), BF, col_pieces), cross_t, r_cross],
        [((members, 2 * block, width), BF, 2), ((members, 2 * block, width), BF, 2), ((rows, width), BF),
         ((groups, keys, 2 * width), BF, 0)],
        [pltpu.VMEM((groups, shards * keys, 2 * width), BF)],
        2 * shards * groups * keys * width * (5 * per // 2 + 2 * mine),
    )
    scatter_keyval = Scatter(keep_keyval, give_keyval, "grp", [1, 2])
    scatter_cross = Scatter(keep_cross, give_cross, "grp", [2, 1])
    dq = hold(dq, scatter_mlp, scatter_self)
    scatter_mlp.step()
    scatter_self.step()
    dkv = after(dkv, scatter_mlp, scatter_self)
    (grad_pixels,) = call(
        pixel_back_kernel, [], [dkv.reshape(groups * keys, 2 * width), in_pieces(w_keyval, 4), yn, ry, gy],
        [((groups * keys, width), F32)],
        [pltpu.VMEM((groups * keys, width), F32)],
        2 * groups * keys * width * 2 * width,
    )
    index = lax.axis_index("grp") * shards + place
    index_ref = index.reshape(1).astype(jnp.int32)
    all_gains = jnp.stack([gain_cross, gain_pixel, gain_self, gain_mlp])
    own_gains = lax.dynamic_slice_in_dim(all_gains, index * block, block, 1)

    def finish(scatters, heights, gained):
        ends = [scatter.rest() for scatter in scatters]

        def joined(arrays):
            pieces, start = [], 0
            for array in arrays:
                where = pl.ds(start, array.shape[0])
                pieces.append((array, lambda scalars, where=where: where, None))
                start += array.shape[0]
            return Stack((start, width), BF, pieces)

        wides = [(heights_of[0], width * len(heights_of)) for heights_of in heights]
        return call(
            functools.partial(finish_kernel, heights, list(gained), len(ends)), [index_ref],
            [joined([keep for keep, _ in ends])] + [Near(got) for _, got in ends]
            + [part_of(weight, lambda scalars: scalars[0][0] * block, block) for weight, _ in gained.values()]
            + [own_gains[row : row + 1] for _, row in gained.values()],
            [(shape, F32) for shape in wides] + [((1, block), F32)] * len(gained),
            [], 1e6,
        )

    grad_pixels = hold(grad_pixels, scatter_keyval, scatter_cross, scatter_self)
    scatter_keyval.step()
    scatter_cross.step()
    grad_pixels = after(grad_pixels, scatter_keyval, scatter_cross)
    d_w_qkv, d_w_self_out, d_g_self = finish([scatter_self], [[block] * 3, [block]], {0: (w_qkv, 2)})
    dq, d_w_qkv, scatter_mlp.got = lax.optimization_barrier((dq, d_w_qkv, scatter_mlp.got))
    dq, grad_pixels = after((dq, grad_pixels), scatter_keyval, scatter_cross)
    (grad_latents,) = call(
        query_back_kernel, [], [dq, in_pieces(w_query, 2), xn, rx, gx, grad_cross],
        [((rows, width), F32)],
        [pltpu.VMEM((rows, width), F32)],
        2 * rows * width * width,
    )

    grad_latents = hold(grad_latents, scatter_mlp, scatter_keyval, scatter_cross)
    scatter_keyval.step()
    scatter_cross.step()
    d_w_out, d_w_in, d_g_mlp = finish(
        [scatter_mlp], [[wide_block], [block] * (wide // width)], {1: (w_in, 3)}
    )
    d_w_keyval, d_w_query, d_w_cross_out, d_g_pixel, d_g_cross = finish(
        [scatter_keyval, scatter_cross], [[block] * 2, [block], [block]], {0: (w_keyval, 1), 1: (w_query, 0)}
    )
    return (
        out_low,
        grad_latents,
        grad_pixels.reshape(groups, keys, width),
        d_g_cross.reshape(block),
        d_g_pixel.reshape(block),
        d_w_query,
        d_w_keyval,
        d_w_cross_out,
        d_g_self.reshape(block),
        d_w_qkv,
        d_w_self_out,
        d_g_mlp.reshape(block),
        d_w_in,
        d_w_out,
        averaged.reshape(IMAGES),
    )


def solution(mesh):
    both = ("grp", "pix")
    in_specs = (
        P("grp", None), P("grp", "pix", None), P("grp", "pix"), P("grp"), P("grp", None),
    ) + (P(),) * 11
    out_specs = (
        P("grp", None), P("grp", None), P("grp", "pix", None), P(both), P(both),
        P(both, None), P(both, None), P(both, None), P(both), P(both, None), P(both, None),
        P(both), P(both, None), P(both, None), P(),
    )
    return jax.shard_map(
        per_device, mesh=mesh, in_specs=in_specs, out_specs=out_specs, check_vma=False
    )
```

```python
import functools
import math

import jax
import jax.numpy as jnp
from jax import lax
from jax.experimental import pallas as pl
from jax.experimental.pallas import tpu as pltpu
from jax.sharding import PartitionSpec as P

HEADS = 8
IMAGES = 8
NEG_FILL = -1e30
EPSILON = 1e-05
BF = jnp.bfloat16
F32 = jnp.float32
LOG2E = 1.0 / math.log(2.0)
LANES = 128
COUNTS = 64
HBM = pl.BlockSpec(memory_space=pltpu.HBM)
SM = pl.BlockSpec(memory_space=pltpu.SMEM)


def dot(left, right, left_dim, right_dim):
    return lax.dot_general(
        left, right, (((left_dim,), (right_dim,)), ((), ())), preferred_element_type=F32
    )


def tiles(total, most):
    return [(start, min(most, total - start)) for start in range(0, total, most)]


def span(index, size):
    return pl.ds(pl.multiple_of(index * size, size), size)


def loop(count, body):
    lax.fori_loop(0, count, lambda index, carry: (body(index), carry)[1], 0)


class Stack:
    separate = False

    def __init__(self, shape, dtype, pieces):
        self.shape, self.dtype, self.pieces = shape, dtype, pieces


def whole_of(array):
    return Stack(array.shape, array.dtype, [(array, None, None)])


class Near:
    def __init__(self, array, start=0, size=None):
        self.array = pltpu.with_memory_space_constraint(array, pltpu.VMEM)
        self.start, self.size = start, size

    def box(self, ref):
        return Box(ref if self.size is None else ref.at[pl.ds(self.start, self.size)], [])


def in_pieces(array, count):
    size = array.shape[0] // count
    pieces = [
        (array, lambda scalars, j=j: j, lambda scalars, j=j: pl.ds(j * size, size)) for j in range(count)
    ]
    stack = Stack((count, size) + array.shape[1:], array.dtype, pieces)
    stack.separate = True
    return stack


def by_columns(array, size=1024):
    count = array.shape[1] // size
    pieces = [
        (array, lambda scalars, j=j: j, lambda scalars, j=j: (slice(None), pl.ds(j * size, size)))
        for j in range(count)
    ]
    stack = Stack((count, array.shape[0], size), array.dtype, pieces)
    stack.separate = True
    return stack


def each_of(array):
    pieces = [(array, lambda scalars, j=j: j, lambda scalars, j=j: j) for j in range(array.shape[0])]
    stack = Stack(array.shape, array.dtype, pieces)
    stack.separate = True
    return stack


def part_of(array, start, size):
    def which(scalars):
        return pl.ds(pl.multiple_of(start(scalars), size) if callable(start) else start, size)

    return Stack((size,) + array.shape[1:], array.dtype, [(array, None, which)])


class Box:
    def __init__(self, ref, copies):
        self.ref, self.copies = ref, copies

    def ready(self):
        for copy in self.copies:
            copy.wait()
        self.copies = []
        return self.ref


class Pieces(Box):
    def __init__(self, ref, copies, sems):
        super().__init__(ref, [])
        self.sources, self.sems = copies, sems

    def wait_piece(self, index):
        pltpu.make_async_copy(self.sources[0], self.ref.at[index], self.sems.at[index]).wait()


class Slot:
    def __init__(self, ref, targets, sems):
        self.ref, self.targets, self.sems, self.copies = ref, targets, sems, []

    def send(self, source):
        each = source.shape[0] // len(self.targets)
        for i, target in enumerate(self.targets):
            part = source if len(self.targets) == 1 else source.at[pl.ds(i * each, each)]
            copy = pltpu.make_async_copy(part, target, self.sems.at[i])
            copy.start()
            self.copies.append(copy)

    def send_rows(self, start, size, part):
        rows = pl.ds(start, size)
        copy = pltpu.make_async_copy(self.ref.at[rows], self.targets[0].at[rows], self.sems.at[part])
        copy.start()
        self.copies.append(copy)

    def send_to(self, pieces):
        for i, (source, index) in enumerate(pieces):
            copy = pltpu.make_async_copy(source, self.targets[0].at[index], self.sems.at[i])
            copy.start()
            self.copies.append(copy)

    def done(self):
        self.send(self.ref)


def call(kernel, scalars, loads, outs, scratch, flops):
    order = [isinstance(item, Near) for item in loads]
    near = [item for item in loads if isinstance(item, Near)]
    loads = [item for item in loads if not isinstance(item, Near)]
    loads = [item if isinstance(item, Stack) else whole_of(item) for item in loads]
    parts = [out[2] if len(out) > 2 else 1 for out in outs]
    targets = []
    for out, count in zip(outs, parts):
        count = max(count, 1)
        shape = (out[0][0] // count,) + tuple(out[0][1:])
        targets += [jax.ShapeDtypeStruct(shape, out[1])] * count
    most = max(max(parts), 2)
    arrays = [piece[0] for item in loads for piece in item.pieces]
    deep = max(len(item.pieces) for item in loads)

    def whole(*refs):
        refs = list(refs)

        def take(count):
            taken = refs[:count]
            del refs[:count]
            return taken

        scalar_refs = take(len(scalars))
        near_boxes = [item.box(ref) for item, ref in zip(near, take(len(near)))]
        load_refs = [take(len(item.pieces)) for item in loads]
        target_refs = take(len(targets))
        load_bufs = take(len(loads))
        out_bufs = [take(1)[0] if count else None for count in parts]
        extra = take(len(scratch))
        load_sems, out_sems = refs
        boxes, first, late = [], [], {}
        for i, (item, sources, buf) in enumerate(zip(loads, load_refs, load_bufs)):
            copies = []
            for j, (source, (_, where, which)) in enumerate(zip(sources, item.pieces)):
                copy = pltpu.make_async_copy(
                    source if which is None else source.at[which(scalar_refs)],
                    buf if where is None else buf.at[where(scalar_refs)],
                    load_sems.at[i, j],
                )
                copies.append(copy)
                if item.separate and j:
                    late.setdefault(j, []).append(copy)
                else:
                    first.append(copy)
            after_item = i + 1 == len(loads) or not (item.separate and loads[i + 1].separate)
            if after_item:
                for copy in first + [copy for j in sorted(late) for copy in late[j]]:
                    copy.start()
                first, late = [], {}
            if item.separate:
                boxes.append(Pieces(buf, [source.at[item.pieces[0][2](scalar_refs)]], load_sems.at[i]))
            else:
                boxes.append(Box(buf, copies))
        slots = []
        for i, (buf, count) in enumerate(zip(out_bufs, parts)):
            count = max(count, 1)
            slots.append(Slot(buf, target_refs[:count], out_sems.at[i]))
            del target_refs[:count]
        far = list(boxes)
        everything = [near_boxes.pop(0) if is_near else far.pop(0) for is_near in order]
        kernel(*scalar_refs, *everything, *slots, *extra)
        for box in boxes:
            box.ready()
        for slot in slots:
            if not slot.copies:
                slot.done()
        for slot in slots:
            for copy in slot.copies:
                copy.wait()

    moved = sum(a.size * a.dtype.itemsize for a in arrays)
    return pl.pallas_call(
        whole,
        out_shape=targets,
        in_specs=[SM] * len(scalars) + [pl.BlockSpec(memory_space=pltpu.VMEM)] * len(near) + [HBM] * len(arrays),
        out_specs=[HBM] * len(targets),
        scratch_shapes=[pltpu.VMEM(item.shape, item.dtype) for item in loads]
        + [pltpu.VMEM(out[0], out[1]) for out, count in zip(outs, parts) if count]
        + list(scratch)
        + [pltpu.SemaphoreType.DMA((len(loads), deep)), pltpu.SemaphoreType.DMA((len(outs), most))],
        compiler_params=pltpu.CompilerParams(vmem_limit_bytes=60 * 2**20),
        cost_estimate=pl.CostEstimate(flops=int(flops), bytes_accessed=int(moved), transcendentals=0),
    )(*scalars, *[item.array for item in near], *arrays)


def norm_rows(src, gain, dst, rstd, step=128):
    rows = src.shape[0]

    def body(i):
        sl = span(i, step)
        values = src[sl, :].astype(F32)
        center = values - jnp.mean(values, axis=-1, keepdims=True)
        spread = jnp.mean(center * center, axis=-1, keepdims=True)
        scale = lax.rsqrt(spread + EPSILON)
        dst[sl, :] = (center * scale * gain[...]).astype(BF)
        rstd[sl, :] = jnp.broadcast_to(scale, (step, LANES))

    loop(rows // step, body)


def norm_back(dy, normed, rstd, gain, base, out, low, step=64):
    rows = dy.shape[0]
    half = rows // 2

    def body(i, part):
        sl = span(i, step)
        grad = dy[sl, :]
        normal = normed[sl, :].astype(F32)
        gains = gain[...]
        scaled = grad * gains
        mean_scaled = jnp.mean(scaled, axis=-1, keepdims=True)
        mean_norm = jnp.mean(grad * normal, axis=-1, keepdims=True)
        result = rstd[sl, :1] * (scaled - mean_scaled - normal * (1.0 / gains) * mean_norm)
        if base is not None:
            result = result + (base(sl, part) if callable(base) else base[sl, :])
        out.ref[sl, :] = result
        if low is not None:
            low.ref[sl, :] = result.astype(BF)

    for part in range(2):
        loop(half // step, lambda i: body(part * (half // step) + i, part))
        for slot in (out, low):
            if slot is not None:
                slot.send_rows(part * half, half, part)


def head(h, size, base=0):
    return slice(base + h * size, base + (h + 1) * size)


def attend(heads, limit, factor, scores, weights):
    for i, (q, k, _, _) in enumerate(heads):
        scores[i] = dot(k(), q(), 1, 1)
    totals = []
    for i in range(len(heads)):
        values = scores[i] * factor
        if limit is not None:
            key = lax.broadcasted_iota(jnp.int32, values.shape, 0)
            values = jnp.where(key < limit, values, NEG_FILL)
        most = jnp.max(values, axis=0, keepdims=True)
        values = jnp.exp2(values - most)
        total = jnp.sum(values, axis=0, keepdims=True)
        weights[i] = values.astype(BF)
        totals.append((1.0 / total, most + jnp.log(total) * LOG2E, most))
    for i, (_, _, v, put) in enumerate(heads):
        inverse, lse, most = totals[i]
        put(dot(v(), weights[i], 0, 0) * inverse, lse, most)


def attend_scratch(keys, queries):
    return [pltpu.VMEM((HEADS, keys, queries), F32), pltpu.VMEM((HEADS, keys, queries), BF)]


def scatter_slot(me, target, members):
    different = target ^ me
    slot, left = 0, members
    while left > 1:
        left //= 2
        slot = slot + (different & 1) * left
        different = different >> 1
    return slot


def put_blocks(out, me, members, offset, values):
    each = values.shape[0] // members
    for target in range(members):
        out[scatter_slot(me, target, members), offset : offset + each, :] = values[
            target * each : (target + 1) * each
        ]


def pre_kernel(factor, filled, x, gx, wq, y, gy, wkv, sel,
               xn, q, yn, kv, own_cols, out_t, lse, rx, ry, kept, tops, xn_part, scores):
    groups, width, latents = out_t.ref.shape
    size = width // HEADS
    keys = y.ref.shape[0] // groups
    norm_rows(x.ready(), gx.ready(), xn.ref, rx.ref)
    xn.done(), rx.done()
    wq = wq.ready()
    for start, length in tiles(width, 1024):
        cols = slice(start, start + length)
        q.ref[:, cols] = dot(xn.ref[...], wq[:, cols], 1, 0).astype(BF)
    q.done()
    norm_rows(y.ready(), gy.ready(), yn.ref, ry.ref)
    yn.done(), ry.done()
    kv_ref, wkv = kv.ref, wkv.ready()

    def project(i):
        kv_ref[:, span(i, 1024)] = dot(yn.ref[...], wkv[:, span(i, 1024)], 1, 0).astype(BF)

    loop(2 * width // 1024, project)
    kv.done()
    own_cols.ref[...] = dot(sel.ready()[...], yn.ref[...], 1, 1).astype(BF)
    own_cols.done()
    xn_part.ref[...] = dot(sel.ref[...], xn.ref[...], 1, 1).astype(BF)
    xn_part.done()
    for g in range(groups):
        rows, cols = slice(g * latents, (g + 1) * latents), slice(g * keys, (g + 1) * keys)
        heads = []
        for h in range(HEADS):

            def put(result, total, most, h=h):
                out_t.ref[g, head(h, size), :] = result.astype(BF)
                lse.ref[g, h : h + 1, :] = total
                tops.ref[g, h : h + 1, :] = most

            heads.append((
                lambda h=h: q.ref[rows, head(h, size)], lambda h=h: kv_ref[cols, head(h, size)],
                lambda h=h: kv_ref[cols, head(h, size, width)], put,
            ))
        attend(heads, filled[g], factor, scores, kept.ref.at[g])


def shard_kernel(factor, group, y, gy, wkv, sel, q, filled, kv, own_cols, out_t, lse, kept, tops, yn, ry, scores):
    width, latents = out_t.ref.shape
    shard_body(factor, group, y, gy, wkv, sel, q, filled, kv, own_cols, out_t.ref, lse.ref, kept, tops, yn, ry, scores)


def shard_body(factor, group, y, gy, wkv, sel, q, filled, kv, own_cols, out_t, lse, kept, tops, yn, ry, scores):
    width, latents = out_t.shape
    size = width // HEADS
    norm_rows(y.ready(), gy.ready(), yn, ry)
    kv_ref = kv.ref

    def project(i):
        wkv.wait_piece(i)
        kv_ref[:, span(i, 1024)] = dot(yn[...], wkv.ref[i], 1, 0).astype(BF)

    loop(2 * width // 1024, project)
    kv.done()
    own_cols.ref[...] = dot(sel.ready()[...], yn[...], 1, 1).astype(BF)
    own_cols.done()
    q = q.ready()
    limit = filled.ready()[group : group + 1, :latents].astype(F32).astype(jnp.int32)
    heads = []
    for h in range(HEADS):

        def put(result, total, most, h=h):
            out_t[head(h, size), :] = result.astype(BF)
            lse[h : h + 1, :] = total
            tops.ref[h : h + 1, :] = most

        heads.append((
            lambda h=h: q[:, head(h, size)], lambda h=h: kv_ref[:, head(h, size)],
            lambda h=h: kv_ref[:, head(h, size, width)], put,
        ))
    attend(heads, limit, factor, scores, kept.ref)
    kept.done(), tops.done()


def last_shard_kernel(factor, group, shards, place, y, gy, wkv, sel, q, filled, part_t, part_lse,
                      kv, own_cols, out_t, lse, kept, tops, yn, ry, scores):
    width, _ = out_t.ref.shape
    size = width // HEADS
    mine = lax.rem(place[0] + 1, shards)
    shard_body(
        factor, group, y, gy, wkv, sel, q, filled, kv, own_cols,
        part_t.ref.at[mine], part_lse.ref.at[mine], kept, tops, yn, ry, scores,
    )
    part_t, part_lse = part_t.ready(), part_lse.ready()
    most = functools.reduce(jnp.maximum, [part_lse[z] for z in range(shards)])
    shares = [jnp.exp2(part_lse[z] - most) for z in range(shards)]
    total = functools.reduce(jnp.add, shares)
    lse.ref[...] = most + jnp.log(total) * LOG2E
    shares = [share / total for share in shares]
    for h in range(HEADS):
        merged = functools.reduce(jnp.add, [
            shares[z][h : h + 1, :] * part_t[z, head(h, size), :].astype(F32) for z in range(shards)
        ])
        out_t.ref[head(h, size), :] = merged.astype(BF)


def forward_kernel(factor, block, shards, place, image, cross_t, x, wco, gself, wqkv, wso, gmlp, win, wout,
                   hn, qkv, self_t, lse, mn, slope, hid_out, xf, low, rself, rmlp,
                   sums, norms, resid, hidden, scores, weights):
    groups, width, latents = cross_t.ref.shape
    size = width // HEADS
    wide = win.ref.shape[1]
    cross_t, x, wco = cross_t.ready(), x.ready(), wco.ready()
    for g in range(groups):
        rows = slice(g * latents, (g + 1) * latents)
        resid[rows, :] = x[rows, :].astype(F32) + dot(cross_t[g], wco[...], 0, 0)
    norm_rows(resid, gself.ready(), hn.ref, rself.ref)
    hn.done(), rself.done()
    wqkv = wqkv.ready()

    def project(i):
        qkv.ref[:, span(i, 1024)] = dot(hn.ref[...], wqkv[:, span(i, 1024)], 1, 0).astype(BF)

    loop(3 * width // 1024, project)
    qkv.done()
    for g in range(groups):
        rows = slice(g * latents, (g + 1) * latents)
        heads = []
        for h in range(HEADS):

            def put(result, total, most, h=h):
                self_t.ref[g, head(h, size), :] = result.astype(BF)
                lse.ref[g, h : h + 1, :] = total

            heads.append((
                lambda h=h: qkv.ref[rows, head(h, size)], lambda h=h: qkv.ref[rows, head(h, size, width)],
                lambda h=h: qkv.ref[rows, head(h, size, 2 * width)], put,
            ))
        attend(heads, None, factor, scores, weights)
    self_t.done(), lse.done()
    wso = wso.ready()
    for g in range(groups):
        rows = slice(g * latents, (g + 1) * latents)
        resid[rows, :] += dot(self_t.ref[g], wso[...], 0, 0)
    norm_rows(resid, gmlp.ready(), mn.ref, rmlp.ref)
    mn.done(), rmlp.done()
    win = win.ready()
    if hid_out.ref.shape[1] == wide:
        hidden = hid_out.ref

    def expand(i):
        act = dot(mn.ref[...], win[:, span(i, 1024)], 1, 0).astype(BF)
        root = math.sqrt(2.0 / math.pi)
        square = act * act
        half = BF(0.5) + BF(0.5) * jnp.tanh(act * (BF(root) + BF(root * 0.044715) * square))
        result = act * half
        hidden[:, span(i, 1024)] = result
        bend = BF(2.0 * root) + BF(6.0 * root * 0.044715) * square
        slope.ref[i] = half + result * (BF(1.0) - half) * bend

    loop(wide // 1024, expand)
    slope.done()
    if hid_out.ref.shape[1] != wide:
        for g in range(wide // (block * shards)):
            start = pl.multiple_of(g * block * shards + place[0] * block, block)
            hid_out.ref[:, g * block : (g + 1) * block] = hidden[:, pl.ds(start, block)]
    hid_out.done()
    wout = wout.ready()
    squares = [0.0] * groups
    for start, length in tiles(width, 512):
        cols = slice(start, start + length)
        values = resid[:, cols] + dot(hidden[...], wout[:, cols], 1, 0)
        xf.ref[:, cols] = values
        low.ref[:, cols] = values.astype(BF)
        for g in range(groups):
            own = values[g * latents : (g + 1) * latents]
            squares[g] = squares[g] + jnp.sum((own * own).reshape(latents // 8, 8, length), axis=0)
    xf.done(), low.done()
    lane = lax.broadcasted_iota(jnp.int32, (1, LANES), 1)
    found = jnp.zeros((1, LANES), F32)
    for g in range(groups):
        total = squares[g]
        total = jnp.sum(jnp.sum(total, axis=1, keepdims=True), axis=0, keepdims=True)
        norm = jnp.sqrt(total / (latents * width) + 1e-06)
        norms.ref[g : g + 1, :] = jnp.broadcast_to(norm, (1, LANES))
        found = found + jnp.where(lane == image[g], norm, 0.0)
        found = found + jnp.where(lane == image[g] + COUNTS, 1.0, 0.0)
    sums.ref[...] = found


def mlp_back_kernel(members, me, image, sums, norms, cot, xf, wout, slope, hid, win, sel, mn, rmlp, gmlp,
                    blocks, gself, r_self, averaged, r_low, d_act, d_mn):
    rows, width = xf.ref.shape
    groups = image.shape[0]
    latents = rows // groups
    count, tile = slope.ref.shape[0], slope.ref.shape[2]
    wide = count * tile
    me = me[0]
    sums, norms = sums.ready()[...], norms.ready()
    lane = lax.broadcasted_iota(jnp.int32, (1, LANES), 1)
    counts = jnp.maximum(pltpu.roll(sums, COUNTS, 1), 1.0)
    means = sums / counts
    averaged.ref[...] = means[:, :IMAGES]
    shares = means / counts
    cot, xf = cot.ready(), xf.ready()
    factors = []
    step = 64
    for g in range(groups):
        share = jnp.sum(jnp.where(lane == image[g], shares, 0.0), axis=1, keepdims=True)
        fac = share / norms[g : g + 1, :1]
        factors.append(fac)

        def add(i, g=g, fac=fac):
            sl = pl.ds(pl.multiple_of(g * latents + i * step, step), step)
            grad = cot[sl, :].astype(F32) + fac * xf[sl, :]
            r_low[sl, :] = grad.astype(BF)

        loop(latents // step, add)

    def hidden_back(i):
        wout.wait_piece(i)
        d_hidden = dot(r_low[...], wout.ref[i], 1, 1)
        slope.wait_piece(i)
        d_act[:, span(i, tile)] = slope.ref[i] * d_hidden.astype(BF)

    loop(count, hidden_back)
    put_blocks(blocks.ref, me, members, 0, dot(hid.ready()[...], r_low[...], 0, 0).astype(BF))
    below = hid.ref.shape[1] // members
    part = dot(sel.ready()[...], mn.ready()[...], 1, 1).astype(BF)
    each = part.shape[0] // members
    for j in range(wide // width):
        put_blocks(
            blocks.ref, me, members, below + j * each,
            dot(part, d_act[:, j * width : (j + 1) * width], 1, 0).astype(BF),
        )
    blocks.done()
    win = win.ready()
    for start, length in tiles(width, 512):
        d_mn[:, start : start + length] = dot(d_act[...], win[start : start + length, :], 1, 1)

    def grad_final(sl, part):
        return cot[sl, :].astype(F32) + factors[part * groups // 2] * xf[sl, :]

    norm_back(d_mn, mn.ref, rmlp.ready(), gmlp.ready(), grad_final, gself, r_self)


def self_back_kernel(factor, scale, members, me, wso, r_self, self_t, lse, qkv, hn, sel,
                     d_qkv, blocks, d_t, scores, probs, d_probs, d_scores, low):
    groups, width, latents = self_t.ref.shape
    size = width // HEADS
    me = me[0]
    d_t[...] = dot(wso.ready()[...], r_self.ready()[...], 1, 1)
    self_t, lse, qkv = self_t.ready(), lse.ready(), qkv.ready()
    for g in range(groups):
        rows = slice(g * latents, (g + 1) * latents)
        deltas = []
        for h in range(HEADS):
            d_out = d_t[head(h, size), rows]
            deltas.append(jnp.sum(
                d_out * self_t[g, head(h, size), :].astype(F32), axis=0, keepdims=True
            ))
            low[h] = d_out.astype(BF)
        for h in range(HEADS):
            scores[h] = dot(qkv[rows, head(h, size, width)], qkv[rows, head(h, size)], 1, 1)
            d_probs[h] = dot(qkv[rows, head(h, size, 2 * width)], low[h], 1, 0)
        for h in range(HEADS):
            values = jnp.exp2(scores[h] * factor - lse[g, h : h + 1, :])
            probs[h] = values.astype(BF)
            d_scores[h] = (values * (d_probs[h] - deltas[h])).astype(BF)
        for h in range(HEADS):
            dq = dot(qkv[rows, head(h, size, width)], d_scores[h], 0, 0) * scale
            d_qkv.ref[rows, head(h, size)] = dq.T.astype(BF)
            dk = dot(d_scores[h], qkv[rows, head(h, size)], 1, 0) * scale
            d_qkv.ref[rows, head(h, size, width)] = dk.astype(BF)
            dv = dot(probs[h], low[h], 1, 1)
            d_qkv.ref[rows, head(h, size, 2 * width)] = dv.astype(BF)
    d_qkv.done()
    sel = sel.ready()
    part = dot(sel[...], hn.ready()[...], 1, 1).astype(BF)
    each = part.shape[0] // members
    for j in range(3):
        put_blocks(
            blocks.ref, me, members, j * each,
            dot(part, d_qkv.ref[:, j * width : (j + 1) * width], 1, 0).astype(BF),
        )
    put_blocks(blocks.ref, me, members, 3 * each, weight_part(sel, self_t, r_self.ref))


def weight_part(sel, source_t, low):
    groups, _, latents = source_t.shape
    total = 0.0
    for g in range(groups):
        mine = dot(sel[...], source_t[g], 1, 0).astype(BF)
        total = total + dot(mine, low[g * latents : (g + 1) * latents, :], 1, 0)
    return total.astype(BF)


def between_kernel(d_qkv, wqkv, hn, rself, gain, gself, wco, cross_t, keep, got,
                   total, r_cross, d_out_t, delta, gcross, d_hn, d_t):
    groups, width, latents = cross_t.ref.shape
    size = width // HEADS
    times_pieces(d_hn, d_qkv.ready(), wqkv)
    keep, got = keep.ready(), got.ready()

    def add(i):
        total.ref[i] = keep[i] + got[i]

    loop(keep.shape[0], add)
    total.done()
    norm_back(
        d_hn, hn.ready(), rself.ready(), gain.ready(), gself.ready(), gcross, r_cross
    )
    d_t[...] = dot(wco.ready()[...], r_cross.ref[...], 1, 1)
    cross_t = cross_t.ready()
    for g in range(groups):
        rows = slice(g * latents, (g + 1) * latents)
        for h in range(HEADS):
            d_out = d_t[head(h, size), rows]
            delta.ref[g, h : h + 1, :] = jnp.sum(
                d_out * cross_t[g, head(h, size), :].astype(F32), axis=0, keepdims=True
            )
            d_out_t.ref[g, head(h, size), :] = d_out.astype(BF)


def cross_back_kernel(scale, members, groups, shards, place, me, q, d_out_t, lse, delta, tops, *refs):
    kvs, kepts, refs = refs[: 4 * groups : 2], refs[1 : 4 * groups : 2], refs[4 * groups :]
    sel, xn_part, own_cols, cross_t, r_cross, blocks, more, dq, dkv_own, dkv, probs, d_scores = refs
    _, width, latents = d_out_t.ref.shape
    size = width // HEADS
    keys = dkv_own.targets[0].shape[1]
    q, d_out_t, lse, delta, tops = (box.ready() for box in (q, d_out_t, lse, delta, tops))
    for g in range(groups):
        rows = slice(g * latents, (g + 1) * latents)
        for part in range(2):
            kv, kept = kvs[2 * g + part].ready(), kepts[2 * g + part].ready()
            for j in range(HEADS // 2):
                h = part * (HEADS // 2) + j
                cols, value_cols = head(h, size), head(h, size, width)
                q_h, k_h, d_out = q[rows, cols], kv[:, head(j, size)], d_out_t[g, cols, :]
                d_probs = dot(kv[:, head(j, size, width // 2)], d_out, 1, 0)
                for z in range(shards):
                    own = slice(z * keys, (z + 1) * keys)
                    share = jnp.exp2(tops[g, z, h : h + 1, :] - lse[g, h : h + 1, :])
                    values = kept[j, own, :].astype(F32) * share
                    probs[j, own, :] = values.astype(BF)
                    d_scores[j, own, :] = (values * (d_probs[own, :] - delta[g, h : h + 1, :])).astype(BF)
                dkv[g, :, cols] = (dot(d_scores[j], q_h, 1, 0) * scale).astype(BF)
                dkv[g, :, value_cols] = dot(probs[j], d_out, 1, 1).astype(BF)
                dq.ref[rows, cols] = (dot(k_h, d_scores[j], 0, 0) * scale).T.astype(BF)
    dq.done()
    own_rows = pl.ds(pl.multiple_of(place[0] * keys, keys), keys)
    dkv_own.send_to([(dkv.at[g, own_rows], g) for g in range(groups)])
    own_cols, sel = own_cols.ready(), sel.ready()
    each = sel.shape[0] // members
    for j in range(2):
        total = functools.reduce(jnp.add, [
            dot(own_cols[g], dkv[g, :, j * width : (j + 1) * width], 1, 0) for g in range(groups)
        ])
        put_blocks(blocks.ref, me[0], members, j * each, total.astype(BF))
    blocks.done()
    put_blocks(more.ref, me[0], members, 0, dot(xn_part.ready()[...], dq.ref[...], 1, 0).astype(BF))
    put_blocks(more.ref, me[0], members, each, weight_part(sel, cross_t.ready(), r_cross.ready()))


def pixel_back_kernel(dkv, wkv, yn, ry, gy, gpix, d_yn):
    times_pieces(d_yn, dkv.ready(), wkv)
    norm_back(d_yn, yn.ready(), ry.ready(), gy.ready(), None, gpix, None)


def query_back_kernel(dq, wq, xn, rx, gx, gcross, glat, d_xn):
    times_pieces(d_xn, dq.ready(), wq)
    norm_back(d_xn, xn.ready(), rx.ready(), gx.ready(), gcross.ready(), glat, None)


def times_pieces(out, left, weight):
    count, size, _ = weight.ref.shape

    def body(i):
        weight.wait_piece(i)
        out[:, span(i, size)] = dot(left[...], weight.ref[i], 1, 1)

    loop(count, body)


def finish_kernel(heights, gained, count, index, keep, *refs):
    gots, refs = [got.ready() for got in refs[:count]], refs[count:]
    keep = keep.ready()
    weights, gains = refs[: len(gained)], refs[len(gained) : 2 * len(gained)]
    outs = refs[2 * len(gained) :]
    width = keep.shape[1]
    start, base = 0, 0
    for i, pieces in enumerate(heights):
        for j, height in enumerate(pieces):
            if start - base >= gots[0].shape[0]:
                base += gots.pop(0).shape[0]
            came = gots[0][start - base : start - base + height, :]
            outs[i].ref[:, j * width : (j + 1) * width] = (
                keep[start : start + height, :].astype(F32) + came.astype(F32)
            )
            start += height
        outs[i].done()
    for n, i in enumerate(gained):
        products = weights[n].ready()[...].astype(F32) * outs[i].ref[...]
        ones = jnp.ones((8, products.shape[1]), F32)
        sums = lax.dot_general(
            ones, products, (((1,), (1,)), ((), ())),
            precision=lax.Precision.HIGHEST, preferred_element_type=F32,
        )
        outs[len(heights) + n].ref[...] = sums[:1, :] / gains[n].ready()[...]


def swap_sum(value, axis):
    count = lax.axis_size(axis)
    step = 1
    while step < count:
        value = value + lax.ppermute(value, axis, [(i, i ^ step) for i in range(count)])
        step *= 2
    return value


class Scatter:
    def __init__(self, keep, give, axis, order):
        self.axis, self.count = axis, lax.axis_size(axis)
        bits = self.count.bit_length() - 1
        self.left = list(range(1, bits))
        self.order = [bit for bit in order if bit < bits] + [bit for bit in self.left if bit not in order]
        shape = (2,) * (bits - 1) + keep.shape[1:]
        self.keep, self.got = keep.reshape(shape), self.swap(give, 0).reshape(shape)

    def swap(self, value, bit):
        return lax.ppermute(value, self.axis, [(i, i ^ (1 << bit)) for i in range(self.count)])

    def step(self):
        bit = self.order.pop(0)
        place = self.left.index(bit)
        self.left.remove(bit)

        def half(which):
            first, second = (lax.index_in_dim(a, which, place, keepdims=False) for a in (self.keep, self.got))
            return (first.astype(F32) + second.astype(F32)).astype(BF)

        self.keep, self.got = half(0), self.swap(half(1), bit)

    def step_with(self, keep, give):
        bit = self.order.pop(0)
        place = self.left.index(bit)
        self.left.remove(bit)
        assert place == 0
        shape = (2,) * len(self.left) + keep.shape[1:]
        self.keep, self.got = keep.reshape(shape), self.swap(give, bit).reshape(shape)

    def rest(self):
        while self.order:
            self.step()
        return self.keep, self.got


def after(value, *scatters):
    value, keeps = lax.optimization_barrier((value, [scatter.keep for scatter in scatters]))
    for scatter, keep in zip(scatters, keeps):
        scatter.keep = keep
    return value


def hold(value, *scatters):
    value, gots = lax.optimization_barrier((value, [scatter.got for scatter in scatters]))
    for scatter, got in zip(scatters, gots):
        scatter.got = got
    return value


def per_device(latents, pixels, pixel_mask, group_image, cotangent, gain_cross, gain_pixel, w_query,
               w_keyval, w_cross_out, gain_self, w_qkv, w_self_out, gain_mlp, w_in, w_out):
    groups, keys, width = pixels.shape
    rows = latents.shape[0]
    per = rows // groups
    size = width // HEADS
    wide = w_in.shape[1]
    scale = 1.0 / math.sqrt(size)
    factor = scale * LOG2E
    shards, members = lax.axis_size("pix"), lax.axis_size("grp")
    place = lax.axis_index("pix")
    me = lax.axis_index("grp").reshape(1).astype(jnp.int32)
    block = width // (shards * members)
    wide_block = wide // (shards * members)
    mine = members * block

    y = pixels.reshape(groups * keys, width)
    gx, gy, gs, gm = (g.reshape(1, width) for g in (gain_cross, gain_pixel, gain_self, gain_mlp))
    own_row = lax.broadcasted_iota(jnp.int32, (mine, width), 0)
    column = lax.broadcasted_iota(jnp.int32, (mine, width), 1)
    wanted = ((own_row // block) * shards + place) * block + own_row % block
    sel = (column == wanted).astype(BF)
    own_filled = jnp.sum(pixel_mask, axis=1, dtype=jnp.int32)
    extra = jnp.pad(own_filled.astype(BF), (0, 16 - groups))[:, None]
    turn = [(i, (i + 1) % shards) for i in range(shards)]
    moving = [jnp.concatenate([pixels[0], jnp.broadcast_to(extra, (16, width))], axis=0)]
    moving += [pixels[g] for g in range(1, groups)]
    here = place.reshape(1).astype(jnp.int32)
    stats = ((rows, LANES), F32)
    xn, q, yn, kv, own_cols, out_t, lse, rx, ry, kept, tops, xn_part = call(
        functools.partial(pre_kernel, factor), [own_filled],
        [latents, gx, w_query, y, gy, w_keyval, sel],
        [((rows, width), BF), ((rows, width), BF), ((groups * keys, width), BF),
         ((groups * keys, 2 * width), BF), ((mine, groups * keys), BF), ((groups, width, per), BF),
         ((groups, HEADS, per), F32), stats, ((groups * keys, LANES), F32),
         ((groups, HEADS, keys, per), BF), ((groups, HEADS, per), F32), ((mine, rows), BF)],
        attend_scratch(keys, per)[:1], 2 * (rows * width * width + groups * keys * width * 2 * width),
    )

    def slot(s):
        return lambda scalars: lax.rem(scalars[0][0] + (shards - s), shards)

    def key_rows(s):
        return lambda scalars: pl.ds(pl.multiple_of(slot(s)(scalars) * keys, keys), keys)

    def col_place(s, g):
        return lambda scalars: (g, slice(None), key_rows(s)(scalars))

    own = [pl.ds(g * keys, keys) for g in range(groups)]
    half_width = width // 2
    both = [(base, part) for part in range(2) for base in range(2)]

    def kv_half(pieces, array, s, rows_of):
        for base, part in both:
            pieces[part].append((
                array,
                lambda scalars, base=base: (key_rows(s)(scalars), pl.ds(base * half_width, half_width)),
                lambda scalars, base=base, part=part: (
                    rows_of, pl.ds(base * width + part * half_width, half_width)
                ),
            ))

    kv_pieces = [[[], []] for _ in range(groups)]
    for g in range(groups):
        kv_half(kv_pieces[g], kv, 0, own[g])
    col_pieces = [
        (own_cols, col_place(0, g), lambda scalars, g=g: (slice(None), own[g])) for g in range(groups)
    ]
    out_pieces = [[(out_t, slot(0), lambda scalars, g=g: g)] for g in range(groups)]
    lse_pieces = [[(lse, slot(0), lambda scalars, g=g: g)] for g in range(groups)]
    halves = [pl.ds(part * (HEADS // 2), HEADS // 2) for part in range(2)]

    def kept_place(s):
        return lambda scalars: (slice(None), key_rows(s)(scalars))

    def top_place(s, g):
        return lambda scalars: (g, slot(s)(scalars))

    kept_pieces = [
        [[(kept, kept_place(0), lambda scalars, g=g, half=half: (g, half))] for half in halves]
        for g in range(groups)
    ]
    top_pieces = [(tops, top_place(0, g), lambda scalars, g=g: g) for g in range(groups)]
    ahead = [lse, lse]
    merged = []
    for s in range(1, shards):
        for g in range(groups):
            if s > 1:
                moving[g], ahead[g] = lax.optimization_barrier((moving[g], ahead[g]))
            moving[g] = lax.ppermute(moving[g], "pix", turn)
        for g in range(groups):
            if 0 < g and s == shards - 1:
                moving[g], ahead[g - 1] = lax.optimization_barrier((moving[g], ahead[g - 1]))
            ins = [Near(moving[g], 0, keys), gy, by_columns(w_keyval), sel, part_of(q, g * per, per),
                   Near(moving[0], keys, 16)]
            outs = [((keys, 2 * width), BF), ((mine, keys), BF), ((width, per), BF), ((HEADS, per), F32),
                    ((HEADS, keys, per), BF), ((HEADS, per), F32)]
            scratch = [pltpu.VMEM((keys, width), BF), pltpu.VMEM((keys, LANES), F32)]
            scratch += attend_scratch(keys, per)[:1]
            flops = 2 * keys * width * 2 * width
            if s < shards - 1:
                kv, own_cols, out_t, lse, kept, tops = call(
                    functools.partial(shard_kernel, factor, g), [], ins, outs, scratch, flops
                )
                out_pieces[g].append((out_t, slot(s), None))
                lse_pieces[g].append((lse, slot(s), None))
            else:
                kv, own_cols, out_t, lse, kept, tops = call(
                    functools.partial(last_shard_kernel, factor, g, shards), [here],
                    ins + [Stack((shards, width, per), BF, out_pieces[g]),
                           Stack((shards, HEADS, per), F32, lse_pieces[g])],
                    outs, scratch, flops,
                )
                merged.append([out_t, lse])
            kv_half(kv_pieces[g], kv, s, slice(None))
            col_pieces.append((own_cols, col_place(s, g), None))
            for half, pieces in zip(halves, kept_pieces[g]):
                pieces.append((kept, kept_place(s), lambda scalars, half=half: half))
            top_pieces.append((tops, top_place(s, g), None))
            ahead[g] = lse
    for g in range(groups - 1):
        merged[g][1] = ahead[g]

    def by_group(arrays):
        return Stack(
            (groups,) + arrays[0].shape, arrays[0].dtype,
            [(array, lambda scalars, g=g: g, None) for g, array in enumerate(arrays)],
        )

    cross_t = by_group([pair[0] for pair in merged])
    cross_lse = by_group([pair[1] for pair in merged])
    image = group_image.astype(jnp.int32)

    own_hidden = wide // shards if wide_block % LANES == 0 else wide
    hn, qkv, self_t, self_lse, mn, slope, hid, xf, out_low, rself, rmlp, sums, norms = call(
        functools.partial(forward_kernel, factor, wide_block, shards), [here, image],
        [cross_t, latents, w_cross_out, gs, w_qkv, w_self_out, gm, w_in, w_out],
        [((rows, width), BF), ((rows, 3 * width), BF), ((groups, width, per), BF),
         ((groups, HEADS, per), F32), ((rows, width), BF), ((wide // 1024, rows, 1024), BF),
         ((rows, own_hidden), BF), ((rows, width), F32), ((rows, width), BF),
         stats, stats, ((1, LANES), F32), ((8, LANES), F32)],
        [pltpu.VMEM((rows, width), F32),
         pltpu.VMEM((rows if own_hidden != wide else 16, wide), BF)] + attend_scratch(per, per),
        2 * rows * width * (5 * width + 2 * wide),
    )
    if own_hidden == wide:
        hid = lax.dynamic_index_in_dim(
            hid.reshape(rows, members, shards, wide_block), place, 2, keepdims=False
        ).reshape(rows, members * wide_block)

    sums = swap_sum(sums, "grp")

    depth = wide_block + block * (wide // width)
    keep_mlp, give_mlp, grad_self, r_self, averaged = call(
        functools.partial(mlp_back_kernel, members), [me, image],
        [sums, norms, cotangent, xf, in_pieces(w_out, wide // 1024), each_of(slope), hid, w_in, sel, mn, rmlp, gm],
        [((members, depth, width), BF, 2), ((rows, width), F32), ((rows, width), BF), ((1, IMAGES), F32)],
        [pltpu.VMEM((rows, width), BF), pltpu.VMEM((rows, wide), BF), pltpu.VMEM((rows, width), F32)],
        2 * rows * width * (2 * wide + 2 * wide // shards),
    )
    scatter_mlp = Scatter(keep_mlp, give_mlp, "grp", [1, 2])

    d_qkv, keep_self, give_self = call(
        functools.partial(self_back_kernel, factor, scale, members), [me],
        [w_self_out, r_self, self_t, self_lse, qkv, hn, sel],
        [((rows, 3 * width), BF), ((members, 4 * block, width), BF, 2)],
        [pltpu.VMEM((width, rows), F32)] + attend_scratch(per, per) * 2 + [pltpu.VMEM((HEADS, size, per), BF)],
        2 * rows * width * 3 * width,
    )
    scatter_self = Scatter(keep_self, give_self, "grp", [2, 1])
    keep_next, give_next, r_cross, d_out_t, delta, grad_cross = call(
        between_kernel, [],
        [d_qkv, in_pieces(w_qkv, 4), hn, rself, gs, grad_self, w_cross_out, cross_t, keep_mlp,
         Near(scatter_mlp.got.reshape(keep_mlp.shape))],
        [(keep_mlp.shape, BF, 2), ((rows, width), BF), ((groups, width, per), BF),
         ((groups, HEADS, per), F32), ((rows, width), F32)],
        [pltpu.VMEM((rows, width), F32), pltpu.VMEM((width, rows), F32)],
        2 * rows * width * 4 * width,
    )
    scatter_mlp.step_with(keep_next, give_next)
    d_out_t = hold(d_out_t, scatter_self)
    scatter_self.step()
    d_out_t = after(d_out_t, scatter_self)

    group_loads = []
    for g in range(groups):
        for part in range(2):
            group_loads.append(Stack((shards * keys, width), BF, kv_pieces[g][part]))
            group_loads.append(Stack((HEADS // 2, shards * keys, per), BF, kept_pieces[g][part]))
    keep_keyval, give_keyval, keep_cross, give_cross, dq, dkv = call(
        functools.partial(cross_back_kernel, scale, members, groups, shards), [here, me],
        [q, d_out_t, cross_lse, delta, Stack((groups, shards, HEADS, per), F32, top_pieces)]
        + group_loads
        + [sel, xn_part, Stack((groups, mine, shards * keys), BF, col_pieces), cross_t, r_cross],
        [((members, 2 * block, width), BF, 2), ((members, 2 * block, width), BF, 2), ((rows, width), BF),
         ((groups, keys, 2 * width), BF, 0)],
        [pltpu.VMEM((groups, shards * keys, 2 * width), BF)]
        + [pltpu.VMEM((HEADS // 2, shards * keys, per), BF)] * 2,
        2 * shards * groups * keys * width * (5 * per // 2 + 2 * mine),
    )
    scatter_keyval = Scatter(keep_keyval, give_keyval, "grp", [1, 2])
    scatter_cross = Scatter(keep_cross, give_cross, "grp", [2, 1])
    dq = hold(dq, scatter_mlp, scatter_self)
    scatter_mlp.step()
    scatter_self.step()
    dkv = after(dkv, scatter_mlp, scatter_self)
    (grad_pixels,) = call(
        pixel_back_kernel, [], [dkv.reshape(groups * keys, 2 * width), in_pieces(w_keyval, 4), yn, ry, gy],
        [((groups * keys, width), F32)],
        [pltpu.VMEM((groups * keys, width), F32)],
        2 * groups * keys * width * 2 * width,
    )
    index = lax.axis_index("grp") * shards + place
    index_ref = index.reshape(1).astype(jnp.int32)
    all_gains = jnp.stack([gain_cross, gain_pixel, gain_self, gain_mlp])
    own_gains = lax.dynamic_slice_in_dim(all_gains, index * block, block, 1)

    def finish(scatters, heights, gained):
        ends = [scatter.rest() for scatter in scatters]

        def joined(arrays):
            pieces, start = [], 0
            for array in arrays:
                where = pl.ds(start, array.shape[0])
                pieces.append((array, lambda scalars, where=where: where, None))
                start += array.shape[0]
            return Stack((start, width), BF, pieces)

        wides = [(heights_of[0], width * len(heights_of)) for heights_of in heights]
        return call(
            functools.partial(finish_kernel, heights, list(gained), len(ends)), [index_ref],
            [joined([keep for keep, _ in ends])] + [Near(got) for _, got in ends]
            + [part_of(weight, lambda scalars: scalars[0][0] * block, block) for weight, _ in gained.values()]
            + [own_gains[row : row + 1] for _, row in gained.values()],
            [(shape, F32) for shape in wides] + [((1, block), F32)] * len(gained),
            [], 1e6,
        )

    grad_pixels = hold(grad_pixels, scatter_keyval, scatter_cross, scatter_self)
    scatter_keyval.step()
    scatter_cross.step()
    grad_pixels = after(grad_pixels, scatter_keyval, scatter_cross)
    d_w_qkv, d_w_self_out, d_g_self = finish([scatter_self], [[block] * 3, [block]], {0: (w_qkv, 2)})
    dq, d_w_qkv, scatter_mlp.got = lax.optimization_barrier((dq, d_w_qkv, scatter_mlp.got))
    dq, grad_pixels = after((dq, grad_pixels), scatter_keyval, scatter_cross)
    (grad_latents,) = call(
        query_back_kernel, [], [dq, in_pieces(w_query, 2), xn, rx, gx, grad_cross],
        [((rows, width), F32)],
        [pltpu.VMEM((rows, width), F32)],
        2 * rows * width * width,
    )

    grad_latents = hold(grad_latents, scatter_mlp, scatter_keyval, scatter_cross)
    scatter_keyval.step()
    scatter_cross.step()
    d_w_out, d_w_in, d_g_mlp = finish(
        [scatter_mlp], [[wide_block], [block] * (wide // width)], {1: (w_in, 3)}
    )
    d_w_keyval, d_w_query, d_w_cross_out, d_g_pixel, d_g_cross = finish(
        [scatter_keyval, scatter_cross], [[block] * 2, [block], [block]], {0: (w_keyval, 1), 1: (w_query, 0)}
    )
    return (
        out_low,
        grad_latents,
        grad_pixels.reshape(groups, keys, width),
        d_g_cross.reshape(block),
        d_g_pixel.reshape(block),
        d_w_query,
        d_w_keyval,
        d_w_cross_out,
        d_g_self.reshape(block),
        d_w_qkv,
        d_w_self_out,
        d_g_mlp.reshape(block),
        d_w_in,
        d_w_out,
        averaged.reshape(IMAGES),
    )


def solution(mesh):
    both = ("grp", "pix")
    in_specs = (
        P("grp", None), P("grp", "pix", None), P("grp", "pix"), P("grp"), P("grp", None),
    ) + (P(),) * 11
    out_specs = (
        P("grp", None), P("grp", None), P("grp", "pix", None), P(both), P(both),
        P(both, None), P(both, None), P(both, None), P(both), P(both, None), P(both, None),
        P(both), P(both, None), P(both, None), P(),
    )
    return jax.shard_map(
        per_device, mesh=mesh, in_specs=in_specs, out_specs=out_specs, check_vma=False
    )
```

```python
import functools
import math

import jax
import jax.numpy as jnp
from jax import lax
from jax.experimental import pallas as pl
from jax.experimental.pallas import tpu as pltpu
from jax.sharding import PartitionSpec as P

HEADS = 8
IMAGES = 8
NEG_FILL = -1e30
EPSILON = 1e-05
BF = jnp.bfloat16
F32 = jnp.float32
LOG2E = 1.0 / math.log(2.0)
LANES = 128
COUNTS = 64
HBM = pl.BlockSpec(memory_space=pltpu.HBM)
SM = pl.BlockSpec(memory_space=pltpu.SMEM)


def dot(left, right, left_dim, right_dim):
    return lax.dot_general(
        left, right, (((left_dim,), (right_dim,)), ((), ())), preferred_element_type=F32
    )


def tiles(total, most):
    return [(start, min(most, total - start)) for start in range(0, total, most)]


def span(index, size):
    return pl.ds(pl.multiple_of(index * size, size), size)


def loop(count, body):
    lax.fori_loop(0, count, lambda index, carry: (body(index), carry)[1], 0)


class Stack:
    separate = False

    def __init__(self, shape, dtype, pieces):
        self.shape, self.dtype, self.pieces = shape, dtype, pieces


def whole_of(array):
    return Stack(array.shape, array.dtype, [(array, None, None)])


class Near:
    def __init__(self, array, start=0, size=None):
        self.array = pltpu.with_memory_space_constraint(array, pltpu.VMEM)
        self.start, self.size = start, size

    def box(self, ref):
        return Box(ref if self.size is None else ref.at[pl.ds(self.start, self.size)], [])


def in_pieces(array, count):
    size = array.shape[0] // count
    pieces = [
        (array, lambda scalars, j=j: j, lambda scalars, j=j: pl.ds(j * size, size)) for j in range(count)
    ]
    stack = Stack((count, size) + array.shape[1:], array.dtype, pieces)
    stack.separate = True
    return stack


def by_columns(array, size=1024):
    count = array.shape[1] // size
    pieces = [
        (array, lambda scalars, j=j: j, lambda scalars, j=j: (slice(None), pl.ds(j * size, size)))
        for j in range(count)
    ]
    stack = Stack((count, array.shape[0], size), array.dtype, pieces)
    stack.separate = True
    return stack


def each_of(array):
    pieces = [(array, lambda scalars, j=j: j, lambda scalars, j=j: j) for j in range(array.shape[0])]
    stack = Stack(array.shape, array.dtype, pieces)
    stack.separate = True
    return stack


def part_of(array, start, size):
    def which(scalars):
        return pl.ds(pl.multiple_of(start(scalars), size) if callable(start) else start, size)

    return Stack((size,) + array.shape[1:], array.dtype, [(array, None, which)])


class Box:
    def __init__(self, ref, copies):
        self.ref, self.copies = ref, copies

    def ready(self):
        for copy in self.copies:
            copy.wait()
        self.copies = []
        return self.ref


class Pieces(Box):
    def __init__(self, ref, copies, sems):
        super().__init__(ref, [])
        self.sources, self.sems = copies, sems

    def wait_piece(self, index):
        pltpu.make_async_copy(self.sources[0], self.ref.at[index], self.sems.at[index]).wait()


class Slot:
    def __init__(self, ref, targets, sems):
        self.ref, self.targets, self.sems, self.copies = ref, targets, sems, []

    def send(self, source):
        each = source.shape[0] // len(self.targets)
        for i, target in enumerate(self.targets):
            part = source if len(self.targets) == 1 else source.at[pl.ds(i * each, each)]
            copy = pltpu.make_async_copy(part, target, self.sems.at[i])
            copy.start()
            self.copies.append(copy)

    def send_rows(self, start, size, part):
        rows = pl.ds(start, size)
        copy = pltpu.make_async_copy(self.ref.at[rows], self.targets[0].at[rows], self.sems.at[part])
        copy.start()
        self.copies.append(copy)

    def send_to(self, pieces):
        for i, (source, index) in enumerate(pieces):
            copy = pltpu.make_async_copy(source, self.targets[0].at[index], self.sems.at[i])
            copy.start()
            self.copies.append(copy)

    def done(self):
        self.send(self.ref)


def call(kernel, scalars, loads, outs, scratch, flops):
    order = [isinstance(item, Near) for item in loads]
    near = [item for item in loads if isinstance(item, Near)]
    loads = [item for item in loads if not isinstance(item, Near)]
    loads = [item if isinstance(item, Stack) else whole_of(item) for item in loads]
    parts = [out[2] if len(out) > 2 else 1 for out in outs]
    targets = []
    for out, count in zip(outs, parts):
        count = max(count, 1)
        shape = (out[0][0] // count,) + tuple(out[0][1:])
        targets += [jax.ShapeDtypeStruct(shape, out[1])] * count
    most = max(max(parts), 2)
    arrays = [piece[0] for item in loads for piece in item.pieces]
    deep = max(len(item.pieces) for item in loads)

    def whole(*refs):
        refs = list(refs)

        def take(count):
            taken = refs[:count]
            del refs[:count]
            return taken

        scalar_refs = take(len(scalars))
        near_boxes = [item.box(ref) for item, ref in zip(near, take(len(near)))]
        load_refs = [take(len(item.pieces)) for item in loads]
        target_refs = take(len(targets))
        load_bufs = take(len(loads))
        out_bufs = [take(1)[0] if count else None for count in parts]
        extra = take(len(scratch))
        load_sems, out_sems = refs
        boxes, first, late = [], [], {}
        for i, (item, sources, buf) in enumerate(zip(loads, load_refs, load_bufs)):
            copies = []
            for j, (source, (_, where, which)) in enumerate(zip(sources, item.pieces)):
                copy = pltpu.make_async_copy(
                    source if which is None else source.at[which(scalar_refs)],
                    buf if where is None else buf.at[where(scalar_refs)],
                    load_sems.at[i, j],
                )
                copies.append(copy)
                if item.separate and j:
                    late.setdefault(j, []).append(copy)
                else:
                    first.append(copy)
            after_item = i + 1 == len(loads) or not (item.separate and loads[i + 1].separate)
            if after_item:
                for copy in first + [copy for j in sorted(late) for copy in late[j]]:
                    copy.start()
                first, late = [], {}
            if item.separate:
                boxes.append(Pieces(buf, [source.at[item.pieces[0][2](scalar_refs)]], load_sems.at[i]))
            else:
                boxes.append(Box(buf, copies))
        slots = []
        for i, (buf, count) in enumerate(zip(out_bufs, parts)):
            count = max(count, 1)
            slots.append(Slot(buf, target_refs[:count], out_sems.at[i]))
            del target_refs[:count]
        far = list(boxes)
        everything = [near_boxes.pop(0) if is_near else far.pop(0) for is_near in order]
        kernel(*scalar_refs, *everything, *slots, *extra)
        for box in boxes:
            box.ready()
        for slot in slots:
            if not slot.copies:
                slot.done()
        for slot in slots:
            for copy in slot.copies:
                copy.wait()

    moved = sum(a.size * a.dtype.itemsize for a in arrays)
    return pl.pallas_call(
        whole,
        out_shape=targets,
        in_specs=[SM] * len(scalars) + [pl.BlockSpec(memory_space=pltpu.VMEM)] * len(near) + [HBM] * len(arrays),
        out_specs=[HBM] * len(targets),
        scratch_shapes=[pltpu.VMEM(item.shape, item.dtype) for item in loads]
        + [pltpu.VMEM(out[0], out[1]) for out, count in zip(outs, parts) if count]
        + list(scratch)
        + [pltpu.SemaphoreType.DMA((len(loads), deep)), pltpu.SemaphoreType.DMA((len(outs), most))],
        compiler_params=pltpu.CompilerParams(vmem_limit_bytes=60 * 2**20),
        cost_estimate=pl.CostEstimate(flops=int(flops), bytes_accessed=int(moved), transcendentals=0),
    )(*scalars, *[item.array for item in near], *arrays)


def norm_rows(src, gain, dst, rstd, step=128):
    rows = src.shape[0]

    def body(i):
        sl = span(i, step)
        values = src[sl, :].astype(F32)
        center = values - jnp.mean(values, axis=-1, keepdims=True)
        spread = jnp.mean(center * center, axis=-1, keepdims=True)
        scale = lax.rsqrt(spread + EPSILON)
        dst[sl, :] = (center * scale * gain[...]).astype(BF)
        rstd[sl, :] = jnp.broadcast_to(scale, (step, LANES))

    loop(rows // step, body)


def norm_back(dy, normed, rstd, gain, base, out, low, step=64):
    rows = dy.shape[0]
    half = rows // 2

    def body(i, part):
        sl = span(i, step)
        grad = dy[sl, :]
        normal = normed[sl, :].astype(F32)
        gains = gain[...]
        scaled = grad * gains
        mean_scaled = jnp.mean(scaled, axis=-1, keepdims=True)
        mean_norm = jnp.mean(grad * normal, axis=-1, keepdims=True)
        result = rstd[sl, :1] * (scaled - mean_scaled - normal * (1.0 / gains) * mean_norm)
        if base is not None:
            result = result + (base(sl, part) if callable(base) else base[sl, :])
        out.ref[sl, :] = result
        if low is not None:
            low.ref[sl, :] = result.astype(BF)

    for part in range(2):
        loop(half // step, lambda i: body(part * (half // step) + i, part))
        for slot in (out, low):
            if slot is not None:
                slot.send_rows(part * half, half, part)


def head(h, size, base=0):
    return slice(base + h * size, base + (h + 1) * size)


def attend(heads, limit, factor, scores, weights):
    for i, (q, k, _, _) in enumerate(heads):
        scores[i] = dot(k(), q(), 1, 1)
    totals = []
    for i in range(len(heads)):
        values = scores[i] * factor
        if limit is not None:
            key = lax.broadcasted_iota(jnp.int32, values.shape, 0)
            values = jnp.where(key < limit, values, NEG_FILL)
        most = jnp.max(values, axis=0, keepdims=True)
        values = jnp.exp2(values - most)
        total = jnp.sum(values, axis=0, keepdims=True)
        weights[i] = values.astype(BF)
        totals.append((1.0 / total, most + jnp.log(total) * LOG2E, most))
    for i, (_, _, v, put) in enumerate(heads):
        inverse, lse, most = totals[i]
        put(dot(v(), weights[i], 0, 0) * inverse, lse, most)


def attend_scratch(keys, queries):
    return [pltpu.VMEM((HEADS, keys, queries), F32), pltpu.VMEM((HEADS, keys, queries), BF)]


def scatter_slot(me, target, members):
    different = target ^ me
    slot, left = 0, members
    while left > 1:
        left //= 2
        slot = slot + (different & 1) * left
        different = different >> 1
    return slot


def put_blocks(out, me, members, offset, values):
    each = values.shape[0] // members
    for target in range(members):
        out[scatter_slot(me, target, members), offset : offset + each, :] = values[
            target * each : (target + 1) * each
        ]


def pre_kernel(factor, filled, x, gx, wq, y, gy, wkv, sel,
               xn, q, yn, kv, own_cols, out_t, lse, rx, ry, kept, tops, xn_part, scores):
    groups, width, latents = out_t.ref.shape
    size = width // HEADS
    keys = y.ref.shape[0] // groups
    norm_rows(x.ready(), gx.ready(), xn.ref, rx.ref)
    xn.done(), rx.done()
    wq = wq.ready()
    for start, length in tiles(width, 1024):
        cols = slice(start, start + length)
        q.ref[:, cols] = dot(xn.ref[...], wq[:, cols], 1, 0).astype(BF)
    q.done()
    norm_rows(y.ready(), gy.ready(), yn.ref, ry.ref)
    yn.done(), ry.done()
    kv_ref, wkv = kv.ref, wkv.ready()

    def project(i):
        kv_ref[:, span(i, 1024)] = dot(yn.ref[...], wkv[:, span(i, 1024)], 1, 0).astype(BF)

    loop(2 * width // 1024, project)
    kv.done()
    own_cols.ref[...] = dot(sel.ready()[...], yn.ref[...], 1, 1).astype(BF)
    own_cols.done()
    xn_part.ref[...] = dot(sel.ref[...], xn.ref[...], 1, 1).astype(BF)
    xn_part.done()
    for g in range(groups):
        rows, cols = slice(g * latents, (g + 1) * latents), slice(g * keys, (g + 1) * keys)
        heads = []
        for h in range(HEADS):

            def put(result, total, most, h=h):
                out_t.ref[g, head(h, size), :] = result.astype(BF)
                lse.ref[g, h : h + 1, :] = total
                tops.ref[g, h : h + 1, :] = most

            heads.append((
                lambda h=h: q.ref[rows, head(h, size)], lambda h=h: kv_ref[cols, head(h, size)],
                lambda h=h: kv_ref[cols, head(h, size, width)], put,
            ))
        attend(heads, filled[g], factor, scores, kept.ref.at[g])


def shard_kernel(factor, group, y, gy, wkv, sel, q, filled, kv, own_cols, out_t, lse, kept, tops, yn, ry, scores):
    width, latents = out_t.ref.shape
    shard_body(factor, group, y, gy, wkv, sel, q, filled, kv, own_cols, out_t.ref, lse.ref, kept, tops, yn, ry, scores)


def shard_body(factor, group, y, gy, wkv, sel, q, filled, kv, own_cols, out_t, lse, kept, tops, yn, ry, scores):
    width, latents = out_t.shape
    size = width // HEADS
    norm_rows(y.ready(), gy.ready(), yn, ry)
    kv_ref = kv.ref

    def project(i):
        wkv.wait_piece(i)
        kv_ref[:, span(i, 1024)] = dot(yn[...], wkv.ref[i], 1, 0).astype(BF)

    loop(2 * width // 1024, project)
    kv.done()
    own_cols.ref[...] = dot(sel.ready()[...], yn[...], 1, 1).astype(BF)
    own_cols.done()
    q = q.ready()
    limit = filled.ready()[group : group + 1, :latents].astype(F32).astype(jnp.int32)
    heads = []
    for h in range(HEADS):

        def put(result, total, most, h=h):
            out_t[head(h, size), :] = result.astype(BF)
            lse[h : h + 1, :] = total
            tops.ref[h : h + 1, :] = most

        heads.append((
            lambda h=h: q[:, head(h, size)], lambda h=h: kv_ref[:, head(h, size)],
            lambda h=h: kv_ref[:, head(h, size, width)], put,
        ))
    attend(heads, limit, factor, scores, kept.ref)
    kept.done(), tops.done()


def last_shard_kernel(factor, group, shards, place, y, gy, wkv, sel, q, filled, part_t, part_lse,
                      kv, own_cols, out_t, lse, kept, tops, yn, ry, scores):
    width, _ = out_t.ref.shape
    size = width // HEADS
    mine = lax.rem(place[0] + 1, shards)
    shard_body(
        factor, group, y, gy, wkv, sel, q, filled, kv, own_cols,
        part_t.ref.at[mine], part_lse.ref.at[mine], kept, tops, yn, ry, scores,
    )
    part_t, part_lse = part_t.ready(), part_lse.ready()
    most = functools.reduce(jnp.maximum, [part_lse[z] for z in range(shards)])
    shares = [jnp.exp2(part_lse[z] - most) for z in range(shards)]
    total = functools.reduce(jnp.add, shares)
    lse.ref[...] = most + jnp.log(total) * LOG2E
    shares = [share / total for share in shares]
    for h in range(HEADS):
        merged = functools.reduce(jnp.add, [
            shares[z][h : h + 1, :] * part_t[z, head(h, size), :].astype(F32) for z in range(shards)
        ])
        out_t.ref[head(h, size), :] = merged.astype(BF)


def forward_kernel(factor, block, shards, place, image, cross_t, x, wco, gself, wqkv, wso, gmlp, win, wout,
                   hn, qkv, self_t, lse, mn, slope, hid_out, low, rself, rmlp,
                   sums, norms, resid, hidden, scores, weights):
    groups, width, latents = cross_t.ref.shape
    size = width // HEADS
    wide = win.ref.shape[1]
    cross_t, x, wco = cross_t.ready(), x.ready(), wco.ready()
    for g in range(groups):
        rows = slice(g * latents, (g + 1) * latents)
        resid[rows, :] = x[rows, :].astype(F32) + dot(cross_t[g], wco[...], 0, 0)
    norm_rows(resid, gself.ready(), hn.ref, rself.ref)
    hn.done(), rself.done()
    wqkv = wqkv.ready()

    def project(i):
        qkv.ref[:, span(i, 1024)] = dot(hn.ref[...], wqkv[:, span(i, 1024)], 1, 0).astype(BF)

    loop(3 * width // 1024, project)
    qkv.done()
    for g in range(groups):
        rows = slice(g * latents, (g + 1) * latents)
        heads = []
        for h in range(HEADS):

            def put(result, total, most, h=h):
                self_t.ref[g, head(h, size), :] = result.astype(BF)
                lse.ref[g, h : h + 1, :] = total

            heads.append((
                lambda h=h: qkv.ref[rows, head(h, size)], lambda h=h: qkv.ref[rows, head(h, size, width)],
                lambda h=h: qkv.ref[rows, head(h, size, 2 * width)], put,
            ))
        attend(heads, None, factor, scores, weights)
    self_t.done(), lse.done()
    wso = wso.ready()
    for g in range(groups):
        rows = slice(g * latents, (g + 1) * latents)
        resid[rows, :] += dot(self_t.ref[g], wso[...], 0, 0)
    norm_rows(resid, gmlp.ready(), mn.ref, rmlp.ref)
    mn.done(), rmlp.done()
    win = win.ready()
    if hid_out.ref.shape[1] == wide:
        hidden = hid_out.ref

    def expand(i):
        act = dot(mn.ref[...], win[:, span(i, 1024)], 1, 0).astype(BF)
        root = math.sqrt(2.0 / math.pi)
        square = act * act
        half = BF(0.5) + BF(0.5) * jnp.tanh(act * (BF(root) + BF(root * 0.044715) * square))
        result = act * half
        hidden[:, span(i, 1024)] = result
        bend = BF(2.0 * root) + BF(6.0 * root * 0.044715) * square
        slope.ref[i] = half + result * (BF(1.0) - half) * bend

    loop(wide // 1024, expand)
    slope.done()
    if hid_out.ref.shape[1] != wide:
        for g in range(wide // (block * shards)):
            start = pl.multiple_of(g * block * shards + place[0] * block, block)
            hid_out.ref[:, g * block : (g + 1) * block] = hidden[:, pl.ds(start, block)]
    hid_out.done()
    wout = wout.ready()
    squares = [0.0] * groups
    for start, length in tiles(width, 512):
        cols = slice(start, start + length)
        values = resid[:, cols] + dot(hidden[...], wout[:, cols], 1, 0)
        low.ref[:, cols] = values.astype(BF)
        for g in range(groups):
            own = values[g * latents : (g + 1) * latents]
            squares[g] = squares[g] + jnp.sum((own * own).reshape(latents // 8, 8, length), axis=0)
    low.done()
    lane = lax.broadcasted_iota(jnp.int32, (1, LANES), 1)
    found = jnp.zeros((1, LANES), F32)
    for g in range(groups):
        total = squares[g]
        total = jnp.sum(jnp.sum(total, axis=1, keepdims=True), axis=0, keepdims=True)
        norm = jnp.sqrt(total / (latents * width) + 1e-06)
        norms.ref[g : g + 1, :] = jnp.broadcast_to(norm, (1, LANES))
        found = found + jnp.where(lane == image[g], norm, 0.0)
        found = found + jnp.where(lane == image[g] + COUNTS, 1.0, 0.0)
    sums.ref[...] = found


def mlp_back_kernel(members, me, image, sums, norms, cot, xf, wout, slope, hid, win, sel, mn, rmlp, gmlp,
                    blocks, gself, r_self, averaged, r_low, d_act, d_mn):
    rows, width = xf.ref.shape
    groups = image.shape[0]
    latents = rows // groups
    count, tile = slope.ref.shape[0], slope.ref.shape[2]
    wide = count * tile
    me = me[0]
    sums, norms = sums.ready()[...], norms.ready()
    lane = lax.broadcasted_iota(jnp.int32, (1, LANES), 1)
    counts = jnp.maximum(pltpu.roll(sums, COUNTS, 1), 1.0)
    means = sums / counts
    averaged.ref[...] = means[:, :IMAGES]
    shares = means / counts
    cot, xf = cot.ready(), xf.ready()
    factors = []
    step = 64
    for g in range(groups):
        share = jnp.sum(jnp.where(lane == image[g], shares, 0.0), axis=1, keepdims=True)
        fac = share / norms[g : g + 1, :1]
        factors.append(fac)

        def add(i, g=g, fac=fac):
            sl = pl.ds(pl.multiple_of(g * latents + i * step, step), step)
            grad = cot[sl, :].astype(F32) + fac * xf[sl, :].astype(F32)
            r_low[sl, :] = grad.astype(BF)

        loop(latents // step, add)

    def hidden_back(i):
        wout.wait_piece(i)
        d_hidden = dot(r_low[...], wout.ref[i], 1, 1)
        slope.wait_piece(i)
        d_act[:, span(i, tile)] = slope.ref[i] * d_hidden.astype(BF)

    loop(count, hidden_back)
    put_blocks(blocks.ref, me, members, 0, dot(hid.ready()[...], r_low[...], 0, 0).astype(BF))
    below = hid.ref.shape[1] // members
    part = dot(sel.ready()[...], mn.ready()[...], 1, 1).astype(BF)
    each = part.shape[0] // members
    for j in range(wide // width):
        put_blocks(
            blocks.ref, me, members, below + j * each,
            dot(part, d_act[:, j * width : (j + 1) * width], 1, 0).astype(BF),
        )
    blocks.done()
    win = win.ready()
    for start, length in tiles(width, 512):
        d_mn[:, start : start + length] = dot(d_act[...], win[start : start + length, :], 1, 1)

    def grad_final(sl, part):
        return cot[sl, :].astype(F32) + factors[part * groups // 2] * xf[sl, :].astype(F32)

    norm_back(d_mn, mn.ref, rmlp.ready(), gmlp.ready(), grad_final, gself, r_self)


def self_back_kernel(factor, scale, members, me, wso, r_self, self_t, lse, qkv, hn, sel,
                     d_qkv, blocks, d_t, scores, probs, d_probs, d_scores, low):
    groups, width, latents = self_t.ref.shape
    size = width // HEADS
    me = me[0]
    d_t[...] = dot(wso.ready()[...], r_self.ready()[...], 1, 1)
    self_t, lse, qkv = self_t.ready(), lse.ready(), qkv.ready()
    for g in range(groups):
        rows = slice(g * latents, (g + 1) * latents)
        deltas = []
        for h in range(HEADS):
            d_out = d_t[head(h, size), rows]
            deltas.append(jnp.sum(
                d_out * self_t[g, head(h, size), :].astype(F32), axis=0, keepdims=True
            ))
            low[h] = d_out.astype(BF)
        for h in range(HEADS):
            scores[h] = dot(qkv[rows, head(h, size, width)], qkv[rows, head(h, size)], 1, 1)
            d_probs[h] = dot(qkv[rows, head(h, size, 2 * width)], low[h], 1, 0)
        for h in range(HEADS):
            values = jnp.exp2(scores[h] * factor - lse[g, h : h + 1, :])
            probs[h] = values.astype(BF)
            d_scores[h] = (values * (d_probs[h] - deltas[h])).astype(BF)
        for h in range(HEADS):
            dq = dot(qkv[rows, head(h, size, width)], d_scores[h], 0, 0) * scale
            d_qkv.ref[rows, head(h, size)] = dq.T.astype(BF)
            dk = dot(d_scores[h], qkv[rows, head(h, size)], 1, 0) * scale
            d_qkv.ref[rows, head(h, size, width)] = dk.astype(BF)
            dv = dot(probs[h], low[h], 1, 1)
            d_qkv.ref[rows, head(h, size, 2 * width)] = dv.astype(BF)
    d_qkv.done()
    sel = sel.ready()
    part = dot(sel[...], hn.ready()[...], 1, 1).astype(BF)
    each = part.shape[0] // members
    for j in range(3):
        put_blocks(
            blocks.ref, me, members, j * each,
            dot(part, d_qkv.ref[:, j * width : (j + 1) * width], 1, 0).astype(BF),
        )
    put_blocks(blocks.ref, me, members, 3 * each, weight_part(sel, self_t, r_self.ref))


def weight_part(sel, source_t, low):
    groups, _, latents = source_t.shape
    total = 0.0
    for g in range(groups):
        mine = dot(sel[...], source_t[g], 1, 0).astype(BF)
        total = total + dot(mine, low[g * latents : (g + 1) * latents, :], 1, 0)
    return total.astype(BF)


def between_kernel(d_qkv, wqkv, hn, rself, gain, gself, wco, cross_t, keep, got,
                   total, r_cross, d_out_t, delta, gcross, d_hn, d_t):
    groups, width, latents = cross_t.ref.shape
    size = width // HEADS
    times_pieces(d_hn, d_qkv.ready(), wqkv)
    keep, got = keep.ready(), got.ready()

    def add(i):
        total.ref[i] = keep[i] + got[i]

    loop(keep.shape[0], add)
    total.done()
    norm_back(
        d_hn, hn.ready(), rself.ready(), gain.ready(), gself.ready(), gcross, r_cross
    )
    d_t[...] = dot(wco.ready()[...], r_cross.ref[...], 1, 1)
    cross_t = cross_t.ready()
    for g in range(groups):
        rows = slice(g * latents, (g + 1) * latents)
        for h in range(HEADS):
            d_out = d_t[head(h, size), rows]
            delta.ref[g, h : h + 1, :] = jnp.sum(
                d_out * cross_t[g, head(h, size), :].astype(F32), axis=0, keepdims=True
            )
            d_out_t.ref[g, head(h, size), :] = d_out.astype(BF)


def cross_back_kernel(scale, members, groups, shards, place, me, q, d_out_t, lse, delta, tops, *refs):
    kvs, kepts, refs = refs[: 4 * groups : 2], refs[1 : 4 * groups : 2], refs[4 * groups :]
    sel, xn_part, own_cols, cross_t, r_cross, blocks, more, dq, dkv_own, dkv, probs, d_scores = refs
    _, width, latents = d_out_t.ref.shape
    size = width // HEADS
    keys = dkv_own.targets[0].shape[1]
    q, d_out_t, lse, delta, tops = (box.ready() for box in (q, d_out_t, lse, delta, tops))
    for g in range(groups):
        rows = slice(g * latents, (g + 1) * latents)
        for part in range(2):
            kv, kept = kvs[2 * g + part].ready(), kepts[2 * g + part].ready()
            for j in range(HEADS // 2):
                h = part * (HEADS // 2) + j
                cols, value_cols = head(h, size), head(h, size, width)
                q_h, k_h, d_out = q[rows, cols], kv[:, head(j, size)], d_out_t[g, cols, :]
                d_probs = dot(kv[:, head(j, size, width // 2)], d_out, 1, 0)
                for z in range(shards):
                    own = slice(z * keys, (z + 1) * keys)
                    share = jnp.exp2(tops[g, z, h : h + 1, :] - lse[g, h : h + 1, :])
                    values = kept[j, own, :].astype(F32) * share
                    probs[j, own, :] = values.astype(BF)
                    d_scores[j, own, :] = (values * (d_probs[own, :] - delta[g, h : h + 1, :])).astype(BF)
                dkv[g, :, cols] = (dot(d_scores[j], q_h, 1, 0) * scale).astype(BF)
                dkv[g, :, value_cols] = dot(probs[j], d_out, 1, 1).astype(BF)
                dq.ref[rows, cols] = (dot(k_h, d_scores[j], 0, 0) * scale).T.astype(BF)
    dq.done()
    own_rows = pl.ds(pl.multiple_of(place[0] * keys, keys), keys)
    dkv_own.send_to([(dkv.at[g, own_rows], g) for g in range(groups)])
    own_cols, sel = own_cols.ready(), sel.ready()
    each = sel.shape[0] // members
    for j in range(2):
        total = functools.reduce(jnp.add, [
            dot(own_cols[g], dkv[g, :, j * width : (j + 1) * width], 1, 0) for g in range(groups)
        ])
        put_blocks(blocks.ref, me[0], members, j * each, total.astype(BF))
    blocks.done()
    put_blocks(more.ref, me[0], members, 0, dot(xn_part.ready()[...], dq.ref[...], 1, 0).astype(BF))
    put_blocks(more.ref, me[0], members, each, weight_part(sel, cross_t.ready(), r_cross.ready()))


def pixel_back_kernel(dkv, wkv, yn, ry, gy, gpix, d_yn):
    times_pieces(d_yn, dkv.ready(), wkv)
    norm_back(d_yn, yn.ready(), ry.ready(), gy.ready(), None, gpix, None)


def query_back_kernel(dq, wq, xn, rx, gx, gcross, glat, d_xn):
    times_pieces(d_xn, dq.ready(), wq)
    norm_back(d_xn, xn.ready(), rx.ready(), gx.ready(), gcross.ready(), glat, None)


def times_pieces(out, left, weight):
    count, size, _ = weight.ref.shape

    def body(i):
        weight.wait_piece(i)
        out[:, span(i, size)] = dot(left[...], weight.ref[i], 1, 1)

    loop(count, body)


def finish_kernel(heights, gained, count, index, keep, *refs):
    gots, refs = [got.ready() for got in refs[:count]], refs[count:]
    keep = keep.ready()
    weights, gains = refs[: len(gained)], refs[len(gained) : 2 * len(gained)]
    outs = refs[2 * len(gained) :]
    width = keep.shape[1]
    start, base = 0, 0
    for i, pieces in enumerate(heights):
        for j, height in enumerate(pieces):
            if start - base >= gots[0].shape[0]:
                base += gots.pop(0).shape[0]
            came = gots[0][start - base : start - base + height, :]
            outs[i].ref[:, j * width : (j + 1) * width] = (
                keep[start : start + height, :].astype(F32) + came.astype(F32)
            )
            start += height
        outs[i].done()
    for n, i in enumerate(gained):
        products = weights[n].ready()[...].astype(F32) * outs[i].ref[...]
        ones = jnp.ones((8, products.shape[1]), F32)
        sums = lax.dot_general(
            ones, products, (((1,), (1,)), ((), ())),
            precision=lax.Precision.HIGHEST, preferred_element_type=F32,
        )
        outs[len(heights) + n].ref[...] = sums[:1, :] / gains[n].ready()[...]


def swap_sum(value, axis):
    count = lax.axis_size(axis)
    step = 1
    while step < count:
        value = value + lax.ppermute(value, axis, [(i, i ^ step) for i in range(count)])
        step *= 2
    return value


class Scatter:
    def __init__(self, keep, give, axis, order):
        self.axis, self.count = axis, lax.axis_size(axis)
        bits = self.count.bit_length() - 1
        self.left = list(range(1, bits))
        self.order = [bit for bit in order if bit < bits] + [bit for bit in self.left if bit not in order]
        shape = (2,) * (bits - 1) + keep.shape[1:]
        self.keep, self.got = keep.reshape(shape), self.swap(give, 0).reshape(shape)

    def swap(self, value, bit):
        return lax.ppermute(value, self.axis, [(i, i ^ (1 << bit)) for i in range(self.count)])

    def step(self):
        bit = self.order.pop(0)
        place = self.left.index(bit)
        self.left.remove(bit)

        def half(which):
            first, second = (lax.index_in_dim(a, which, place, keepdims=False) for a in (self.keep, self.got))
            return (first.astype(F32) + second.astype(F32)).astype(BF)

        self.keep, self.got = half(0), self.swap(half(1), bit)

    def step_with(self, keep, give):
        bit = self.order.pop(0)
        place = self.left.index(bit)
        self.left.remove(bit)
        assert place == 0
        shape = (2,) * len(self.left) + keep.shape[1:]
        self.keep, self.got = keep.reshape(shape), self.swap(give, bit).reshape(shape)

    def rest(self):
        while self.order:
            self.step()
        return self.keep, self.got


def after(value, *scatters):
    value, keeps = lax.optimization_barrier((value, [scatter.keep for scatter in scatters]))
    for scatter, keep in zip(scatters, keeps):
        scatter.keep = keep
    return value


def hold(value, *scatters):
    value, gots = lax.optimization_barrier((value, [scatter.got for scatter in scatters]))
    for scatter, got in zip(scatters, gots):
        scatter.got = got
    return value


def per_device(latents, pixels, pixel_mask, group_image, cotangent, gain_cross, gain_pixel, w_query,
               w_keyval, w_cross_out, gain_self, w_qkv, w_self_out, gain_mlp, w_in, w_out):
    groups, keys, width = pixels.shape
    rows = latents.shape[0]
    per = rows // groups
    size = width // HEADS
    wide = w_in.shape[1]
    scale = 1.0 / math.sqrt(size)
    factor = scale * LOG2E
    shards, members = lax.axis_size("pix"), lax.axis_size("grp")
    place = lax.axis_index("pix")
    me = lax.axis_index("grp").reshape(1).astype(jnp.int32)
    block = width // (shards * members)
    wide_block = wide // (shards * members)
    mine = members * block

    y = pixels.reshape(groups * keys, width)
    gx, gy, gs, gm = (g.reshape(1, width) for g in (gain_cross, gain_pixel, gain_self, gain_mlp))
    own_row = lax.broadcasted_iota(jnp.int32, (mine, width), 0)
    column = lax.broadcasted_iota(jnp.int32, (mine, width), 1)
    wanted = ((own_row // block) * shards + place) * block + own_row % block
    sel = (column == wanted).astype(BF)
    own_filled = jnp.sum(pixel_mask, axis=1, dtype=jnp.int32)
    extra = jnp.pad(own_filled.astype(BF), (0, 16 - groups))[:, None]
    turn = [(i, (i + 1) % shards) for i in range(shards)]
    moving = [jnp.concatenate([pixels[0], jnp.broadcast_to(extra, (16, width))], axis=0)]
    moving += [pixels[g] for g in range(1, groups)]
    here = place.reshape(1).astype(jnp.int32)
    stats = ((rows, LANES), F32)
    xn, q, yn, kv, own_cols, out_t, lse, rx, ry, kept, tops, xn_part = call(
        functools.partial(pre_kernel, factor), [own_filled],
        [latents, gx, w_query, y, gy, w_keyval, sel],
        [((rows, width), BF), ((rows, width), BF), ((groups * keys, width), BF),
         ((groups * keys, 2 * width), BF), ((mine, groups * keys), BF), ((groups, width, per), BF),
         ((groups, HEADS, per), F32), stats, ((groups * keys, LANES), F32),
         ((groups, HEADS, keys, per), BF), ((groups, HEADS, per), F32), ((mine, rows), BF)],
        attend_scratch(keys, per)[:1], 2 * (rows * width * width + groups * keys * width * 2 * width),
    )

    def slot(s):
        return lambda scalars: lax.rem(scalars[0][0] + (shards - s), shards)

    def key_rows(s):
        return lambda scalars: pl.ds(pl.multiple_of(slot(s)(scalars) * keys, keys), keys)

    def col_place(s, g):
        return lambda scalars: (g, slice(None), key_rows(s)(scalars))

    own = [pl.ds(g * keys, keys) for g in range(groups)]
    half_width = width // 2
    both = [(base, part) for part in range(2) for base in range(2)]

    def kv_half(pieces, array, s, rows_of):
        for base, part in both:
            pieces[part].append((
                array,
                lambda scalars, base=base: (key_rows(s)(scalars), pl.ds(base * half_width, half_width)),
                lambda scalars, base=base, part=part: (
                    rows_of, pl.ds(base * width + part * half_width, half_width)
                ),
            ))

    kv_pieces = [[[], []] for _ in range(groups)]
    for g in range(groups):
        kv_half(kv_pieces[g], kv, 0, own[g])
    col_pieces = [
        (own_cols, col_place(0, g), lambda scalars, g=g: (slice(None), own[g])) for g in range(groups)
    ]
    out_pieces = [[(out_t, slot(0), lambda scalars, g=g: g)] for g in range(groups)]
    lse_pieces = [[(lse, slot(0), lambda scalars, g=g: g)] for g in range(groups)]
    halves = [pl.ds(part * (HEADS // 2), HEADS // 2) for part in range(2)]

    def kept_place(s):
        return lambda scalars: (slice(None), key_rows(s)(scalars))

    def top_place(s, g):
        return lambda scalars: (g, slot(s)(scalars))

    kept_pieces = [
        [[(kept, kept_place(0), lambda scalars, g=g, half=half: (g, half))] for half in halves]
        for g in range(groups)
    ]
    top_pieces = [(tops, top_place(0, g), lambda scalars, g=g: g) for g in range(groups)]
    ahead = [lse, lse]
    merged = []
    for s in range(1, shards):
        for g in range(groups):
            if s > 1:
                moving[g], ahead[g] = lax.optimization_barrier((moving[g], ahead[g]))
            moving[g] = lax.ppermute(moving[g], "pix", turn)
        for g in range(groups):
            if 0 < g and s == shards - 1:
                moving[g], ahead[g - 1] = lax.optimization_barrier((moving[g], ahead[g - 1]))
            ins = [Near(moving[g], 0, keys), gy, by_columns(w_keyval), sel, part_of(q, g * per, per),
                   Near(moving[0], keys, 16)]
            outs = [((keys, 2 * width), BF), ((mine, keys), BF), ((width, per), BF), ((HEADS, per), F32),
                    ((HEADS, keys, per), BF), ((HEADS, per), F32)]
            scratch = [pltpu.VMEM((keys, width), BF), pltpu.VMEM((keys, LANES), F32)]
            scratch += attend_scratch(keys, per)[:1]
            flops = 2 * keys * width * 2 * width
            if s < shards - 1:
                kv, own_cols, out_t, lse, kept, tops = call(
                    functools.partial(shard_kernel, factor, g), [], ins, outs, scratch, flops
                )
                out_pieces[g].append((out_t, slot(s), None))
                lse_pieces[g].append((lse, slot(s), None))
            else:
                kv, own_cols, out_t, lse, kept, tops = call(
                    functools.partial(last_shard_kernel, factor, g, shards), [here],
                    ins + [Stack((shards, width, per), BF, out_pieces[g]),
                           Stack((shards, HEADS, per), F32, lse_pieces[g])],
                    outs, scratch, flops,
                )
                merged.append([out_t, lse])
            kv_half(kv_pieces[g], kv, s, slice(None))
            col_pieces.append((own_cols, col_place(s, g), None))
            for half, pieces in zip(halves, kept_pieces[g]):
                pieces.append((kept, kept_place(s), lambda scalars, half=half: half))
            top_pieces.append((tops, top_place(s, g), None))
            ahead[g] = lse
    for g in range(groups - 1):
        merged[g][1] = ahead[g]

    def by_group(arrays):
        return Stack(
            (groups,) + arrays[0].shape, arrays[0].dtype,
            [(array, lambda scalars, g=g: g, None) for g, array in enumerate(arrays)],
        )

    cross_t = by_group([pair[0] for pair in merged])
    cross_lse = by_group([pair[1] for pair in merged])
    image = group_image.astype(jnp.int32)

    own_hidden = wide // shards if wide_block % LANES == 0 else wide
    hn, qkv, self_t, self_lse, mn, slope, hid, out_low, rself, rmlp, sums, norms = call(
        functools.partial(forward_kernel, factor, wide_block, shards), [here, image],
        [cross_t, latents, w_cross_out, gs, w_qkv, w_self_out, gm, w_in, w_out],
        [((rows, width), BF), ((rows, 3 * width), BF), ((groups, width, per), BF),
         ((groups, HEADS, per), F32), ((rows, width), BF), ((wide // 1024, rows, 1024), BF),
         ((rows, own_hidden), BF), ((rows, width), BF),
         stats, stats, ((1, LANES), F32), ((8, LANES), F32)],
        [pltpu.VMEM((rows, width), F32),
         pltpu.VMEM((rows if own_hidden != wide else 16, wide), BF)] + attend_scratch(per, per),
        2 * rows * width * (5 * width + 2 * wide),
    )
    if own_hidden == wide:
        hid = lax.dynamic_index_in_dim(
            hid.reshape(rows, members, shards, wide_block), place, 2, keepdims=False
        ).reshape(rows, members * wide_block)

    sums = swap_sum(sums, "grp")

    depth = wide_block + block * (wide // width)
    keep_mlp, give_mlp, grad_self, r_self, averaged = call(
        functools.partial(mlp_back_kernel, members), [me, image],
        [sums, norms, cotangent, out_low, in_pieces(w_out, wide // 1024), each_of(slope), hid, w_in, sel, mn, rmlp, gm],
        [((members, depth, width), BF, 2), ((rows, width), F32), ((rows, width), BF), ((1, IMAGES), F32)],
        [pltpu.VMEM((rows, width), BF), pltpu.VMEM((rows, wide), BF), pltpu.VMEM((rows, width), F32)],
        2 * rows * width * (2 * wide + 2 * wide // shards),
    )
    scatter_mlp = Scatter(keep_mlp, give_mlp, "grp", [1, 2])

    d_qkv, keep_self, give_self = call(
        functools.partial(self_back_kernel, factor, scale, members), [me],
        [w_self_out, r_self, self_t, self_lse, qkv, hn, sel],
        [((rows, 3 * width), BF), ((members, 4 * block, width), BF, 2)],
        [pltpu.VMEM((width, rows), F32)] + attend_scratch(per, per) * 2 + [pltpu.VMEM((HEADS, size, per), BF)],
        2 * rows * width * 3 * width,
    )
    scatter_self = Scatter(keep_self, give_self, "grp", [2, 1])
    keep_next, give_next, r_cross, d_out_t, delta, grad_cross = call(
        between_kernel, [],
        [d_qkv, in_pieces(w_qkv, 4), hn, rself, gs, grad_self, w_cross_out, cross_t, keep_mlp,
         Near(scatter_mlp.got.reshape(keep_mlp.shape))],
        [(keep_mlp.shape, BF, 2), ((rows, width), BF), ((groups, width, per), BF),
         ((groups, HEADS, per), F32), ((rows, width), F32)],
        [pltpu.VMEM((rows, width), F32), pltpu.VMEM((width, rows), F32)],
        2 * rows * width * 4 * width,
    )
    scatter_mlp.step_with(keep_next, give_next)
    d_out_t = hold(d_out_t, scatter_self)
    scatter_self.step()
    d_out_t = after(d_out_t, scatter_self)

    group_loads = []
    for g in range(groups):
        for part in range(2):
            group_loads.append(Stack((shards * keys, width), BF, kv_pieces[g][part]))
            group_loads.append(Stack((HEADS // 2, shards * keys, per), BF, kept_pieces[g][part]))
    keep_keyval, give_keyval, keep_cross, give_cross, dq, dkv = call(
        functools.partial(cross_back_kernel, scale, members, groups, shards), [here, me],
        [q, d_out_t, cross_lse, delta, Stack((groups, shards, HEADS, per), F32, top_pieces)]
        + group_loads
        + [sel, xn_part, Stack((groups, mine, shards * keys), BF, col_pieces), cross_t, r_cross],
        [((members, 2 * block, width), BF, 2), ((members, 2 * block, width), BF, 2), ((rows, width), BF),
         ((groups, keys, 2 * width), BF, 0)],
        [pltpu.VMEM((groups, shards * keys, 2 * width), BF)]
        + [pltpu.VMEM((HEADS // 2, shards * keys, per), BF)] * 2,
        2 * shards * groups * keys * width * (5 * per // 2 + 2 * mine),
    )
    scatter_keyval = Scatter(keep_keyval, give_keyval, "grp", [1, 2])
    scatter_cross = Scatter(keep_cross, give_cross, "grp", [2, 1])
    dq = hold(dq, scatter_mlp, scatter_self)
    scatter_mlp.step()
    scatter_self.step()
    dkv = after(dkv, scatter_mlp, scatter_self)
    (grad_pixels,) = call(
        pixel_back_kernel, [], [dkv.reshape(groups * keys, 2 * width), in_pieces(w_keyval, 4), yn, ry, gy],
        [((groups * keys, width), F32)],
        [pltpu.VMEM((groups * keys, width), F32)],
        2 * groups * keys * width * 2 * width,
    )
    index = lax.axis_index("grp") * shards + place
    index_ref = index.reshape(1).astype(jnp.int32)
    all_gains = jnp.stack([gain_cross, gain_pixel, gain_self, gain_mlp])
    own_gains = lax.dynamic_slice_in_dim(all_gains, index * block, block, 1)

    def finish(scatters, heights, gained):
        ends = [scatter.rest() for scatter in scatters]

        def joined(arrays):
            pieces, start = [], 0
            for array in arrays:
                where = pl.ds(start, array.shape[0])
                pieces.append((array, lambda scalars, where=where: where, None))
                start += array.shape[0]
            return Stack((start, width), BF, pieces)

        wides = [(heights_of[0], width * len(heights_of)) for heights_of in heights]
        return call(
            functools.partial(finish_kernel, heights, list(gained), len(ends)), [index_ref],
            [joined([keep for keep, _ in ends])] + [Near(got) for _, got in ends]
            + [part_of(weight, lambda scalars: scalars[0][0] * block, block) for weight, _ in gained.values()]
            + [own_gains[row : row + 1] for _, row in gained.values()],
            [(shape, F32) for shape in wides] + [((1, block), F32)] * len(gained),
            [], 1e6,
        )

    grad_pixels = hold(grad_pixels, scatter_keyval, scatter_cross, scatter_self)
    scatter_keyval.step()
    scatter_cross.step()
    grad_pixels = after(grad_pixels, scatter_keyval, scatter_cross)
    d_w_qkv, d_w_self_out, d_g_self = finish([scatter_self], [[block] * 3, [block]], {0: (w_qkv, 2)})
    dq, d_w_qkv, scatter_mlp.got = lax.optimization_barrier((dq, d_w_qkv, scatter_mlp.got))
    dq, grad_pixels = after((dq, grad_pixels), scatter_keyval, scatter_cross)
    (grad_latents,) = call(
        query_back_kernel, [], [dq, in_pieces(w_query, 2), xn, rx, gx, grad_cross],
        [((rows, width), F32)],
        [pltpu.VMEM((rows, width), F32)],
        2 * rows * width * width,
    )

    grad_latents = hold(grad_latents, scatter_mlp, scatter_keyval, scatter_cross)
    scatter_keyval.step()
    scatter_cross.step()
    d_w_out, d_w_in, d_g_mlp = finish(
        [scatter_mlp], [[wide_block], [block] * (wide // width)], {1: (w_in, 3)}
    )
    d_w_keyval, d_w_query, d_w_cross_out, d_g_pixel, d_g_cross = finish(
        [scatter_keyval, scatter_cross], [[block] * 2, [block], [block]], {0: (w_keyval, 1), 1: (w_query, 0)}
    )
    return (
        out_low,
        grad_latents,
        grad_pixels.reshape(groups, keys, width),
        d_g_cross.reshape(block),
        d_g_pixel.reshape(block),
        d_w_query,
        d_w_keyval,
        d_w_cross_out,
        d_g_self.reshape(block),
        d_w_qkv,
        d_w_self_out,
        d_g_mlp.reshape(block),
        d_w_in,
        d_w_out,
        averaged.reshape(IMAGES),
    )


def solution(mesh):
    both = ("grp", "pix")
    in_specs = (
        P("grp", None), P("grp", "pix", None), P("grp", "pix"), P("grp"), P("grp", None),
    ) + (P(),) * 11
    out_specs = (
        P("grp", None), P("grp", None), P("grp", "pix", None), P(both), P(both),
        P(both, None), P(both, None), P(both, None), P(both), P(both, None), P(both, None),
        P(both), P(both, None), P(both, None), P(),
    )
    return jax.shard_map(
        per_device, mesh=mesh, in_specs=in_specs, out_specs=out_specs, check_vma=False
    )
```
